512 devices in a mesh: snap: 8 (over z), tile: 64 (over x, y, core).
Axes of the slice: x: 4, y: 8, z: 8, core: 2. Of those that a mesh axis runs over, the one named last changes fastest.
Arguments:
- modes: bfloat16 [8192, 256], P(('snap', 'tile')), may hold values from -8 to 8
- targets: bfloat16 [8192, 256], P(('snap', 'tile')), may hold values from -16 to 16
- pairs: int32 [4096, 2], replicated, may hold values from 0 to 256, as said below
- support: int32 [4096, 256], P(('snap', 'tile')), may hold values from 0 to 1, as said below
Outputs:
- coeffs: float32 [4096, 256], P(('snap', 'tile'))
- resid: float32 [4096, 256], P(('snap', 'tile'))
The draws below stay inside these ranges and needn't reach their ends.
Inputs may be any that keep to these rules, and one draw needn't show every extreme that they name: Rows are distinct unordered pairs; the first entry is below 256; every index below 256 is the first entry of exactly 16 rows. `support`: every target has at least one active term.
All inputs are finite; a program needn't handle non-finite values.
Results may differ from the reference program's by a relative error of at most 0.0036.
Values may be sent and summed in bfloat16 or wider, within the bound.
A program may use at most 64 MiB of HBM per device.

```python
import math
import jax
import jax.numpy as jnp
from jax import lax

M = 256
P_SIZE = 4096
ITERS = 2
K = 256
SNAPS = 8192


def shared_modes(key):
    base_key = jax.random.fold_in(key, 11)
    first_key, second_key = jax.random.split(base_key)
    spreads = jnp.exp(jax.random.uniform(first_key, (M,), jnp.float32, jnp.log(0.5), jnp.log(2.0)))
    raw = jnp.clip(jax.random.normal(second_key, (SNAPS, M), jnp.float32), -4.0, 4.0)
    return raw * spreads


def draw_modes(key, part):
    return shared_modes(key).astype(jnp.bfloat16)


def draw_targets(key, part):
    amplitudes = shared_modes(key).astype(jnp.bfloat16).astype(jnp.float32)
    noise_key = jax.random.fold_in(key, 23)
    noise = jnp.clip(jax.random.normal(noise_key, (SNAPS, K), jnp.float32), -4.0, 4.0) * 0.5
    quadratic = amplitudes * jnp.roll(amplitudes, 1, axis=1)
    linear = jnp.roll(amplitudes, 7, axis=1)
    values = 0.5 * quadratic + 0.5 * linear + noise
    return jnp.clip(values, -16.0, 16.0).astype(jnp.bfloat16)


def draw_pairs(key, part):
    groups = P_SIZE // M
    offset_key, order_key, shuffle_key = jax.random.split(jax.random.fold_in(key, 31), 3)
    offsets = jax.random.permutation(offset_key, jnp.arange(M // 2 + 1, dtype=jnp.int32))[:groups]
    orders = jax.vmap(lambda sub_key: jax.random.permutation(sub_key, jnp.arange(M, dtype=jnp.int32)))(jax.random.split(order_key, groups))
    first = orders
    second = (orders + offsets[:, None]) % (M + 1)
    table = jnp.stack([first.reshape(-1), second.reshape(-1)], axis=1).astype(jnp.int32)
    shuffled = jax.random.permutation(shuffle_key, jnp.arange(P_SIZE, dtype=jnp.int32))
    return table[shuffled]


def draw_support(key, part):
    score_key, forced_key = jax.random.split(jax.random.fold_in(key, 47))
    scores = jax.random.randint(score_key, (P_SIZE, K), 0, 8 * P_SIZE, dtype=jnp.int32)
    positions = jnp.arange(P_SIZE, dtype=jnp.int32)[:, None]
    chosen = scores < P_SIZE + 2 * positions
    forced = jax.random.randint(forced_key, (K,), 0, P_SIZE, dtype=jnp.int32)
    chosen = jnp.logical_or(chosen, positions == forced[None, :])
    return chosen.astype(jnp.int32)


def setup_inputs(seed: int = 0) -> dict:
    arg_keys = jax.random.split(jax.random.key(seed), 5)
    modes = draw_modes(jax.random.fold_in(arg_keys[4], 71), 0)
    targets = draw_targets(jax.random.fold_in(arg_keys[4], 71), 0)
    pairs = draw_pairs(jax.random.fold_in(arg_keys[4], 71), 0)
    support = draw_support(jax.random.fold_in(arg_keys[4], 71), 0)
    return {"modes": modes, "targets": targets, "pairs": pairs, "support": support}


def build_library(rows, pairs):
    extended = jnp.concatenate([rows.astype(jnp.float32), jnp.ones((rows.shape[0], 1), jnp.float32)], axis=1)
    first = jnp.take(extended, pairs[:, 0], axis=1)
    second = jnp.take(extended, pairs[:, 1], axis=1)
    return (first * second).astype(jnp.bfloat16)


def reference(modes, targets, pairs, support):
    block_rows = math.gcd(SNAPS, 2048)
    count_blocks = SNAPS // block_rows
    mode_blocks = modes.reshape(count_blocks, block_rows, M)
    target_blocks = targets.reshape(count_blocks, block_rows, K)

    def accumulate(carry, block_item):
        gram_sum, cross_sum = carry
        rows_in, targets_in = block_item
        library = build_library(rows_in, pairs)
        gram_sum = gram_sum + jnp.dot(library.T, library, preferred_element_type=jnp.float32)
        cross_sum = cross_sum + jnp.dot(library.T, targets_in, preferred_element_type=jnp.float32)
        return (gram_sum, cross_sum), None

    start_sums = (jnp.zeros((P_SIZE, P_SIZE), jnp.float32), jnp.zeros((P_SIZE, K), jnp.float32))
    (gram_sum, cross_sum), _ = lax.scan(accumulate, start_sums, (mode_blocks, target_blocks))
    gram = gram_sum / SNAPS
    cross = cross_sum / SNAPS
    support_mask = support.astype(jnp.float32)
    resid = support_mask * cross
    direction = resid
    coeffs = jnp.zeros((P_SIZE, K), jnp.float32)
    energy = jnp.sum(resid * resid, axis=0)
    for step in range(ITERS):
        image = support_mask * jnp.dot(gram, direction, precision=lax.Precision.HIGHEST, preferred_element_type=jnp.float32)
        step_len = energy / jnp.sum(direction * image, axis=0)
        coeffs = coeffs + step_len * direction
        resid = resid - step_len * image
        if step + 1 < ITERS:
            fresh = jnp.sum(resid * resid, axis=0)
            direction = resid + (fresh / energy) * direction
            energy = fresh
    return (coeffs, resid)
```

```python
import jax
import jax.numpy as jnp
from jax import lax
from jax.experimental import pallas as pl
from jax.experimental.pallas import tpu as pltpu
from jax.sharding import PartitionSpec as P

NX, NY, NZ, NC = 4, 8, 8, 2
RING = NZ * NC
PLANE = NX * NY
MODES = 256
TARGETS = 256
TERMS = 4096
ROWS = 16
SNAPS = 8192
LOCAL = PLANE * ROWS
OWN = TERMS // RING
GROUP = TARGETS // PLANE
CHUNK = 1024
F32 = jnp.float32
BF16 = jnp.bfloat16
MESH = pl.DeviceIdType.MESH


def split(value):
    high = value.astype(BF16)
    low = (value - high.astype(F32)).astype(BF16)
    return jnp.concatenate([high, low], axis=0)


def merge(value):
    return value[:GROUP] + value[GROUP:]


def dot_nt(lhs, rhs):
    return lax.dot_general(lhs, rhs, (((1,), (1,)), ((), ())), preferred_element_type=F32)


def dot_nn(lhs, rhs):
    return jnp.dot(lhs, rhs, preferred_element_type=F32)


def iota(shape, dim):
    return lax.broadcasted_iota(jnp.int32, shape, dim)


def drain(ref, sem):
    pltpu.make_async_copy(ref, ref, sem).wait()


def kernel(
    modes_ref, targets_ref, pairs_ref, support_ref, coeffs_ref, resid_ref,
    rows, extra, hot_a, hot_b, terms, library,
    part0, part1, part2, got0, got1, got2, full0, full1,
    curve1, curve2, curves1, curves2, turn_x, got_x, turn_y, got_y,
    send_sem, recv_sem,
):
    z = lax.axis_index("snap")
    tile = lax.axis_index("tile")
    x = tile // (NY * NC)
    y = (tile // NC) % NY
    core = tile % NC
    spot = x * NY + y
    me = z * NC + core

    def at_x(step):
        other = lax.rem(x + step, NX)
        return other, (z, (other * NY + y) * NC + core)

    def at_y(step):
        other = lax.rem(y + step, NY)
        return other, (z, (x * NY + other) * NC + core)

    def at_ring(step):
        other = lax.rem(me + step, RING)
        return other, (other // NC, spot * NC + lax.rem(other, NC))

    barrier = pltpu.get_barrier_semaphore()
    for step in range(1, NY):
        pl.semaphore_signal(barrier, inc=1, device_id=at_y(step)[1], device_id_type=MESH)
    for step in range(1, NX):
        pl.semaphore_signal(barrier, inc=1, device_id=at_x(step)[1], device_id_type=MESH)
    for step in range(1, RING):
        pl.semaphore_signal(barrier, inc=1, device_id=at_ring(step)[1], device_id_type=MESH)

    def send(src, dst, stage, device):
        pltpu.make_async_remote_copy(
            src_ref=src, dst_ref=dst, send_sem=send_sem.at[stage], recv_sem=recv_sem.at[stage],
            device_id=device, device_id_type=MESH,
        ).start()

    own_rows = pl.ds(pl.multiple_of(spot * ROWS, ROWS), ROWS)
    slab = pl.ds(pl.multiple_of(x * (NY * ROWS), NY * ROWS), NY * ROWS)
    rows[own_rows, :] = modes_ref[...]
    extra[own_rows, 0:TARGETS] = targets_ref[...]
    active = support_ref[...].astype(F32)
    extra[own_rows, TARGETS:] = jnp.concatenate(
        [active[:, :128], active[:, 128:]], axis=0
    ).astype(BF16)
    pl.semaphore_wait(barrier, NY - 1 + NX - 1 + RING - 1)

    for step in range(1, NY):
        send(rows.at[own_rows], rows.at[own_rows], 0, at_y(step)[1])
    for step in range(1, NY):
        send(extra.at[own_rows], extra.at[own_rows], 1, at_y(step)[1])

    pairs = pairs_ref[...].astype(F32)
    stacked = jnp.concatenate(
        [pairs[side : side + 1, 512 * k : 512 * k + 512] for side in (0, 1) for k in range(NZ)],
        axis=0,
    ).astype(BF16)
    place = iota((512, 512), 1)
    origin = (place % 256) // 8 * 16 + place // 256 * 8 + place % 8
    order = (iota((512, 512), 0) == origin).astype(F32).astype(BF16)
    terms[...] = dot_nn(stacked, order).astype(jnp.int32)
    for k in range(NZ):
        span = slice(512 * k, 512 * k + 512)
        index = iota((MODES, 512), 0)
        hot_a[:, span] = (index == terms[k : k + 1, :]).astype(F32).astype(BF16)
        hot_b[:, span] = (index == terms[NZ + k : NZ + k + 1, :]).astype(F32).astype(BF16)

    drain(rows.at[pl.ds(0, (NY - 1) * ROWS)], recv_sem.at[0])
    for step in range(1, NX):
        send(rows.at[slab], rows.at[slab], 2, at_x(step)[1])
    drain(extra.at[pl.ds(0, (NY - 1) * ROWS)], recv_sem.at[1])
    for step in range(1, NX):
        send(extra.at[slab], extra.at[slab], 3, at_x(step)[1])
    drain(rows.at[pl.ds(0, (NX - 1) * NY * ROWS)], recv_sem.at[2])

    for k in range(TERMS // CHUNK):
        span = slice(k * CHUNK, (k + 1) * CHUNK)
        per = CHUNK // 512
        constant = jnp.concatenate(
            [terms[NZ + k * per + j : NZ + k * per + j + 1, :] for j in range(per)], axis=1
        )
        constant = (constant == MODES).astype(F32)
        first = dot_nn(rows[...], hot_a[:, span])
        second = dot_nn(rows[...], hot_b[:, span]) + constant
        library[:, span] = (first * second).astype(BF16)

    drain(extra.at[pl.ds(0, (NX - 1) * NY * ROWS)], recv_sem.at[3])

    group = y * NX + x
    pick = (iota((2 * GROUP, TARGETS), 1) == group * GROUP + iota((2 * GROUP, TARGETS), 0)) & (
        iota((2 * GROUP, TARGETS), 0) < GROUP
    )
    wanted = dot_nt(pick.astype(F32).astype(BF16), extra[:, 0:TARGETS]).astype(BF16)
    half = group // (PLANE // 2)
    column = group % (PLANE // 2) * GROUP
    pick = (iota((2 * GROUP, 128), 1) == column + iota((2 * GROUP, 128), 0)) & (
        iota((2 * GROUP, 128), 0) < GROUP
    )
    flags = dot_nt(pick.astype(F32).astype(BF16), extra[:, TARGETS:]).astype(BF16)
    lane = iota((512, 256), 1)
    pick = iota((512, 256), 0) == lane // 8 * 16 + half * 8 + lane % 8
    mask = dot_nn(flags, pick.astype(F32).astype(BF16))[:GROUP]

    own_terms = pl.ds(pl.multiple_of(me * OWN, OWN), OWN)

    def scatter_sums(value, part, got, stage):
        part[...] = value
        for step in range(1, RING):
            other, device = at_ring(step)
            theirs = pl.ds(pl.multiple_of(other * OWN, OWN), OWN)
            send(part.at[:, theirs], got.at[step - 1], stage, device)

    def sum_up(part, got, stage):
        drain(got, recv_sem.at[stage])
        total = part[:, own_terms]
        for step in range(1, RING):
            total = total + got[step - 1]
        return total * mask * (1.0 / SNAPS)

    def gather_terms(value, full, stage):
        full[:, own_terms] = value
        for step in range(1, RING):
            send(full.at[:, own_terms], full.at[:, own_terms], stage, at_ring(step)[1])
        drain(full.at[:, pl.ds(0, TERMS - OWN)], recv_sem.at[stage])
        return full[...]

    def apply(vector, curve, curves, part, got, stage):
        image = merge(dot_nt(split(vector), library[...]))
        curve[...] = jnp.broadcast_to(jnp.sum(image * image, axis=1, keepdims=True), (GROUP, 128))
        for step in range(1, RING):
            send(curve, curves.at[step - 1], stage, at_ring(step)[1])
        scatter_sums(merge(dot_nn(split(image), library[...])), part, got, stage + 1)
        drain(curves, recv_sem.at[stage])
        total = curve[...]
        for step in range(1, RING):
            total = total + curves[step - 1]
        return total[:, 0:1] * (1.0 / SNAPS), sum_up(part, got, stage + 1)

    def squares(vector):
        return jnp.sum(vector * vector, axis=1, keepdims=True)

    scatter_sums(dot_nn(wanted, library[...])[:GROUP], part0, got0, 4)
    direction = sum_up(part0, got0, 4)
    whole = gather_terms(direction, full0, 5)
    energy = squares(whole)
    curvature, product = apply(whole, curve1, curves1, part1, got1, 6)
    step_len = energy / curvature
    coeffs = step_len * direction
    resid = direction - step_len * product
    whole_resid = gather_terms(resid, full1, 8)
    fresh = squares(whole_resid)
    ratio = fresh / energy
    direction = resid + ratio * direction
    whole = whole_resid + ratio * whole
    curvature, product = apply(whole, curve2, curves2, part2, got2, 9)
    step_len = fresh / curvature
    coeffs = coeffs + step_len * direction
    resid = resid - step_len * product

    lane = iota((GROUP, 128), 1)
    for k in range(NX):
        pair = slice(k // 2 * 128, k // 2 * 128 + 128)
        left, right = coeffs[:, pair], resid[:, pair]
        if k % 2 == 0:
            right = pltpu.roll(right, 64, 1)
        else:
            left = pltpu.roll(left, 64, 1)
        turn_x[8 * k : 8 * k + 8, :] = jnp.where(lane < 64, left, right)
    at = pl.ds(pl.multiple_of(x * 8, 8), 8)
    for step in range(1, NX):
        other, device = at_x(step)
        send(turn_x.at[pl.ds(pl.multiple_of(other * 8, 8), 8)], got_x.at[at], 11, device)
    got_x[at, :] = turn_x[at, :]
    drain(got_x.at[pl.ds(0, (NX - 1) * 8)], recv_sem.at[11])
    held = got_x[...]
    square = jnp.concatenate(
        [held, pltpu.roll(held, 64, 1), jnp.zeros((64, 128), F32)], axis=0
    )
    turn_y[...] = square.T[:64]
    at = pl.ds(pl.multiple_of(y * 8, 8), 8)
    for step in range(1, NY):
        other, device = at_y(step)
        send(turn_y.at[pl.ds(pl.multiple_of(other * 8, 8), 8)], got_y.at[at], 12, device)
    got_y[at, :] = turn_y[at, :]
    drain(got_y.at[pl.ds(0, (NY - 1) * 8)], recv_sem.at[12])
    for half_at in range(2):
        left = jnp.zeros((8, 128), F32)
        right = left
        for k in range(4):
            block = got_y[8 * (4 * half_at + k) : 8 * (4 * half_at + k) + 8, :]
            here = lane // 32 == k
            left = jnp.where(here, pltpu.roll(block, 32 * k, 1) if k else block, left)
            shift = (32 * k - 32) % 128
            right = jnp.where(here, pltpu.roll(block, shift, 1) if shift else block, right)
        coeffs_ref[:, 128 * half_at : 128 * half_at + 128] = left
        resid_ref[:, 128 * half_at : 128 * half_at + 128] = right

    drain(rows.at[pl.ds(0, (NY - 1) * ROWS)], send_sem.at[0])
    drain(extra.at[pl.ds(0, (NY - 1) * ROWS)], send_sem.at[1])
    drain(rows.at[pl.ds(0, (NX - 1) * NY * ROWS)], send_sem.at[2])
    drain(extra.at[pl.ds(0, (NX - 1) * NY * ROWS)], send_sem.at[3])
    for stage, got in ((4, got0), (7, got1), (10, got2), (6, curves1), (9, curves2)):
        drain(got, send_sem.at[stage])
    for stage, full in ((5, full0), (8, full1)):
        drain(full.at[:, pl.ds(0, TERMS - OWN)], send_sem.at[stage])
    drain(got_x.at[pl.ds(0, (NX - 1) * 8)], send_sem.at[11])
    drain(got_y.at[pl.ds(0, (NY - 1) * 8)], send_sem.at[12])


def body(modes, targets, pairs, support):
    vmem = pl.BlockSpec(memory_space=pltpu.VMEM)
    out = jax.ShapeDtypeStruct(support.shape, F32)
    return pl.pallas_call(
        kernel,
        out_shape=(out, out),
        in_specs=[vmem] * 4,
        out_specs=(vmem, vmem),
        scratch_shapes=[
            pltpu.VMEM((LOCAL, MODES), BF16),
            pltpu.VMEM((LOCAL, TARGETS + 128), BF16),
            pltpu.VMEM((MODES, TERMS), BF16),
            pltpu.VMEM((MODES, TERMS), BF16),
            pltpu.VMEM((2 * NZ, 512), jnp.int32),
            pltpu.VMEM((LOCAL, TERMS), BF16),
        ]
        + [pltpu.VMEM((GROUP, TERMS), F32)] * 3
        + [pltpu.VMEM((RING - 1, GROUP, OWN), F32)] * 3
        + [pltpu.VMEM((GROUP, TERMS), F32)] * 2
        + [pltpu.VMEM((GROUP, 128), F32)] * 2
        + [pltpu.VMEM((RING - 1, GROUP, 128), F32)] * 2
        + [pltpu.VMEM((NX * 8, 128), F32)] * 2
        + [pltpu.VMEM((NY * 8, 128), F32)] * 2
        + [pltpu.SemaphoreType.DMA((13,))] * 2,
        compiler_params=pltpu.CompilerParams(
            collective_id=0, has_side_effects=True, vmem_limit_bytes=48 * 2**20
        ),
        name="regression",
    )(modes, targets, pairs.T, support)


def solution(mesh):
    rows = P(("snap", "tile"), None)
    return jax.shard_map(
        body,
        mesh=mesh,
        in_specs=(rows, rows, P(), rows),
        out_specs=(rows, rows),
        check_vma=False,
    )
```

```python
import jax
import jax.numpy as jnp
from jax import lax
from jax.experimental import pallas as pl
from jax.experimental.pallas import tpu as pltpu
from jax.sharding import PartitionSpec as P

NX, NY, NZ, NC = 4, 8, 8, 2
RING = NZ * NC
PLANE = NX * NY
MODES = 256
TARGETS = 256
TERMS = 4096
ROWS = 16
SNAPS = 8192
SLAB = NY * ROWS
LOCAL = PLANE * ROWS
OWN = TERMS // RING
HALF = TERMS // NC
GROUP = TARGETS // PLANE
CHUNK = 1024
FAR_FIRST = (4, 3, 5, 2, 6, 1, 7)
NEAR_FIRST = (1, 7, 2, 6, 3, 5, 4)
F32 = jnp.float32
BF16 = jnp.bfloat16
MESH = pl.DeviceIdType.MESH

EXTRA, SLABS, COMPACT, PAIR, SUMS, SLICES, HALVES, CURVE, TURN = 7, 8, 11, 12, 15, 18, 20, 22, 23
STAGES = 24


def split(value):
    high = value.astype(BF16)
    low = (value - high.astype(F32)).astype(BF16)
    return jnp.concatenate([high, low], axis=0)


def merge(value):
    return value[:GROUP] + value[GROUP:]


def dot_nt(lhs, rhs):
    return lax.dot_general(lhs, rhs, (((1,), (1,)), ((), ())), preferred_element_type=F32)


def dot_nn(lhs, rhs):
    return jnp.dot(lhs, rhs, preferred_element_type=F32)


def iota(shape, dim):
    return lax.broadcasted_iota(jnp.int32, shape, dim)


def chosen(condition):
    return condition.astype(F32).astype(BF16)


def drain(ref, sem):
    pltpu.make_async_copy(ref, ref, sem).wait()


def kernel(
    modes_ref, targets_ref, pairs_ref, support_ref, out_ref,
    targets_in, pairs_in, support_in, rows, extra, compact, compact_in,
    hot_a, hot_b, terms, library,
    out0, out1, out2, pair0, pair1, pair2, pre0, pre1, pre2, got0, got1, got2,
    full0, full1, curve, curves, turn, square, turned,
    load_sem, send_sem, recv_sem,
):
    z = lax.axis_index("snap")
    tile = lax.axis_index("tile")
    x = tile // (NY * NC)
    y = (tile // NC) % NY
    core = tile % NC

    def at_plane(step_x, step_y):
        return z, (lax.rem(x + step_x, NX) * NY + lax.rem(y + step_y, NY)) * NC + core

    def at_line(step):
        other = lax.rem(z + step, NZ)
        return other, (other, tile)

    sibling = (z, tile + 1 - 2 * core)

    own_block = pl.ds(pl.multiple_of(y * ROWS, ROWS), ROWS)
    loads = [
        pltpu.make_async_copy(modes_ref, rows.at[own_block], load_sem.at[0]),
        pltpu.make_async_copy(targets_ref, targets_in, load_sem.at[1]),
        pltpu.make_async_copy(support_ref, support_in, load_sem.at[2]),
        pltpu.make_async_copy(pairs_ref, pairs_in, load_sem.at[3]),
    ]
    for load in loads:
        load.start()

    barrier = pltpu.get_barrier_semaphore()
    peers = [(a, b) for a in range(NX) for b in range(NY) if a or b]
    for a, b in peers:
        pl.semaphore_signal(barrier, inc=1, device_id=at_plane(a, b), device_id_type=MESH)
    for step in range(1, NZ):
        pl.semaphore_signal(barrier, inc=1, device_id=at_line(step)[1], device_id_type=MESH)
    pl.semaphore_signal(barrier, inc=1, device_id=sibling, device_id_type=MESH)

    def send(src, dst, stage, device, arrive=None):
        pltpu.make_async_remote_copy(
            src_ref=src, dst_ref=dst, send_sem=send_sem.at[stage],
            recv_sem=recv_sem.at[stage if arrive is None else arrive],
            device_id=device, device_id_type=MESH,
        ).start()

    for load in loads[:3]:
        load.wait()
    extra[own_block, 0:TARGETS] = targets_in[...]
    active = support_in[...].astype(F32)
    extra[own_block, TARGETS:] = jnp.concatenate(
        [active[:, :128], active[:, 128:]], axis=0
    ).astype(BF16)
    pl.semaphore_wait(barrier, len(peers) + NZ - 1 + 1)

    for step in FAR_FIRST:
        send(rows.at[own_block], rows.at[own_block], 0, at_plane(0, step), step - 1)

    def forward(block):
        source = pl.multiple_of(block * ROWS, ROWS)
        for step in (2, 1, 3):
            target = pl.multiple_of(step * SLAB + block * ROWS, ROWS)
            send(
                rows.at[pl.ds(source, ROWS)], rows.at[pl.ds(target, ROWS)], SLABS + step - 1,
                at_plane(step, 0),
            )

    forward(y)
    for step in FAR_FIRST:
        send(extra.at[own_block], extra.at[own_block], EXTRA, at_plane(0, step))

    loads[3].wait()
    pairs = pairs_in[...].astype(F32)
    stacked = jnp.concatenate(
        [pairs[side : side + 1, 512 * k : 512 * k + 512] for side in (0, 1) for k in range(NZ)],
        axis=0,
    ).astype(BF16)
    place = iota((512, 512), 1)
    origin = (place % 256) // 8 * 16 + place // 256 * 8 + place % 8
    terms[...] = dot_nn(stacked, chosen(iota((512, 512), 0) == origin)).astype(jnp.int32)
    index = iota((MODES, OWN), 0)

    def make_hot(c):
        for k in range(NZ):
            from_lane = slice(OWN * c, OWN * c + OWN)
            span = slice(HALF * c + OWN * k, HALF * c + OWN * k + OWN)
            hot_a[:, span] = chosen(index == terms[k : k + 1, from_lane])
            hot_b[:, span] = chosen(index == terms[NZ + k : NZ + k + 1, from_lane])

    make_hot(0)
    for step in NEAR_FIRST:
        drain(rows.at[pl.ds(0, ROWS)], recv_sem.at[step - 1])
        forward(lax.rem(y - step + NY, NY))
    make_hot(1)

    drain(extra.at[pl.ds(0, (NY - 1) * ROWS)], recv_sem.at[EXTRA])
    line = iota((NX * ROWS, TARGETS), 0)
    wanted = (NX * y + line // ROWS) * GROUP + line % ROWS
    pick_targets = chosen((iota((NX * ROWS, TARGETS), 1) == wanted) & (line % ROWS < GROUP))
    line = iota((NX * ROWS, 128), 0)
    wanted = (NX * (y % 4) + line // ROWS) * GROUP + line % ROWS - GROUP
    pick_flags = chosen((iota((NX * ROWS, 128), 1) == wanted) & (line % ROWS >= GROUP))
    compact[...] = (
        dot_nt(pick_targets, extra[:, 0:TARGETS]) + dot_nt(pick_flags, extra[:, TARGETS:])
    ).astype(BF16)
    for step in (2, 1, 3):
        theirs = pl.ds(pl.multiple_of(lax.rem(x + step, NX) * ROWS, ROWS), ROWS)
        send(
            compact.at[theirs], compact_in.at[pl.ds(step * ROWS, ROWS)], COMPACT,
            at_plane(step, 0),
        )
    compact_in[0:ROWS, :] = compact[pl.ds(pl.multiple_of(x * ROWS, ROWS), ROWS), :]

    def build(begin, end):
        for k in range(TERMS // CHUNK):
            span = slice(k * CHUNK, (k + 1) * CHUNK)
            c, first_z = k * CHUNK // HALF, k * CHUNK % HALF // OWN
            constant = jnp.concatenate(
                [
                    terms[NZ + j : NZ + j + 1, OWN * c : OWN * c + OWN]
                    for j in range(first_z, first_z + CHUNK // OWN)
                ],
                axis=1,
            )
            constant = (constant == MODES).astype(F32)
            first = dot_nn(rows[begin:end, :], hot_a[:, span])
            second = dot_nn(rows[begin:end, :], hot_b[:, span]) + constant
            library[begin:end, span] = (first * second).astype(BF16)

    build(0, SLAB)
    square[...] = jnp.zeros_like(square)
    for step in (1, 3, 2):
        drain(rows.at[pl.ds(0, SLAB)], recv_sem.at[SLABS + step - 1])
    build(SLAB, LOCAL)

    drain(compact_in.at[pl.ds(0, (NX - 1) * ROWS)], recv_sem.at[COMPACT])
    given = jnp.concatenate([compact_in[k * ROWS : (k + 1) * ROWS, :] for k in range(NX)], axis=1)
    line, lane = iota((LOCAL, OWN), 0), iota((LOCAL, OWN), 1)
    from_x = lax.rem(x - line // 128 + NX, NX)
    pick = (
        (from_x * NY + line % 128 // 16 == lane // 8)
        & (line % 16 // 8 == y // 4)
        & (line % 8 == lane % 8)
    )
    mask = dot_nn(given, chosen(pick))[GROUP:]

    own_half = pl.ds(pl.multiple_of(core * HALF, HALF), HALF)
    their_half = pl.ds(pl.multiple_of((1 - core) * HALF, HALF), HALF)
    own_terms = pl.ds(pl.multiple_of(core * HALF + z * OWN, OWN), OWN)
    own_slice = pl.ds(pl.multiple_of(z * OWN, OWN), OWN)

    def scatter_sums(lhs, finish, out, pair, pre, got, at):
        out[...] = finish(dot_nn(lhs, library[:, their_half]))
        send(out, pair, PAIR + at, sibling)
        own = finish(dot_nn(lhs, library[:, own_half]))
        drain(pair, recv_sem.at[PAIR + at])
        pre[...] = own + pair[...]
        for step in FAR_FIRST:
            other, device = at_line(step)
            theirs = pl.ds(pl.multiple_of(other * OWN, OWN), OWN)
            send(pre.at[:, theirs], got.at[step - 1], SUMS + at, device)

    def sum_up(pre, got, at):
        drain(got, recv_sem.at[SUMS + at])
        total = pre[:, own_slice]
        for step in range(1, NZ):
            total = total + got[step - 1]
        return total * mask * (1.0 / SNAPS)

    def gather_slices(value, full, at):
        full[:, own_terms] = value
        for step in FAR_FIRST:
            send(full.at[:, own_terms], full.at[:, own_terms], SLICES + at, at_line(step)[1])
        drain(full.at[:, pl.ds(0, HALF - OWN)], recv_sem.at[SLICES + at])
        send(full.at[:, own_half], full.at[:, own_half], HALVES + at, sibling)

    def gather_halves(full, at):
        drain(full.at[:, pl.ds(0, HALF)], recv_sem.at[HALVES + at])

    def squares(vector):
        return jnp.sum(vector * vector, axis=1, keepdims=True)

    scatter_sums(given, lambda value: value[:GROUP], out0, pair0, pre0, got0, 0)
    direction = sum_up(pre0, got0, 0)
    gather_slices(direction, full0, 0)
    image = dot_nt(split(full0[:, own_half]), library[:, own_half])
    gather_halves(full0, 0)
    image = merge(image + dot_nt(split(full0[:, their_half]), library[:, their_half]))
    scatter_sums(split(image), merge, out1, pair1, pre1, got1, 1)
    whole = full0[...]
    energy = squares(whole)
    product = sum_up(pre1, got1, 1)
    gather_slices(product, full1, 1)
    gather_halves(full1, 1)
    whole_product = full1[...]
    step_len = energy / jnp.sum(whole * whole_product, axis=1, keepdims=True)
    whole_resid = whole - step_len * whole_product
    fresh = squares(whole_resid)
    ratio = fresh / energy
    coeffs = step_len * direction
    resid = direction - step_len * product
    direction = resid + ratio * direction
    image = merge(dot_nt(split(whole_resid + ratio * whole), library[...]))

    curve[0] = jnp.broadcast_to(squares(image), (GROUP, 128))
    send(curve.at[0], curve.at[1], CURVE, sibling)
    scatter_sums(split(image), merge, out2, pair2, pre2, got2, 2)
    drain(curve.at[1], recv_sem.at[CURVE])
    curve[2] = curve[0] + curve[1]
    for step in FAR_FIRST:
        send(curve.at[2], curves.at[step - 1], STAGES, at_line(step)[1])
    drain(curves, recv_sem.at[STAGES])
    total = curve[2]
    for step in range(1, NZ):
        total = total + curves[step - 1]
    product = sum_up(pre2, got2, 2)
    step_len = fresh / (total[:, 0:1] * (1.0 / SNAPS))
    coeffs = coeffs + step_len * direction
    resid = resid - step_len * product

    group = NX * y + x
    at = group % (PLANE // 2) * GROUP
    square[pl.ds(pl.multiple_of(at, GROUP), GROUP), :] = coeffs
    square[pl.ds(pl.multiple_of(lax.rem(at + 64, 128), GROUP), GROUP), :] = resid
    turn[...] = square[...].T
    here = pl.ds(pl.multiple_of((x * NY + y) * 8, 8), 8)
    for a, b in sorted(peers, key=lambda peer: -min(peer[0], NX - peer[0]) - min(peer[1], NY - peer[1])):
        spot = lax.rem(x + a, NX) * NY + lax.rem(y + b, NY)
        theirs = pl.ds(pl.multiple_of(spot * 8, 8), 8)
        send(turn.at[theirs], turned.at[here], TURN, at_plane(a, b))
    turned[here, :] = turn[here, :]
    drain(turned.at[pl.ds(0, OWN - 8)], recv_sem.at[TURN])
    lane = iota((8, 128), 1) // GROUP
    for side in range(2):
        left = jnp.zeros((8, 128), F32)
        right = left
        for a in range(NX):
            for b in range(4 * side, 4 * side + 4):
                block = turned[8 * (a * NY + b) : 8 * (a * NY + b) + 8, :]
                at = (NX * b + a) % (PLANE // 2)
                left = jnp.where(lane == at, block, left)
                right = jnp.where(lane == (at + 8) % 16, block, right)
        out_ref[0:8, 128 * side : 128 * side + 128] = left
        out_ref[8:16, 128 * side : 128 * side + 128] = pltpu.roll(right, 64, 1)

    drain(rows.at[pl.ds(0, (NY - 1) * ROWS)], send_sem.at[0])
    drain(extra.at[pl.ds(0, (NY - 1) * ROWS)], send_sem.at[EXTRA])
    for step in (1, 2, 3):
        drain(rows.at[pl.ds(0, SLAB)], send_sem.at[SLABS + step - 1])
    drain(compact_in.at[pl.ds(0, (NX - 1) * ROWS)], send_sem.at[COMPACT])
    for k, (pair, got) in enumerate(((pair0, got0), (pair1, got1), (pair2, got2))):
        drain(pair, send_sem.at[PAIR + k])
        drain(got, send_sem.at[SUMS + k])
    for k, full in enumerate((full0, full1)):
        drain(full.at[:, pl.ds(0, HALF - OWN)], send_sem.at[SLICES + k])
        drain(full.at[:, pl.ds(0, HALF)], send_sem.at[HALVES + k])
    drain(curve.at[1], send_sem.at[CURVE])
    drain(curves, send_sem.at[STAGES])
    drain(turned.at[pl.ds(0, OWN - 8)], send_sem.at[TURN])


def body(modes, targets, pairs, support):
    vmem = pl.BlockSpec(memory_space=pltpu.VMEM)
    hbm = pl.BlockSpec(memory_space=pltpu.HBM)
    both = pl.pallas_call(
        kernel,
        out_shape=jax.ShapeDtypeStruct((16, TARGETS), F32),
        in_specs=[hbm] * 4,
        out_specs=vmem,
        scratch_shapes=[
            pltpu.VMEM((ROWS, TARGETS), BF16),
            pltpu.VMEM((2, TERMS), jnp.int32),
            pltpu.VMEM((8, TARGETS), jnp.int32),
            pltpu.VMEM((LOCAL, MODES), BF16),
            pltpu.VMEM((SLAB, TARGETS + 128), BF16),
            pltpu.VMEM((NX * ROWS, 128), BF16),
            pltpu.VMEM((NX * ROWS, 128), BF16),
            pltpu.VMEM((MODES, TERMS), BF16),
            pltpu.VMEM((MODES, TERMS), BF16),
            pltpu.VMEM((2 * NZ, 512), jnp.int32),
            pltpu.VMEM((LOCAL, TERMS), BF16),
        ]
        + [pltpu.VMEM((GROUP, HALF), F32)] * 9
        + [pltpu.VMEM((NZ - 1, GROUP, OWN), F32)] * 3
        + [pltpu.VMEM((GROUP, TERMS), F32)] * 2
        + [
            pltpu.VMEM((3, GROUP, 128), F32),
            pltpu.VMEM((NZ - 1, GROUP, 128), F32),
            pltpu.VMEM((OWN, 128), F32),
            pltpu.VMEM((128, OWN), F32),
            pltpu.VMEM((OWN, 128), F32),
            pltpu.SemaphoreType.DMA((4,)),
            pltpu.SemaphoreType.DMA((STAGES + 1,)),
            pltpu.SemaphoreType.DMA((STAGES + 1,)),
        ],
        compiler_params=pltpu.CompilerParams(
            collective_id=0, has_side_effects=True, vmem_limit_bytes=64 * 2**20
        ),
        name="regression",
    )(modes, targets, pairs.T, support)
    return both[:8], both[8:]


def solution(mesh):
    rows = P(("snap", "tile"), None)
    return jax.shard_map(
        body,
        mesh=mesh,
        in_specs=(rows, rows, P(), rows),
        out_specs=(rows, rows),
        check_vma=False,
    )
```

```python
import jax
import jax.numpy as jnp
from jax import lax
from jax.experimental import pallas as pl
from jax.experimental.pallas import tpu as pltpu
from jax.sharding import PartitionSpec as P

NX, NY, NZ, NC = 4, 8, 8, 2
RING = NZ * NC
PLANE = NX * NY
MODES = 256
TARGETS = 256
TERMS = 4096
ROWS = 16
SNAPS = 8192
SLAB = NY * ROWS
LOCAL = PLANE * ROWS
OWN = TERMS // RING
HALF = TERMS // NC
GROUP = TARGETS // PLANE
CHUNK = 1024
FAR_FIRST = (4, 3, 5, 2, 6, 1, 7)
NEAR_FIRST = (1, 7, 2, 6, 3, 5, 4)
F32 = jnp.float32
BF16 = jnp.bfloat16
MESH = pl.DeviceIdType.MESH

EXTRA, SLABS, COMPACT, PAIR, SUMS, SLICES, HALVES, CURVE, CURVES, TURN = 7, 8, 11, 12, 15, 18, 20, 22, 24, 26
ARRIVED = 27
STAGES = ARRIVED + 2 * RING


def split(value):
    high = value.astype(BF16)
    low = (value - high.astype(F32)).astype(BF16)
    return jnp.concatenate([high, low], axis=0)


def merge(value):
    return value[:GROUP] + value[GROUP:]


def dot_nt(lhs, rhs):
    return lax.dot_general(lhs, rhs, (((1,), (1,)), ((), ())), preferred_element_type=F32)


def dot_nn(lhs, rhs):
    return jnp.dot(lhs, rhs, preferred_element_type=F32)


def iota(shape, dim):
    return lax.broadcasted_iota(jnp.int32, shape, dim)


def chosen(condition):
    return condition.astype(F32).astype(BF16)


def drain(ref, sem):
    pltpu.make_async_copy(ref, ref, sem).wait()


def kernel(
    modes_ref, targets_ref, pairs_ref, support_ref, out_ref,
    targets_in, pairs_in, support_in, rows, extra, compact, compact_in,
    hot_a, hot_b, terms, library,
    out0, out1, out2, pair0, pair1, pair2, pre0, pre1, pre2, got0, got1, got2,
    full0, full1, curve1, curve2, curves1, curves2, turn, square, turned,
    load_sem, send_sem, recv_sem,
):
    z = lax.axis_index("snap")
    tile = lax.axis_index("tile")
    x = tile // (NY * NC)
    y = (tile // NC) % NY
    core = tile % NC

    def at_plane(step_x, step_y):
        return z, (lax.rem(x + step_x, NX) * NY + lax.rem(y + step_y, NY)) * NC + core

    def at_line(step):
        other = lax.rem(z + step, NZ)
        return other, (other, tile)

    sibling = (z, tile + 1 - 2 * core)

    own_block = pl.ds(pl.multiple_of(y * ROWS, ROWS), ROWS)
    loads = [
        pltpu.make_async_copy(modes_ref, rows.at[own_block], load_sem.at[0]),
        pltpu.make_async_copy(targets_ref, targets_in, load_sem.at[1]),
        pltpu.make_async_copy(support_ref, support_in, load_sem.at[2]),
        pltpu.make_async_copy(pairs_ref, pairs_in, load_sem.at[3]),
    ]
    for load in loads:
        load.start()

    barrier = pltpu.get_barrier_semaphore()
    peers = [(a, b) for a in range(NX) for b in range(NY) if a or b]
    for a, b in peers:
        pl.semaphore_signal(barrier, inc=1, device_id=at_plane(a, b), device_id_type=MESH)
    for step in range(1, NZ):
        pl.semaphore_signal(barrier, inc=1, device_id=at_line(step)[1], device_id_type=MESH)
    pl.semaphore_signal(barrier, inc=1, device_id=sibling, device_id_type=MESH)

    def send(src, dst, stage, device, arrive=None):
        pltpu.make_async_remote_copy(
            src_ref=src, dst_ref=dst, send_sem=send_sem.at[stage],
            recv_sem=recv_sem.at[stage if arrive is None else arrive],
            device_id=device, device_id_type=MESH,
        ).start()

    for load in loads[:3]:
        load.wait()
    extra[own_block, 0:TARGETS] = targets_in[...]
    active = support_in[...].astype(F32)
    extra[own_block, TARGETS:] = jnp.concatenate(
        [active[:, :128], active[:, 128:]], axis=0
    ).astype(BF16)
    pl.semaphore_wait(barrier, len(peers) + NZ - 1 + 1)

    for step in FAR_FIRST:
        send(rows.at[own_block], rows.at[own_block], 0, at_plane(0, step), step - 1)

    def forward(block):
        source = pl.multiple_of(block * ROWS, ROWS)
        for step in (2, 1, 3):
            target = pl.multiple_of(step * SLAB + block * ROWS, ROWS)
            send(
                rows.at[pl.ds(source, ROWS)], rows.at[pl.ds(target, ROWS)], SLABS + step - 1,
                at_plane(step, 0),
            )

    forward(y)
    for step in FAR_FIRST:
        send(extra.at[own_block], extra.at[own_block], EXTRA, at_plane(0, step))

    loads[3].wait()
    pairs = pairs_in[...].astype(F32)
    stacked = jnp.concatenate(
        [pairs[side : side + 1, 512 * k : 512 * k + 512] for side in (0, 1) for k in range(NZ)],
        axis=0,
    ).astype(BF16)
    place = iota((512, 512), 1)
    origin = (place % 256) // 8 * 16 + place // 256 * 8 + place % 8
    terms[...] = dot_nn(stacked, chosen(iota((512, 512), 0) == origin)).astype(jnp.int32)
    index = iota((MODES, OWN), 0)

    def make_hot(c):
        for k in range(NZ):
            from_lane = slice(OWN * c, OWN * c + OWN)
            span = slice(HALF * c + OWN * k, HALF * c + OWN * k + OWN)
            hot_a[:, span] = chosen(index == terms[k : k + 1, from_lane])
            hot_b[:, span] = chosen(index == terms[NZ + k : NZ + k + 1, from_lane])

    make_hot(0)
    for step in NEAR_FIRST:
        drain(rows.at[pl.ds(0, ROWS)], recv_sem.at[step - 1])
        forward(lax.rem(y - step + NY, NY))

    drain(extra.at[pl.ds(0, (NY - 1) * ROWS)], recv_sem.at[EXTRA])
    line = iota((NX * ROWS, TARGETS), 0)
    wanted = (NX * y + line // ROWS) * GROUP + line % ROWS
    pick_targets = chosen((iota((NX * ROWS, TARGETS), 1) == wanted) & (line % ROWS < GROUP))
    line = iota((NX * ROWS, 128), 0)
    wanted = (NX * (y % 4) + line // ROWS) * GROUP + line % ROWS - GROUP
    pick_flags = chosen((iota((NX * ROWS, 128), 1) == wanted) & (line % ROWS >= GROUP))
    compact[...] = (
        dot_nt(pick_targets, extra[:, 0:TARGETS]) + dot_nt(pick_flags, extra[:, TARGETS:])
    ).astype(BF16)
    for step in (2, 1, 3):
        theirs = pl.ds(pl.multiple_of(lax.rem(x + step, NX) * ROWS, ROWS), ROWS)
        send(
            compact.at[theirs], compact_in.at[pl.ds(step * ROWS, ROWS)], COMPACT,
            at_plane(step, 0),
        )
    compact_in[0:ROWS, :] = compact[pl.ds(pl.multiple_of(x * ROWS, ROWS), ROWS), :]

    make_hot(1)

    def build(begin, end):
        for k in range(TERMS // CHUNK):
            span = slice(k * CHUNK, (k + 1) * CHUNK)
            c, first_z = k * CHUNK // HALF, k * CHUNK % HALF // OWN
            constant = jnp.concatenate(
                [
                    terms[NZ + j : NZ + j + 1, OWN * c : OWN * c + OWN]
                    for j in range(first_z, first_z + CHUNK // OWN)
                ],
                axis=1,
            )
            constant = (constant == MODES).astype(F32)
            first = dot_nn(rows[begin:end, :], hot_a[:, span])
            second = dot_nn(rows[begin:end, :], hot_b[:, span]) + constant
            library[begin:end, span] = (first * second).astype(BF16)

    build(0, SLAB)
    square[...] = jnp.zeros_like(square)
    for step in (1, 3, 2):
        drain(rows.at[pl.ds(0, SLAB)], recv_sem.at[SLABS + step - 1])
    build(SLAB, LOCAL)

    drain(compact_in.at[pl.ds(0, (NX - 1) * ROWS)], recv_sem.at[COMPACT])
    given = jnp.concatenate([compact_in[k * ROWS : (k + 1) * ROWS, :] for k in range(NX)], axis=1)
    own_half = pl.ds(pl.multiple_of(core * HALF, HALF), HALF)
    their_half = pl.ds(pl.multiple_of((1 - core) * HALF, HALF), HALF)
    own_terms = pl.ds(pl.multiple_of(core * HALF + z * OWN, OWN), OWN)
    own_slice = pl.ds(pl.multiple_of(z * OWN, OWN), OWN)

    def squares(vector):
        return jnp.sum(vector * vector, axis=1, keepdims=True)

    diagonal = iota((GROUP, 128), 0) == iota((GROUP, 128), 1)

    def to_row(column):
        return jnp.sum(jnp.where(diagonal, column, 0.0), axis=0, keepdims=True)

    def to_column(row):
        return jnp.sum(jnp.where(diagonal, row, 0.0), axis=1, keepdims=True)

    def scatter_sums(lhs, finish, out, pair, pre, got, at, image=None, curve=None, curves=None):
        if image is not None:
            curve[0] = to_row(squares(image))
            send(curve.at[0], curve.at[1], CURVE + at - 1, sibling)
        out[...] = finish(dot_nn(lhs, library[:, their_half]))
        send(out, pair, PAIR + at, sibling)
        own = finish(dot_nn(lhs, library[:, own_half]))
        if image is not None:
            drain(curve.at[1], recv_sem.at[CURVE + at - 1])
            curve[2] = curve[0] + curve[1]
        drain(pair, recv_sem.at[PAIR + at])
        pre[...] = own + pair[...]
        for step in FAR_FIRST:
            other, device = at_line(step)
            theirs = pl.ds(pl.multiple_of(other * OWN, OWN), OWN)
            send(pre.at[:, theirs], got.at[step - 1], SUMS + at, device)
            if image is not None:
                send(curve.at[2], curves.at[step - 1], CURVES + at - 1, device)

    def sum_up(pre, got, at):
        drain(got, recv_sem.at[SUMS + at])
        total = pre[:, own_slice]
        for step in range(1, NZ):
            total = total + got[step - 1]
        return total * mask * (1.0 / SNAPS)

    def curvature(curve, curves, at):
        drain(curves, recv_sem.at[CURVES + at - 1])
        total = curve[2]
        for step in range(1, NZ):
            total = total + curves[step - 1]
        return to_column(total) * (1.0 / SNAPS)

    def gather_terms(value, full, at):
        arrived = ARRIVED + RING * at

        def slice_of(side, step):
            begin = side * HALF + lax.rem(z - step + NZ, NZ) * OWN
            return full.at[:, pl.ds(pl.multiple_of(begin, OWN), OWN)]

        def forward(step):
            send(slice_of(core, step), slice_of(core, step), HALVES + at, sibling, arrived + NZ + step)

        def wait(side, steps):
            for step in steps:
                slot = arrived + step if side == 0 else arrived + NZ + step
                drain(full.at[:, pl.ds(0, OWN)], recv_sem.at[slot])
                if side == 0:
                    forward(step)

        def product(side, steps):
            total = None
            for step in steps:
                which = core if side == 0 else 1 - core
                begin = which * HALF + lax.rem(z - step + NZ, NZ) * OWN
                span = pl.ds(pl.multiple_of(begin, OWN), OWN)
                term = dot_nt(split(full[:, span]), library[:, span])
                total = term if total is None else total + term
            return total

        full[:, own_terms] = value
        for step in FAR_FIRST:
            send(
                slice_of(core, 0), slice_of(core, 0), SLICES + at, at_line(step)[1], arrived + step
            )
        forward(0)
        wait(0, (1, 7))
        image = product(0, (0, 1, 7))
        wait(0, (2, 6))
        wait(1, (0,))
        image = image + product(0, (2, 6)) + product(1, (0,))
        wait(0, (3, 5))
        wait(1, (1, 7))
        image = image + product(0, (3, 5)) + product(1, (1, 7))
        wait(0, (4,))
        wait(1, (2, 6))
        image = image + product(0, (4,)) + product(1, (2, 6))
        wait(1, (3, 5))
        image = image + product(1, (3, 5))
        wait(1, (4,))
        return merge(image + product(1, (4,)))

    scatter_sums(given, lambda value: value[:GROUP], out0, pair0, pre0, got0, 0)
    line, lane = iota((LOCAL, OWN), 0), iota((LOCAL, OWN), 1)
    from_x = lax.rem(x - line // 128 + NX, NX)
    pick = (
        (from_x * NY + line % 128 // 16 == lane // 8)
        & (line % 16 // 8 == y // 4)
        & (line % 8 == lane % 8)
    )
    mask = dot_nn(given, chosen(pick))[GROUP:]

    direction = sum_up(pre0, got0, 0)
    image = gather_terms(direction, full0, 0)
    scatter_sums(split(image), merge, out1, pair1, pre1, got1, 1, image, curve1, curves1)
    energy = squares(full0[...])
    step_len = energy / curvature(curve1, curves1, 1)
    coeffs = step_len * direction
    resid = direction - step_len * sum_up(pre1, got1, 1)
    next_image = gather_terms(resid, full1, 1)
    fresh = squares(full1[...])
    ratio = fresh / energy
    direction = resid + ratio * direction
    image = next_image + ratio * image
    scatter_sums(split(image), merge, out2, pair2, pre2, got2, 2, image, curve2, curves2)
    step_len = fresh / curvature(curve2, curves2, 2)
    coeffs = coeffs + step_len * direction
    resid = resid - step_len * sum_up(pre2, got2, 2)

    group = NX * y + x
    at = group % (PLANE // 2) * GROUP
    square[pl.ds(pl.multiple_of(at, GROUP), GROUP), :] = coeffs
    square[pl.ds(pl.multiple_of(lax.rem(at + 64, 128), GROUP), GROUP), :] = resid
    turn[...] = square[...].T
    here = pl.ds(pl.multiple_of((x * NY + y) * 8, 8), 8)
    for a, b in sorted(peers, key=lambda peer: -min(peer[0], NX - peer[0]) - min(peer[1], NY - peer[1])):
        spot = lax.rem(x + a, NX) * NY + lax.rem(y + b, NY)
        theirs = pl.ds(pl.multiple_of(spot * 8, 8), 8)
        send(turn.at[theirs], turned.at[here], TURN, at_plane(a, b))
    turned[here, :] = turn[here, :]
    drain(turned.at[pl.ds(0, OWN - 8)], recv_sem.at[TURN])
    lane = iota((8, 128), 1) // GROUP
    for side in range(2):
        left = jnp.zeros((8, 128), F32)
        right = left
        for a in range(NX):
            for b in range(4 * side, 4 * side + 4):
                block = turned[8 * (a * NY + b) : 8 * (a * NY + b) + 8, :]
                at = (NX * b + a) % (PLANE // 2)
                left = jnp.where(lane == at, block, left)
                right = jnp.where(lane == (at + 8) % 16, block, right)
        out_ref[0:8, 128 * side : 128 * side + 128] = left
        out_ref[8:16, 128 * side : 128 * side + 128] = pltpu.roll(right, 64, 1)

    drain(rows.at[pl.ds(0, (NY - 1) * ROWS)], send_sem.at[0])
    drain(extra.at[pl.ds(0, (NY - 1) * ROWS)], send_sem.at[EXTRA])
    for step in (1, 2, 3):
        drain(rows.at[pl.ds(0, SLAB)], send_sem.at[SLABS + step - 1])
    drain(compact_in.at[pl.ds(0, (NX - 1) * ROWS)], send_sem.at[COMPACT])
    for k, (pair, got) in enumerate(((pair0, got0), (pair1, got1), (pair2, got2))):
        drain(pair, send_sem.at[PAIR + k])
        drain(got, send_sem.at[SUMS + k])
    for k, full in enumerate((full0, full1)):
        drain(full.at[:, pl.ds(0, HALF - OWN)], send_sem.at[SLICES + k])
        drain(full.at[:, pl.ds(0, HALF)], send_sem.at[HALVES + k])
    for k, (curve, curves) in enumerate(((curve1, curves1), (curve2, curves2))):
        drain(curve.at[1], send_sem.at[CURVE + k])
        drain(curves, send_sem.at[CURVES + k])
    drain(turned.at[pl.ds(0, OWN - 8)], send_sem.at[TURN])


def body(modes, targets, pairs, support):
    vmem = pl.BlockSpec(memory_space=pltpu.VMEM)
    hbm = pl.BlockSpec(memory_space=pltpu.HBM)
    both = pl.pallas_call(
        kernel,
        out_shape=jax.ShapeDtypeStruct((16, TARGETS), F32),
        in_specs=[hbm] * 4,
        out_specs=vmem,
        scratch_shapes=[
            pltpu.VMEM((ROWS, TARGETS), BF16),
            pltpu.VMEM((2, TERMS), jnp.int32),
            pltpu.VMEM((8, TARGETS), jnp.int32),
            pltpu.VMEM((LOCAL, MODES), BF16),
            pltpu.VMEM((SLAB, TARGETS + 128), BF16),
            pltpu.VMEM((NX * ROWS, 128), BF16),
            pltpu.VMEM((NX * ROWS, 128), BF16),
            pltpu.VMEM((MODES, TERMS), BF16),
            pltpu.VMEM((MODES, TERMS), BF16),
            pltpu.VMEM((2 * NZ, 512), jnp.int32),
            pltpu.VMEM((LOCAL, TERMS), BF16),
        ]
        + [pltpu.VMEM((GROUP, HALF), F32)] * 9
        + [pltpu.VMEM((NZ - 1, GROUP, OWN), F32)] * 3
        + [pltpu.VMEM((GROUP, TERMS), F32)] * 2
        + [
            pltpu.VMEM((3, 1, 128), F32),
            pltpu.VMEM((3, 1, 128), F32),
            pltpu.VMEM((NZ - 1, 1, 128), F32),
            pltpu.VMEM((NZ - 1, 1, 128), F32),
            pltpu.VMEM((OWN, 128), F32),
            pltpu.VMEM((128, OWN), F32),
            pltpu.VMEM((OWN, 128), F32),
            pltpu.SemaphoreType.DMA((4,)),
            pltpu.SemaphoreType.DMA((ARRIVED,)),
            pltpu.SemaphoreType.DMA((STAGES,)),
        ],
        compiler_params=pltpu.CompilerParams(
            collective_id=0, has_side_effects=True, vmem_limit_bytes=48 * 2**20
        ),
        name="regression",
    )(*(pltpu.with_memory_space_constraint(v, pltpu.HBM) for v in (modes, targets, pairs.T, support)))
    return both[:8], both[8:]


def solution(mesh):
    rows = P(("snap", "tile"), None)
    return jax.shard_map(
        body,
        mesh=mesh,
        in_specs=(rows, rows, P(), rows),
        out_specs=(rows, rows),
        check_vma=False,
    )
```

```python
import jax
import jax.numpy as jnp
from jax import lax
from jax.experimental import pallas as pl
from jax.experimental.pallas import tpu as pltpu
from jax.sharding import PartitionSpec as P

NX, NY, NZ, NC = 4, 8, 8, 2
RING = NZ * NC
PLANE = NX * NY
MODES = 256
TARGETS = 256
TERMS = 4096
ROWS = 16
SNAPS = 8192
SLAB = NY * ROWS
LOCAL = PLANE * ROWS
OWN = TERMS // RING
HALF = TERMS // NC
GROUP = TARGETS // PLANE
CHUNK = 1024
FAR_FIRST = (4, 3, 5, 2, 6, 1, 7)
NEAR_FIRST = (1, 7, 2, 6, 3, 5, 4)
F32 = jnp.float32
BF16 = jnp.bfloat16
MESH = pl.DeviceIdType.MESH

EXTRA, SLABS, COMPACT, PAIR, SUMS, SLICES, HALVES, CURVE, CURVES, TURN = 7, 8, 11, 12, 15, 18, 20, 22, 24, 26
ARRIVED = 27
STAGES = ARRIVED + 2 * RING


def split(value):
    high = value.astype(BF16)
    low = (value - high.astype(F32)).astype(BF16)
    return jnp.concatenate([high, low], axis=0)


def merge(value):
    return value[:GROUP] + value[GROUP:]


def dot_nt(lhs, rhs):
    return lax.dot_general(lhs, rhs, (((1,), (1,)), ((), ())), preferred_element_type=F32)


def dot_nn(lhs, rhs):
    return jnp.dot(lhs, rhs, preferred_element_type=F32)


def iota(shape, dim):
    return lax.broadcasted_iota(jnp.int32, shape, dim)


def chosen(condition):
    return condition.astype(F32).astype(BF16)


def drain(ref, sem):
    pltpu.make_async_copy(ref, ref, sem).wait()


def kernel(
    modes_ref, targets_ref, pairs_ref, support_ref, out_ref,
    targets_in, pairs_in, support_in, rows, extra, compact, compact_in,
    hot_a, hot_b, terms, library,
    out0, out1, out2, mine0, mine1, mine2, pair0, pair1, pair2, pre0, pre1, pre2, got0, got1, got2,
    full0, full1, curve1, curve2, curves1, curves2, turn, square, turned,
    load_sem, send_sem, recv_sem,
):
    z = lax.axis_index("snap")
    tile = lax.axis_index("tile")
    x = tile // (NY * NC)
    y = (tile // NC) % NY
    core = tile % NC

    def at_plane(step_x, step_y):
        return z, (lax.rem(x + step_x, NX) * NY + lax.rem(y + step_y, NY)) * NC + core

    def at_line(step):
        other = lax.rem(z + step, NZ)
        return other, (other, tile)

    sibling = (z, tile + 1 - 2 * core)
    opposite = lax.rem(z + NZ // 2, NZ)
    across = (opposite, tile + 1 - 2 * core)

    own_block = pl.ds(pl.multiple_of(y * ROWS, ROWS), ROWS)
    loads = [
        pltpu.make_async_copy(modes_ref, rows.at[own_block], load_sem.at[0]),
        pltpu.make_async_copy(targets_ref, targets_in, load_sem.at[1]),
        pltpu.make_async_copy(support_ref, support_in, load_sem.at[2]),
        pltpu.make_async_copy(pairs_ref, pairs_in, load_sem.at[3]),
    ]
    for load in loads:
        load.start()

    barrier = pltpu.get_barrier_semaphore()
    peers = [(a, b) for a in range(NX) for b in range(NY) if a or b]
    for a, b in peers:
        pl.semaphore_signal(barrier, inc=1, device_id=at_plane(a, b), device_id_type=MESH)
    for step in range(1, NZ):
        pl.semaphore_signal(barrier, inc=1, device_id=at_line(step)[1], device_id_type=MESH)
    pl.semaphore_signal(barrier, inc=1, device_id=sibling, device_id_type=MESH)
    pl.semaphore_signal(barrier, inc=1, device_id=across, device_id_type=MESH)

    def send(src, dst, stage, device, arrive=None):
        pltpu.make_async_remote_copy(
            src_ref=src, dst_ref=dst, send_sem=send_sem.at[stage],
            recv_sem=recv_sem.at[stage if arrive is None else arrive],
            device_id=device, device_id_type=MESH,
        ).start()

    for load in loads[:3]:
        load.wait()
    extra[own_block, 0:TARGETS] = targets_in[...]
    active = support_in[...].astype(F32)
    extra[own_block, TARGETS:] = jnp.concatenate(
        [active[:, :128], active[:, 128:]], axis=0
    ).astype(BF16)
    pl.semaphore_wait(barrier, len(peers) + NZ - 1 + 2)

    for step in FAR_FIRST:
        send(rows.at[own_block], rows.at[own_block], 0, at_plane(0, step), step - 1)

    def forward(block):
        source = pl.multiple_of(block * ROWS, ROWS)
        for step in (2, 1, 3):
            target = pl.multiple_of(step * SLAB + block * ROWS, ROWS)
            send(
                rows.at[pl.ds(source, ROWS)], rows.at[pl.ds(target, ROWS)], SLABS + step - 1,
                at_plane(step, 0),
            )

    forward(y)
    for step in FAR_FIRST:
        send(extra.at[own_block], extra.at[own_block], EXTRA, at_plane(0, step))

    loads[3].wait()
    pairs = pairs_in[...].astype(F32)
    stacked = jnp.concatenate(
        [pairs[side : side + 1, 512 * k : 512 * k + 512] for side in (0, 1) for k in range(NZ)],
        axis=0,
    ).astype(BF16)
    place = iota((512, 512), 1)
    origin = (place % 256) // 8 * 16 + place // 256 * 8 + place % 8
    terms[...] = dot_nn(stacked, chosen(iota((512, 512), 0) == origin)).astype(jnp.int32)
    index = iota((MODES, OWN), 0)

    def make_hot(c):
        for k in range(NZ):
            from_lane = slice(OWN * c, OWN * c + OWN)
            span = slice(HALF * c + OWN * k, HALF * c + OWN * k + OWN)
            hot_a[:, span] = chosen(index == terms[k : k + 1, from_lane])
            hot_b[:, span] = chosen(index == terms[NZ + k : NZ + k + 1, from_lane])

    make_hot(0)
    for step in NEAR_FIRST:
        drain(rows.at[pl.ds(0, ROWS)], recv_sem.at[step - 1])
        forward(lax.rem(y - step + NY, NY))

    drain(extra.at[pl.ds(0, (NY - 1) * ROWS)], recv_sem.at[EXTRA])
    line = iota((NX * ROWS, TARGETS), 0)
    wanted = (NX * y + line // ROWS) * GROUP + line % ROWS
    pick_targets = chosen((iota((NX * ROWS, TARGETS), 1) == wanted) & (line % ROWS < GROUP))
    line = iota((NX * ROWS, 128), 0)
    wanted = (NX * (y % 4) + line // ROWS) * GROUP + line % ROWS - GROUP
    pick_flags = chosen((iota((NX * ROWS, 128), 1) == wanted) & (line % ROWS >= GROUP))
    compact[...] = (
        dot_nt(pick_targets, extra[:, 0:TARGETS]) + dot_nt(pick_flags, extra[:, TARGETS:])
    ).astype(BF16)
    for step in (2, 1, 3):
        theirs = pl.ds(pl.multiple_of(lax.rem(x + step, NX) * ROWS, ROWS), ROWS)
        send(
            compact.at[theirs], compact_in.at[pl.ds(step * ROWS, ROWS)], COMPACT,
            at_plane(step, 0),
        )
    compact_in[0:ROWS, :] = compact[pl.ds(pl.multiple_of(x * ROWS, ROWS), ROWS), :]

    make_hot(1)

    def build(begin, end):
        for k in range(TERMS // CHUNK):
            span = slice(k * CHUNK, (k + 1) * CHUNK)
            c, first_z = k * CHUNK // HALF, k * CHUNK % HALF // OWN
            constant = jnp.concatenate(
                [
                    terms[NZ + j : NZ + j + 1, OWN * c : OWN * c + OWN]
                    for j in range(first_z, first_z + CHUNK // OWN)
                ],
                axis=1,
            )
            constant = (constant == MODES).astype(F32)
            first = dot_nn(rows[begin:end, :], hot_a[:, span])
            second = dot_nn(rows[begin:end, :], hot_b[:, span]) + constant
            library[begin:end, span] = (first * second).astype(BF16)

    build(0, SLAB)
    square[...] = jnp.zeros_like(square)
    for step in (1, 3, 2):
        drain(rows.at[pl.ds(0, SLAB)], recv_sem.at[SLABS + step - 1])
    build(SLAB, LOCAL)

    drain(compact_in.at[pl.ds(0, (NX - 1) * ROWS)], recv_sem.at[COMPACT])
    given = jnp.concatenate([compact_in[k * ROWS : (k + 1) * ROWS, :] for k in range(NX)], axis=1)
    own_half = pl.ds(pl.multiple_of(core * HALF, HALF), HALF)
    their_half = pl.ds(pl.multiple_of((1 - core) * HALF, HALF), HALF)
    own_terms = pl.ds(pl.multiple_of(core * HALF + z * OWN, OWN), OWN)
    own_slice = pl.ds(pl.multiple_of(z * OWN, OWN), OWN)

    def squares(vector):
        return jnp.sum(vector * vector, axis=1, keepdims=True)

    diagonal = iota((GROUP, 128), 0) == iota((GROUP, 128), 1)

    def to_row(column):
        return jnp.sum(jnp.where(diagonal, column, 0.0), axis=0, keepdims=True)

    def to_column(row):
        return jnp.sum(jnp.where(diagonal, row, 0.0), axis=1, keepdims=True)

    def scatter_sums(lhs, finish, out, mine, pair, pre, got, at, image=None, curve=None, curves=None):
        if image is not None:
            curve[0] = to_row(squares(image))
            send(curve.at[0], curve.at[1], CURVE + at - 1, sibling)
        out[...] = finish(dot_nn(lhs, library[:, their_half]))
        send(out, pair, PAIR + at, sibling)
        far = pl.ds(pl.multiple_of(opposite * OWN, OWN), OWN)
        send(out.at[:, far], got.at[NZ - 1], SUMS + at, across)
        mine[...] = finish(dot_nn(lhs, library[:, own_half]))
        send(mine.at[:, far], got.at[NZ // 2 - 1], SUMS + at, at_line(NZ // 2)[1])
        if image is not None:
            drain(curve.at[1], recv_sem.at[CURVE + at - 1])
            curve[2] = curve[0] + curve[1]
        drain(pair, recv_sem.at[PAIR + at])
        pre[...] = mine[...] + pair[...]
        for step in FAR_FIRST:
            other, device = at_line(step)
            theirs = pl.ds(pl.multiple_of(other * OWN, OWN), OWN)
            if step != NZ // 2:
                send(pre.at[:, theirs], got.at[step - 1], SUMS + at, device)
            if image is not None:
                send(curve.at[2], curves.at[step - 1], CURVES + at - 1, device)

    def sum_up(pre, got, at):
        drain(got, recv_sem.at[SUMS + at])
        total = pre[:, own_slice]
        for step in range(NZ):
            total = total + got[step]
        return total * mask * (1.0 / SNAPS)

    def curvature(curve, curves, at):
        drain(curves, recv_sem.at[CURVES + at - 1])
        total = curve[2]
        for step in range(1, NZ):
            total = total + curves[step - 1]
        return to_column(total) * (1.0 / SNAPS)

    def gather_terms(value, full, at):
        arrived = ARRIVED + RING * at

        def slice_of(side, step):
            begin = side * HALF + lax.rem(z - step + NZ, NZ) * OWN
            return full.at[:, pl.ds(pl.multiple_of(begin, OWN), OWN)]

        def forward(step):
            send(slice_of(core, step), slice_of(core, step), HALVES + at, sibling, arrived + NZ + step)

        def wait(side, steps):
            for step in steps:
                slot = arrived + step if side == 0 else arrived + NZ + step
                drain(full.at[:, pl.ds(0, OWN)], recv_sem.at[slot])
                if side == 0 and step != NZ // 2:
                    forward(step)

        def product(side, steps):
            total = None
            for step in steps:
                which = core if side == 0 else 1 - core
                begin = which * HALF + lax.rem(z - step + NZ, NZ) * OWN
                span = pl.ds(pl.multiple_of(begin, OWN), OWN)
                term = dot_nt(split(full[:, span]), library[:, span])
                total = term if total is None else total + term
            return total

        full[:, own_terms] = value
        for step in FAR_FIRST:
            send(
                slice_of(core, 0), slice_of(core, 0), SLICES + at, at_line(step)[1], arrived + step
            )
            if step == NZ // 2:
                send(slice_of(core, 0), slice_of(core, 0), SLICES + at, across, arrived + NZ + step)
        forward(0)
        wait(0, (1, 7))
        image = product(0, (0, 1, 7))
        wait(0, (2, 6))
        wait(1, (0,))
        image = image + product(0, (2, 6)) + product(1, (0,))
        wait(0, (3, 5))
        wait(1, (1, 7))
        image = image + product(0, (3, 5)) + product(1, (1, 7))
        wait(1, (2, 6))
        image = image + product(1, (2, 6))
        wait(0, (4,))
        wait(1, (4, 3, 5))
        return merge(image + product(0, (4,)) + product(1, (4, 3, 5)))

    scatter_sums(given, lambda value: value[:GROUP], out0, mine0, pair0, pre0, got0, 0)
    line, lane = iota((LOCAL, OWN), 0), iota((LOCAL, OWN), 1)
    from_x = lax.rem(x - line // 128 + NX, NX)
    pick = (
        (from_x * NY + line % 128 // 16 == lane // 8)
        & (line % 16 // 8 == y // 4)
        & (line % 8 == lane % 8)
    )
    mask = dot_nn(given, chosen(pick))[GROUP:]

    direction = sum_up(pre0, got0, 0)
    image = gather_terms(direction, full0, 0)
    scatter_sums(split(image), merge, out1, mine1, pair1, pre1, got1, 1, image, curve1, curves1)
    energy = squares(full0[...])
    step_len = energy / curvature(curve1, curves1, 1)
    coeffs = step_len * direction
    resid = direction - step_len * sum_up(pre1, got1, 1)
    next_image = gather_terms(resid, full1, 1)
    fresh = squares(full1[...])
    ratio = fresh / energy
    direction = resid + ratio * direction
    image = next_image + ratio * image
    scatter_sums(split(image), merge, out2, mine2, pair2, pre2, got2, 2, image, curve2, curves2)
    step_len = fresh / curvature(curve2, curves2, 2)
    coeffs = coeffs + step_len * direction
    resid = resid - step_len * sum_up(pre2, got2, 2)

    group = NX * y + x
    at = group % (PLANE // 2) * GROUP
    square[pl.ds(pl.multiple_of(at, GROUP), GROUP), :] = coeffs
    square[pl.ds(pl.multiple_of(lax.rem(at + 64, 128), GROUP), GROUP), :] = resid
    turn[...] = square[...].T
    here = pl.ds(pl.multiple_of((x * NY + y) * 8, 8), 8)
    for a, b in sorted(peers, key=lambda peer: -min(peer[0], NX - peer[0]) - min(peer[1], NY - peer[1])):
        spot = lax.rem(x + a, NX) * NY + lax.rem(y + b, NY)
        theirs = pl.ds(pl.multiple_of(spot * 8, 8), 8)
        send(turn.at[theirs], turned.at[here], TURN, at_plane(a, b))
    turned[here, :] = turn[here, :]
    drain(rows.at[pl.ds(0, (NY - 1) * ROWS)], send_sem.at[0])
    drain(extra.at[pl.ds(0, (NY - 1) * ROWS)], send_sem.at[EXTRA])
    for step in (1, 2, 3):
        drain(rows.at[pl.ds(0, SLAB)], send_sem.at[SLABS + step - 1])
    drain(compact_in.at[pl.ds(0, (NX - 1) * ROWS)], send_sem.at[COMPACT])
    for k, (pair, got) in enumerate(((pair0, got0), (pair1, got1), (pair2, got2))):
        drain(pair, send_sem.at[PAIR + k])
        drain(got, send_sem.at[SUMS + k])
    for k, full in enumerate((full0, full1)):
        drain(full.at[:, pl.ds(0, HALF)], send_sem.at[SLICES + k])
        drain(full.at[:, pl.ds(0, HALF - OWN)], send_sem.at[HALVES + k])
    for k, (curve, curves) in enumerate(((curve1, curves1), (curve2, curves2))):
        drain(curve.at[1], send_sem.at[CURVE + k])
        drain(curves, send_sem.at[CURVES + k])
    drain(turned.at[pl.ds(0, OWN - 8)], recv_sem.at[TURN])
    lane = iota((8, 128), 1) // GROUP
    for side in range(2):
        left = jnp.zeros((8, 128), F32)
        right = left
        for a in range(NX):
            for b in range(4 * side, 4 * side + 4):
                block = turned[8 * (a * NY + b) : 8 * (a * NY + b) + 8, :]
                at = (NX * b + a) % (PLANE // 2)
                left = jnp.where(lane == at, block, left)
                right = jnp.where(lane == (at + 8) % 16, block, right)
        out_ref[0:8, 128 * side : 128 * side + 128] = left
        out_ref[8:16, 128 * side : 128 * side + 128] = pltpu.roll(right, 64, 1)

    drain(turned.at[pl.ds(0, OWN - 8)], send_sem.at[TURN])


def body(modes, targets, pairs, support):
    vmem = pl.BlockSpec(memory_space=pltpu.VMEM)
    hbm = pl.BlockSpec(memory_space=pltpu.HBM)
    both = pl.pallas_call(
        kernel,
        out_shape=jax.ShapeDtypeStruct((16, TARGETS), F32),
        in_specs=[hbm] * 4,
        out_specs=vmem,
        scratch_shapes=[
            pltpu.VMEM((ROWS, TARGETS), BF16),
            pltpu.VMEM((2, TERMS), jnp.int32),
            pltpu.VMEM((8, TARGETS), jnp.int32),
            pltpu.VMEM((LOCAL, MODES), BF16),
            pltpu.VMEM((SLAB, TARGETS + 128), BF16),
            pltpu.VMEM((NX * ROWS, 128), BF16),
            pltpu.VMEM((NX * ROWS, 128), BF16),
            pltpu.VMEM((MODES, TERMS), BF16),
            pltpu.VMEM((MODES, TERMS), BF16),
            pltpu.VMEM((2 * NZ, 512), jnp.int32),
            pltpu.VMEM((LOCAL, TERMS), BF16),
        ]
        + [pltpu.VMEM((GROUP, HALF), F32)] * 12
        + [pltpu.VMEM((NZ, GROUP, OWN), F32)] * 3
        + [pltpu.VMEM((GROUP, TERMS), F32)] * 2
        + [
            pltpu.VMEM((3, 1, 128), F32),
            pltpu.VMEM((3, 1, 128), F32),
            pltpu.VMEM((NZ - 1, 1, 128), F32),
            pltpu.VMEM((NZ - 1, 1, 128), F32),
            pltpu.VMEM((OWN, 128), F32),
            pltpu.VMEM((128, OWN), F32),
            pltpu.VMEM((OWN, 128), F32),
            pltpu.SemaphoreType.DMA((4,)),
            pltpu.SemaphoreType.DMA((ARRIVED,)),
            pltpu.SemaphoreType.DMA((STAGES,)),
        ],
        compiler_params=pltpu.CompilerParams(
            collective_id=0, has_side_effects=True, vmem_limit_bytes=48 * 2**20
        ),
        name="regression",
    )(*(pltpu.with_memory_space_constraint(v, pltpu.HBM) for v in (modes, targets, pairs.T, support)))
    return both[:8], both[8:]


def solution(mesh):
    rows = P(("snap", "tile"), None)
    return jax.shard_map(
        body,
        mesh=mesh,
        in_specs=(rows, rows, P(), rows),
        out_specs=(rows, rows),
        check_vma=False,
    )
```

```python
import jax
import jax.numpy as jnp
from jax import lax
from jax.experimental import pallas as pl
from jax.experimental.pallas import tpu as pltpu
from jax.sharding import PartitionSpec as P

NX, NY, NZ, NC = 4, 8, 8, 2
RING = NZ * NC
PLANE = NX * NY
MODES = 256
TARGETS = 256
TERMS = 4096
ROWS = 16
SNAPS = 8192
SLAB = NY * ROWS
BAND = NX * ROWS
EARLY = 5 * BAND
LOCAL = PLANE * ROWS
OWN = TERMS // RING
HALF = TERMS // NC
GROUP = TARGETS // PLANE
CHUNK = 1024
FAR_FIRST = (4, 3, 5, 2, 6, 1, 7)
NEAR_FIRST = (1, 7, 2, 6, 3, 5, 4)
BAND_OF = (0, 1, 3, 5, 7, 6, 4, 2)
F32 = jnp.float32
BF16 = jnp.bfloat16
MESH = pl.DeviceIdType.MESH

BANDS, COMPACT, PAIR, SUMS, SLICES, HALVES, CURVE, CURVES, TURN = 7, 9, 10, 13, 16, 18, 20, 22, 24
ARRIVED = 25
STAGES = ARRIVED + 2 * RING


def split(value):
    high = value.astype(BF16)
    low = (value - high.astype(F32)).astype(BF16)
    return jnp.concatenate([high, low], axis=0)


def merge(value):
    return value[:GROUP] + value[GROUP:]


def dot_nt(lhs, rhs):
    return lax.dot_general(lhs, rhs, (((1,), (1,)), ((), ())), preferred_element_type=F32)


def dot_nn(lhs, rhs):
    return jnp.dot(lhs, rhs, preferred_element_type=F32)


def iota(shape, dim):
    return lax.broadcasted_iota(jnp.int32, shape, dim)


def chosen(condition):
    return condition.astype(F32).astype(BF16)


def drain(ref, sem):
    pltpu.make_async_copy(ref, ref, sem).wait()


def kernel(
    modes_ref, targets_ref, pairs_ref, support_ref, out_ref,
    targets_in, pairs_in, support_in, rows, extra, compact, compact_in, reorder, pick_mask,
    hot_a, hot_b, terms, library,
    out0, out1, out2, mine0, mine1, mine2, pair0, pair1, pair2, pre0, pre1, pre2, got0, got1, got2,
    full0, full1, curve1, curve2, curves1, curves2, turn, square, turned,
    load_sem, send_sem, recv_sem,
):
    z = lax.axis_index("snap")
    tile = lax.axis_index("tile")
    x = tile // (NY * NC)
    y = (tile // NC) % NY
    core = tile % NC

    def at_plane(step_x, step_y):
        return z, (lax.rem(x + step_x, NX) * NY + lax.rem(y + step_y, NY)) * NC + core

    def at_line(step):
        other = lax.rem(z + step, NZ)
        return other, (other, tile)

    sibling = (z, tile + 1 - 2 * core)
    opposite = lax.rem(z + NZ // 2, NZ)
    across = (opposite, tile + 1 - 2 * core)

    own_block = pl.ds(pl.multiple_of(y * ROWS, ROWS), ROWS)
    loads = [
        pltpu.make_async_copy(modes_ref, rows.at[pl.ds(0, ROWS)], load_sem.at[0]),
        pltpu.make_async_copy(targets_ref, targets_in, load_sem.at[1]),
        pltpu.make_async_copy(support_ref, support_in, load_sem.at[2]),
        pltpu.make_async_copy(pairs_ref, pairs_in, load_sem.at[3]),
    ]
    for load in loads:
        load.start()

    barrier = pltpu.get_barrier_semaphore()
    peers = [(a, b) for a in range(NX) for b in range(NY) if a or b]
    for a, b in peers:
        pl.semaphore_signal(barrier, inc=1, device_id=at_plane(a, b), device_id_type=MESH)
    for step in range(1, NZ):
        pl.semaphore_signal(barrier, inc=1, device_id=at_line(step)[1], device_id_type=MESH)
    pl.semaphore_signal(barrier, inc=1, device_id=sibling, device_id_type=MESH)
    pl.semaphore_signal(barrier, inc=1, device_id=across, device_id_type=MESH)

    def send(src, dst, stage, device, arrive=None):
        pltpu.make_async_remote_copy(
            src_ref=src, dst_ref=dst, send_sem=send_sem.at[stage],
            recv_sem=recv_sem.at[stage if arrive is None else arrive],
            device_id=device, device_id_type=MESH,
        ).start()

    def block(step_y, step_x):
        return rows.at[pl.ds(BAND_OF[step_y] * BAND + step_x * ROWS, ROWS)]

    extra[...] = jnp.zeros_like(extra)
    for load in loads[:3]:
        load.wait()
    extra[own_block, 0:TARGETS] = targets_in[...]
    active = support_in[...].astype(F32)
    extra[own_block, TARGETS:] = jnp.concatenate(
        [active[:, :128], active[:, 128:]], axis=0
    ).astype(BF16)
    pl.semaphore_wait(barrier, len(peers) + NZ - 1 + 2)

    for step in FAR_FIRST:
        send(block(0, 0), block(step, 0), 0, at_plane(0, step), step - 1)

    def forward(step_y):
        for step in (2, 1, 3):
            stage = BANDS + (BAND_OF[step_y] >= EARLY // BAND)
            send(block(step_y, 0), block(step_y, step), stage, at_plane(step, 0))

    def pass_on(steps):
        for step in steps:
            drain(rows.at[pl.ds(0, ROWS)], recv_sem.at[step - 1])
            forward(step)

    forward(0)

    line = iota((PLANE * ROWS, TARGETS), 0)
    ring = line // ROWS % NY * NX + line // (ROWS * NY)
    pick_targets = chosen(
        (iota((PLANE * ROWS, TARGETS), 1) == ring * GROUP + line % ROWS) & (line % ROWS < GROUP)
    )
    line = iota((PLANE * ROWS, 128), 0)
    ring = (line // ROWS % NY * NX + line // (ROWS * NY)) % (PLANE // 2)
    pick_flags = chosen(
        (iota((PLANE * ROWS, 128), 1) == ring * GROUP + line % ROWS - GROUP) & (line % ROWS >= GROUP)
    )
    compact[...] = (
        dot_nt(pick_targets, extra[:, 0:TARGETS]) + dot_nt(pick_flags, extra[:, TARGETS:])
    ).astype(BF16)
    far_first = sorted(peers, key=lambda peer: -min(peer[0], NX - peer[0]) - min(peer[1], NY - peer[1]))
    for a, b in far_first:
        spot = lax.rem(x + a, NX) * NY + lax.rem(y + b, NY)
        send(
            compact.at[pl.ds(pl.multiple_of(spot * ROWS, ROWS), ROWS)],
            compact_in.at[pl.ds(pl.multiple_of((a * NY + y) * ROWS, ROWS), ROWS)],
            COMPACT, at_plane(a, b),
        )
    compact_in[own_block, :] = compact[
        pl.ds(pl.multiple_of((x * NY + y) * ROWS, ROWS), ROWS), :
    ]

    loads[3].wait()
    pass_on((1, 7))
    pairs = pairs_in[...].astype(F32)
    stacked = jnp.concatenate(
        [pairs[side : side + 1, 512 * k : 512 * k + 512] for side in (0, 1) for k in range(NZ)],
        axis=0,
    ).astype(BF16)
    place = iota((512, 512), 1)
    origin = (place % 256) // 8 * 16 + place // 256 * 8 + place % 8
    terms[...] = dot_nn(stacked, chosen(iota((512, 512), 0) == origin)).astype(jnp.int32)
    index = iota((MODES, OWN), 0)

    def make_hot(c):
        for k in range(NZ):
            from_lane = slice(OWN * c, OWN * c + OWN)
            span = slice(HALF * c + OWN * k, HALF * c + OWN * k + OWN)
            hot_a[:, span] = chosen(index == terms[k : k + 1, from_lane])
            hot_b[:, span] = chosen(index == terms[NZ + k : NZ + k + 1, from_lane])

    pass_on((2, 6))
    make_hot(0)
    pass_on((3, 5, 4))
    make_hot(1)

    def build(begin, end):
        for k in range(TERMS // CHUNK):
            span = slice(k * CHUNK, (k + 1) * CHUNK)
            c, first_z = k * CHUNK // HALF, k * CHUNK % HALF // OWN
            constant = jnp.concatenate(
                [
                    terms[NZ + j : NZ + j + 1, OWN * c : OWN * c + OWN]
                    for j in range(first_z, first_z + CHUNK // OWN)
                ],
                axis=1,
            )
            constant = (constant == MODES).astype(F32)
            first = dot_nn(rows[begin:end, :], hot_a[:, span])
            second = dot_nn(rows[begin:end, :], hot_b[:, span]) + constant
            library[begin:end, span] = (first * second).astype(BF16)

    square[...] = jnp.zeros_like(square)
    line, lane = iota((LOCAL, LOCAL), 0), iota((LOCAL, LOCAL), 1)
    back = lax.rem(y - line % SLAB // ROWS + NY, NY)
    band = jnp.where(back <= 4, 2 * back - 1, 16 - 2 * back)
    band = jnp.where(back == 0, 0, band)
    reorder[...] = chosen(band * BAND + line // SLAB * ROWS + line % ROWS == lane)
    line, lane = iota((LOCAL, OWN), 0), iota((LOCAL, OWN), 1)
    from_x = lax.rem(x - line // 128 + NX, NX)
    pick_mask[...] = chosen(
        (from_x * NY + line % 128 // 16 == lane // 8)
        & (line % 16 // 8 == y // 4)
        & (line % 8 == lane % 8)
    )

    drain(rows.at[pl.ds(0, EARLY // NX * (NX - 1))], recv_sem.at[BANDS])
    build(0, EARLY)
    drain(rows.at[pl.ds(0, (LOCAL - EARLY) // NX * (NX - 1))], recv_sem.at[BANDS + 1])
    build(EARLY, LOCAL)

    drain(compact_in.at[pl.ds(0, (PLANE - 1) * ROWS)], recv_sem.at[COMPACT])
    slabs = []
    for k in range(NX):
        total = compact_in[k * SLAB : k * SLAB + ROWS, :]
        for j in range(1, NY):
            total = total + compact_in[k * SLAB + j * ROWS : k * SLAB + (j + 1) * ROWS, :]
        slabs.append(total)
    given = jnp.concatenate(slabs, axis=1)
    wanted = dot_nn(given, reorder[...]).astype(BF16)

    own_half = pl.ds(pl.multiple_of(core * HALF, HALF), HALF)
    their_half = pl.ds(pl.multiple_of((1 - core) * HALF, HALF), HALF)
    own_terms = pl.ds(pl.multiple_of(core * HALF + z * OWN, OWN), OWN)
    own_slice = pl.ds(pl.multiple_of(z * OWN, OWN), OWN)

    def squares(vector):
        return jnp.sum(vector * vector, axis=1, keepdims=True)

    diagonal = iota((GROUP, 128), 0) == iota((GROUP, 128), 1)

    def to_row(column):
        return jnp.sum(jnp.where(diagonal, column, 0.0), axis=0, keepdims=True)

    def to_column(row):
        return jnp.sum(jnp.where(diagonal, row, 0.0), axis=1, keepdims=True)

    def scatter_sums(lhs, finish, out, mine, pair, pre, got, at, image=None, curve=None, curves=None):
        if image is not None:
            curve[0] = to_row(squares(image))
            send(curve.at[0], curve.at[1], CURVE + at - 1, sibling)
        out[...] = finish(dot_nn(lhs, library[:, their_half]))
        send(out, pair, PAIR + at, sibling)
        far = pl.ds(pl.multiple_of(opposite * OWN, OWN), OWN)
        send(out.at[:, far], got.at[NZ - 1], SUMS + at, across)
        mine[...] = finish(dot_nn(lhs, library[:, own_half]))
        send(mine.at[:, far], got.at[NZ // 2 - 1], SUMS + at, at_line(NZ // 2)[1])
        if image is not None:
            drain(curve.at[1], recv_sem.at[CURVE + at - 1])
            curve[2] = curve[0] + curve[1]
        drain(pair, recv_sem.at[PAIR + at])
        pre[...] = mine[...] + pair[...]
        for step in FAR_FIRST:
            other, device = at_line(step)
            theirs = pl.ds(pl.multiple_of(other * OWN, OWN), OWN)
            if step != NZ // 2:
                send(pre.at[:, theirs], got.at[step - 1], SUMS + at, device)
            if image is not None:
                send(curve.at[2], curves.at[step - 1], CURVES + at - 1, device)

    def sum_up(pre, got, at):
        drain(got, recv_sem.at[SUMS + at])
        total = pre[:, own_slice]
        for step in range(NZ):
            total = total + got[step]
        return total * mask * (1.0 / SNAPS)

    def curvature(curve, curves, at):
        drain(curves, recv_sem.at[CURVES + at - 1])
        total = curve[2]
        for step in range(1, NZ):
            total = total + curves[step - 1]
        return to_column(total) * (1.0 / SNAPS)

    def gather_terms(value, full, at):
        arrived = ARRIVED + RING * at

        def slice_of(side, step):
            begin = side * HALF + lax.rem(z - step + NZ, NZ) * OWN
            return full.at[:, pl.ds(pl.multiple_of(begin, OWN), OWN)]

        def forward(step):
            send(slice_of(core, step), slice_of(core, step), HALVES + at, sibling, arrived + NZ + step)

        def wait(side, steps):
            for step in steps:
                slot = arrived + step if side == 0 else arrived + NZ + step
                drain(full.at[:, pl.ds(0, OWN)], recv_sem.at[slot])
                if side == 0 and step != NZ // 2:
                    forward(step)

        def product(side, steps):
            total = None
            for step in steps:
                which = core if side == 0 else 1 - core
                begin = which * HALF + lax.rem(z - step + NZ, NZ) * OWN
                span = pl.ds(pl.multiple_of(begin, OWN), OWN)
                term = dot_nt(split(full[:, span]), library[:, span])
                total = term if total is None else total + term
            return total

        full[:, own_terms] = value
        for step in FAR_FIRST:
            send(
                slice_of(core, 0), slice_of(core, 0), SLICES + at, at_line(step)[1], arrived + step
            )
            if step == NZ // 2:
                send(slice_of(core, 0), slice_of(core, 0), SLICES + at, across, arrived + NZ + step)
        forward(0)
        wait(0, (1, 7))
        image = product(0, (0, 1, 7))
        wait(0, (2, 6))
        wait(1, (0,))
        image = image + product(0, (2, 6)) + product(1, (0,))
        wait(0, (3, 5))
        wait(1, (1, 7))
        image = image + product(0, (3, 5)) + product(1, (1, 7))
        wait(1, (2, 6))
        image = image + product(1, (2, 6))
        wait(0, (4,))
        wait(1, (4, 3, 5))
        return merge(image + product(0, (4,)) + product(1, (4, 3, 5)))

    scatter_sums(wanted, lambda value: value[:GROUP], out0, mine0, pair0, pre0, got0, 0)
    mask = dot_nn(given, pick_mask[...])[GROUP:]
    direction = sum_up(pre0, got0, 0)
    image = gather_terms(direction, full0, 0)
    scatter_sums(split(image), merge, out1, mine1, pair1, pre1, got1, 1, image, curve1, curves1)
    energy = squares(full0[...])
    step_len = energy / curvature(curve1, curves1, 1)
    coeffs = step_len * direction
    resid = direction - step_len * sum_up(pre1, got1, 1)
    next_image = gather_terms(resid, full1, 1)
    fresh = squares(full1[...])
    ratio = fresh / energy
    direction = resid + ratio * direction
    image = next_image + ratio * image
    scatter_sums(split(image), merge, out2, mine2, pair2, pre2, got2, 2, image, curve2, curves2)
    step_len = fresh / curvature(curve2, curves2, 2)
    coeffs = coeffs + step_len * direction
    resid = resid - step_len * sum_up(pre2, got2, 2)

    group = NX * y + x
    at = group % (PLANE // 2) * GROUP
    square[pl.ds(pl.multiple_of(at, GROUP), GROUP), :] = coeffs
    square[pl.ds(pl.multiple_of(lax.rem(at + 64, 128), GROUP), GROUP), :] = resid
    turn[...] = square[...].T
    here = pl.ds(pl.multiple_of((x * NY + y) * 8, 8), 8)
    for a, b in far_first:
        spot = lax.rem(x + a, NX) * NY + lax.rem(y + b, NY)
        theirs = pl.ds(pl.multiple_of(spot * 8, 8), 8)
        send(turn.at[theirs], turned.at[here], TURN, at_plane(a, b))
    turned[here, :] = turn[here, :]
    drain(rows.at[pl.ds(0, (NY - 1) * ROWS)], send_sem.at[0])
    drain(rows.at[pl.ds(0, EARLY // NX * (NX - 1))], send_sem.at[BANDS])
    drain(rows.at[pl.ds(0, (LOCAL - EARLY) // NX * (NX - 1))], send_sem.at[BANDS + 1])
    drain(compact_in.at[pl.ds(0, (PLANE - 1) * ROWS)], send_sem.at[COMPACT])
    for k, (pair, got) in enumerate(((pair0, got0), (pair1, got1), (pair2, got2))):
        drain(pair, send_sem.at[PAIR + k])
        drain(got, send_sem.at[SUMS + k])
    for k, full in enumerate((full0, full1)):
        drain(full.at[:, pl.ds(0, HALF)], send_sem.at[SLICES + k])
        drain(full.at[:, pl.ds(0, HALF - OWN)], send_sem.at[HALVES + k])
    for k, (curve, curves) in enumerate(((curve1, curves1), (curve2, curves2))):
        drain(curve.at[1], send_sem.at[CURVE + k])
        drain(curves, send_sem.at[CURVES + k])
    drain(turned.at[pl.ds(0, OWN - 8)], recv_sem.at[TURN])
    lane = iota((8, 128), 1) // GROUP
    for side in range(2):
        left = jnp.zeros((8, 128), F32)
        right = left
        for a in range(NX):
            for b in range(4 * side, 4 * side + 4):
                block = turned[8 * (a * NY + b) : 8 * (a * NY + b) + 8, :]
                at = (NX * b + a) % (PLANE // 2)
                left = jnp.where(lane == at, block, left)
                right = jnp.where(lane == (at + 8) % 16, block, right)
        out_ref[0:8, 128 * side : 128 * side + 128] = left
        out_ref[8:16, 128 * side : 128 * side + 128] = pltpu.roll(right, 64, 1)

    drain(turned.at[pl.ds(0, OWN - 8)], send_sem.at[TURN])


def body(modes, targets, pairs, support):
    vmem = pl.BlockSpec(memory_space=pltpu.VMEM)
    hbm = pl.BlockSpec(memory_space=pltpu.HBM)
    both = pl.pallas_call(
        kernel,
        out_shape=jax.ShapeDtypeStruct((16, TARGETS), F32),
        in_specs=[hbm] * 4,
        out_specs=vmem,
        scratch_shapes=[
            pltpu.VMEM((ROWS, TARGETS), BF16),
            pltpu.VMEM((2, TERMS), jnp.int32),
            pltpu.VMEM((8, TARGETS), jnp.int32),
            pltpu.VMEM((LOCAL, MODES), BF16),
            pltpu.VMEM((SLAB, TARGETS + 128), BF16),
            pltpu.VMEM((PLANE * ROWS, 128), BF16),
            pltpu.VMEM((PLANE * ROWS, 128), BF16),
            pltpu.VMEM((LOCAL, LOCAL), BF16),
            pltpu.VMEM((LOCAL, OWN), BF16),
            pltpu.VMEM((MODES, TERMS), BF16),
            pltpu.VMEM((MODES, TERMS), BF16),
            pltpu.VMEM((2 * NZ, 512), jnp.int32),
            pltpu.VMEM((LOCAL, TERMS), BF16),
        ]
        + [pltpu.VMEM((GROUP, HALF), F32)] * 12
        + [pltpu.VMEM((NZ, GROUP, OWN), F32)] * 3
        + [pltpu.VMEM((GROUP, TERMS), F32)] * 2
        + [
            pltpu.VMEM((3, 1, 128), F32),
            pltpu.VMEM((3, 1, 128), F32),
            pltpu.VMEM((NZ - 1, 1, 128), F32),
            pltpu.VMEM((NZ - 1, 1, 128), F32),
            pltpu.VMEM((OWN, 128), F32),
            pltpu.VMEM((128, OWN), F32),
            pltpu.VMEM((OWN, 128), F32),
            pltpu.SemaphoreType.DMA((4,)),
            pltpu.SemaphoreType.DMA((ARRIVED,)),
            pltpu.SemaphoreType.DMA((STAGES,)),
        ],
        compiler_params=pltpu.CompilerParams(
            collective_id=0, has_side_effects=True, vmem_limit_bytes=48 * 2**20
        ),
        name="regression",
    )(*(pltpu.with_memory_space_constraint(v, pltpu.HBM) for v in (modes, targets, pairs.T, support)))
    return both[:8], both[8:]


def solution(mesh):
    rows = P(("snap", "tile"), None)
    return jax.shard_map(
        body,
        mesh=mesh,
        in_specs=(rows, rows, P(), rows),
        out_specs=(rows, rows),
        check_vma=False,
    )
```

```python
import jax
import jax.numpy as jnp
from jax import lax
from jax.experimental import pallas as pl
from jax.experimental.pallas import tpu as pltpu
from jax.sharding import PartitionSpec as P

NX, NY, NZ, NC = 4, 8, 8, 2
RING = NZ * NC
PLANE = NX * NY
MODES = 256
TARGETS = 256
TERMS = 4096
ROWS = 16
SNAPS = 8192
SLAB = NY * ROWS
BAND = NX * ROWS
BATCHES = (0, 3, 5, 7, 8)
LOCAL = PLANE * ROWS
OWN = TERMS // RING
HALF = TERMS // NC
GROUP = TARGETS // PLANE
CHUNK = 1024
FAR_FIRST = (4, 3, 5, 2, 6, 1, 7)
NEAR_FIRST = (1, 7, 2, 6, 3, 5, 4)
DIRECT = (4, 3, 5)
BAND_OF = (0, 1, 3, 5, 7, 6, 4, 2)
F32 = jnp.float32
BF16 = jnp.bfloat16
MESH = pl.DeviceIdType.MESH

BANDS, COMPACT, PAIR, SUMS, SLICES, HALVES, CURVE, CURVES, TURN = 7, 11, 12, 15, 18, 20, 22, 24, 26
ARRIVED = 27
STAGES = ARRIVED + 2 * RING


def split(value):
    high = value.astype(BF16)
    low = (value - high.astype(F32)).astype(BF16)
    return jnp.concatenate([high, low], axis=0)


def merge(value):
    return value[:GROUP] + value[GROUP:]


def dot_nt(lhs, rhs):
    return lax.dot_general(lhs, rhs, (((1,), (1,)), ((), ())), preferred_element_type=F32)


def dot_nn(lhs, rhs):
    return jnp.dot(lhs, rhs, preferred_element_type=F32)


def iota(shape, dim):
    return lax.broadcasted_iota(jnp.int32, shape, dim)


def chosen(condition):
    return condition.astype(F32).astype(BF16)


def drain(ref, sem):
    pltpu.make_async_copy(ref, ref, sem).wait()


def kernel(
    modes_ref, targets_ref, pairs_ref, support_ref, out_ref,
    targets_in, pairs_in, support_in, rows, extra, compact, compact_in, reorder, pick_mask,
    hot_a, hot_b, terms, library,
    out0, out1, out2, mine0, mine1, mine2, pair0, pair1, pair2, pre0, pre1, pre2, got0, got1, got2,
    full0, full1, curve1, curve2, curves1, curves2, turn, square, turned,
    load_sem, send_sem, recv_sem,
):
    z = lax.axis_index("snap")
    tile = lax.axis_index("tile")
    x = tile // (NY * NC)
    y = (tile // NC) % NY
    core = tile % NC

    def at_plane(step_x, step_y):
        return z, (lax.rem(x + step_x, NX) * NY + lax.rem(y + step_y, NY)) * NC + core

    def at_line(step):
        other = lax.rem(z + step, NZ)
        return other, (other, tile)

    sibling = (z, tile + 1 - 2 * core)

    def across(step):
        return lax.rem(z + step, NZ), tile + 1 - 2 * core


    own_block = pl.ds(pl.multiple_of(y * ROWS, ROWS), ROWS)
    loads = [
        pltpu.make_async_copy(modes_ref, rows.at[pl.ds(0, ROWS)], load_sem.at[0]),
        pltpu.make_async_copy(targets_ref, targets_in, load_sem.at[1]),
        pltpu.make_async_copy(support_ref, support_in, load_sem.at[2]),
        pltpu.make_async_copy(pairs_ref, pairs_in, load_sem.at[3]),
    ]
    for load in loads:
        load.start()

    barrier = pltpu.get_barrier_semaphore()
    peers = [(a, b) for a in range(NX) for b in range(NY) if a or b]
    for a, b in peers:
        pl.semaphore_signal(barrier, inc=1, device_id=at_plane(a, b), device_id_type=MESH)
    for step in range(1, NZ):
        pl.semaphore_signal(barrier, inc=1, device_id=at_line(step)[1], device_id_type=MESH)
    pl.semaphore_signal(barrier, inc=1, device_id=sibling, device_id_type=MESH)
    for step in DIRECT:
        pl.semaphore_signal(barrier, inc=1, device_id=across(step), device_id_type=MESH)

    def send(src, dst, stage, device, arrive=None):
        pltpu.make_async_remote_copy(
            src_ref=src, dst_ref=dst, send_sem=send_sem.at[stage],
            recv_sem=recv_sem.at[stage if arrive is None else arrive],
            device_id=device, device_id_type=MESH,
        ).start()

    def block(step_y, step_x):
        return rows.at[pl.ds(BAND_OF[step_y] * BAND + step_x * ROWS, ROWS)]

    extra[...] = jnp.zeros_like(extra)
    for load in loads[:3]:
        load.wait()
    extra[own_block, 0:TARGETS] = targets_in[...]
    active = support_in[...].astype(F32)
    extra[own_block, TARGETS:] = jnp.concatenate(
        [active[:, :128], active[:, 128:]], axis=0
    ).astype(BF16)
    pl.semaphore_wait(barrier, len(peers) + NZ - 1 + 1 + len(DIRECT))

    for step in FAR_FIRST:
        send(modes_ref, block(step, 0), 0, at_plane(0, step), step - 1)

    def forward(step_y):
        for step in (2, 1, 3):
            stage = BANDS + sum(BAND_OF[step_y] >= end for end in BATCHES[1:-1])
            send(block(step_y, 0), block(step_y, step), stage, at_plane(step, 0))

    def pass_on(steps):
        for step in steps:
            drain(rows.at[pl.ds(0, ROWS)], recv_sem.at[step - 1])
            forward(step)

    forward(0)

    line = iota((PLANE * ROWS, TARGETS), 0)
    ring = line // ROWS % NY * NX + line // (ROWS * NY)
    pick_targets = chosen(
        (iota((PLANE * ROWS, TARGETS), 1) == ring * GROUP + line % ROWS) & (line % ROWS < GROUP)
    )
    line = iota((PLANE * ROWS, 128), 0)
    ring = (line // ROWS % NY * NX + line // (ROWS * NY)) % (PLANE // 2)
    pick_flags = chosen(
        (iota((PLANE * ROWS, 128), 1) == ring * GROUP + line % ROWS - GROUP) & (line % ROWS >= GROUP)
    )
    compact[...] = (
        dot_nt(pick_targets, extra[:, 0:TARGETS]) + dot_nt(pick_flags, extra[:, TARGETS:])
    ).astype(BF16)
    far_first = sorted(peers, key=lambda peer: -min(peer[0], NX - peer[0]) - min(peer[1], NY - peer[1]))

    def give(some):
        for a, b in some:
            spot = lax.rem(x + a, NX) * NY + lax.rem(y + b, NY)
            send(
                compact.at[pl.ds(pl.multiple_of(spot * ROWS, ROWS), ROWS)],
                compact_in.at[pl.ds(pl.multiple_of((a * NY + y) * ROWS, ROWS), ROWS)],
                COMPACT, at_plane(a, b),
            )

    compact_in[own_block, :] = compact[
        pl.ds(pl.multiple_of((x * NY + y) * ROWS, ROWS), ROWS), :
    ]

    loads[3].wait()
    give(far_first[:8])
    pairs = pairs_in[...].astype(F32)
    stacked = jnp.concatenate(
        [pairs[side : side + 1, 512 * k : 512 * k + 512] for side in (0, 1) for k in range(NZ)],
        axis=0,
    ).astype(BF16)
    place = iota((512, 512), 1)
    origin = (place % 256) // 8 * 16 + place // 256 * 8 + place % 8
    terms[...] = dot_nn(stacked, chosen(iota((512, 512), 0) == origin)).astype(jnp.int32)
    index = iota((MODES, OWN), 0)

    def make_hot(c):
        for k in range(NZ):
            from_lane = slice(OWN * c, OWN * c + OWN)
            span = slice(HALF * c + OWN * k, HALF * c + OWN * k + OWN)
            hot_a[:, span] = chosen(index == terms[k : k + 1, from_lane])
            hot_b[:, span] = chosen(index == terms[NZ + k : NZ + k + 1, from_lane])

    pass_on((1, 7))
    give(far_first[8:14])
    pass_on((2, 6))
    give(far_first[14:20])
    pass_on((3, 5))
    give(far_first[20:])
    pass_on((4,))
    make_hot(0)
    make_hot(1)

    def build(begin, end):
        for k in range(TERMS // CHUNK):
            span = slice(k * CHUNK, (k + 1) * CHUNK)
            c, first_z = k * CHUNK // HALF, k * CHUNK % HALF // OWN
            constant = jnp.concatenate(
                [
                    terms[NZ + j : NZ + j + 1, OWN * c : OWN * c + OWN]
                    for j in range(first_z, first_z + CHUNK // OWN)
                ],
                axis=1,
            )
            constant = (constant == MODES).astype(F32)
            first = dot_nn(rows[begin:end, :], hot_a[:, span])
            second = dot_nn(rows[begin:end, :], hot_b[:, span]) + constant
            library[begin:end, span] = (first * second).astype(BF16)

    square[...] = jnp.zeros_like(square)
    line, lane = iota((LOCAL, LOCAL), 0), iota((LOCAL, LOCAL), 1)
    back = lax.rem(y - line % SLAB // ROWS + NY, NY)
    band = jnp.where(back <= 4, 2 * back - 1, 16 - 2 * back)
    band = jnp.where(back == 0, 0, band)
    reorder[...] = chosen(band * BAND + line // SLAB * ROWS + line % ROWS == lane)
    line, lane = iota((LOCAL, OWN), 0), iota((LOCAL, OWN), 1)
    from_x = lax.rem(x - line // 128 + NX, NX)
    pick_mask[...] = chosen(
        (from_x * NY + line % 128 // 16 == lane // 8)
        & (line % 16 // 8 == y // 4)
        & (line % 8 == lane % 8)
    )

    for k in range(len(BATCHES) - 1):
        begin, end = BATCHES[k : k + 2]
        drain(rows.at[pl.ds(0, (end - begin) * ROWS * (NX - 1))], recv_sem.at[BANDS + k])
        build(begin * BAND, end * BAND)

    drain(compact_in.at[pl.ds(0, (PLANE - 1) * ROWS)], recv_sem.at[COMPACT])
    slabs = []
    for k in range(NX):
        total = compact_in[k * SLAB : k * SLAB + ROWS, :]
        for j in range(1, NY):
            total = total + compact_in[k * SLAB + j * ROWS : k * SLAB + (j + 1) * ROWS, :]
        slabs.append(total)
    given = jnp.concatenate(slabs, axis=1)
    wanted = dot_nn(given, reorder[...]).astype(BF16)

    own_half = pl.ds(pl.multiple_of(core * HALF, HALF), HALF)
    their_half = pl.ds(pl.multiple_of((1 - core) * HALF, HALF), HALF)
    own_terms = pl.ds(pl.multiple_of(core * HALF + z * OWN, OWN), OWN)
    own_slice = pl.ds(pl.multiple_of(z * OWN, OWN), OWN)

    def squares(vector):
        return jnp.sum(vector * vector, axis=1, keepdims=True)

    diagonal = iota((GROUP, 128), 0) == iota((GROUP, 128), 1)

    def to_row(column):
        return jnp.sum(jnp.where(diagonal, column, 0.0), axis=0, keepdims=True)

    def to_column(row):
        return jnp.sum(jnp.where(diagonal, row, 0.0), axis=1, keepdims=True)

    def scatter_sums(lhs, finish, out, mine, pair, pre, got, at, image=None, curve=None, curves=None):
        if image is not None:
            curve[0] = to_row(squares(image))
            send(curve.at[0], curve.at[1], CURVE + at - 1, sibling)
        out[...] = finish(dot_nn(lhs, library[:, their_half]))
        send(out, pair, PAIR + at, sibling)
        for k, step in enumerate(DIRECT):
            far = pl.ds(pl.multiple_of(at_line(step)[0] * OWN, OWN), OWN)
            send(out.at[:, far], got.at[NZ - 1 + k], SUMS + at, across(step))
        mine[...] = finish(dot_nn(lhs, library[:, own_half]))
        for step in DIRECT:
            other, device = at_line(step)
            far = pl.ds(pl.multiple_of(other * OWN, OWN), OWN)
            send(mine.at[:, far], got.at[step - 1], SUMS + at, device)
        if image is not None:
            drain(curve.at[1], recv_sem.at[CURVE + at - 1])
            curve[2] = curve[0] + curve[1]
        drain(pair, recv_sem.at[PAIR + at])
        pre[...] = mine[...] + pair[...]
        for step in FAR_FIRST:
            other, device = at_line(step)
            theirs = pl.ds(pl.multiple_of(other * OWN, OWN), OWN)
            if step not in DIRECT:
                send(pre.at[:, theirs], got.at[step - 1], SUMS + at, device)
            if image is not None:
                send(curve.at[2], curves.at[step - 1], CURVES + at - 1, device)

    def sum_up(pre, got, at):
        drain(got, recv_sem.at[SUMS + at])
        total = pre[:, own_slice]
        for step in range(NZ - 1 + len(DIRECT)):
            total = total + got[step]
        return total * mask * (1.0 / SNAPS)

    def curvature(curve, curves, at):
        drain(curves, recv_sem.at[CURVES + at - 1])
        total = curve[2]
        for step in range(1, NZ):
            total = total + curves[step - 1]
        return to_column(total) * (1.0 / SNAPS)

    def gather_terms(value, full, at):
        arrived = ARRIVED + RING * at

        def slice_of(side, step):
            begin = side * HALF + lax.rem(z - step + NZ, NZ) * OWN
            return full.at[:, pl.ds(pl.multiple_of(begin, OWN), OWN)]

        def forward(step):
            send(slice_of(core, step), slice_of(core, step), HALVES + at, sibling, arrived + NZ + step)

        def wait(side, steps):
            for step in steps:
                slot = arrived + step if side == 0 else arrived + NZ + step
                drain(full.at[:, pl.ds(0, OWN)], recv_sem.at[slot])
                if side == 0 and step not in DIRECT:
                    forward(step)

        def product(side, steps):
            total = None
            for step in steps:
                which = core if side == 0 else 1 - core
                begin = which * HALF + lax.rem(z - step + NZ, NZ) * OWN
                span = pl.ds(pl.multiple_of(begin, OWN), OWN)
                term = dot_nt(split(full[:, span]), library[:, span])
                total = term if total is None else total + term
            return total

        full[:, own_terms] = value
        for step in FAR_FIRST:
            send(
                slice_of(core, 0), slice_of(core, 0), SLICES + at, at_line(step)[1], arrived + step
            )
            if step in DIRECT:
                send(
                    slice_of(core, 0), slice_of(core, 0), SLICES + at, across(step), arrived + NZ + step
                )
        forward(0)
        image = product(0, (0,))
        wait(1, (0,))
        image = image + product(1, (0,))
        wait(0, (1, 7))
        wait(0, (2, 6))
        image = image + product(0, (1, 7, 2, 6))
        wait(0, (3, 5))
        wait(1, (3, 5))
        image = image + product(0, (3, 5)) + product(1, (3, 5))
        wait(1, (1, 7, 2, 6))
        image = image + product(1, (1, 7, 2, 6))
        wait(0, (4,))
        wait(1, (4,))
        return merge(image + product(0, (4,)) + product(1, (4,)))

    scatter_sums(wanted, lambda value: value[:GROUP], out0, mine0, pair0, pre0, got0, 0)
    mask = dot_nn(given, pick_mask[...])[GROUP:]
    direction = sum_up(pre0, got0, 0)
    image = gather_terms(direction, full0, 0)
    scatter_sums(split(image), merge, out1, mine1, pair1, pre1, got1, 1, image, curve1, curves1)
    energy = squares(full0[...])
    step_len = energy / curvature(curve1, curves1, 1)
    coeffs = step_len * direction
    resid = direction - step_len * sum_up(pre1, got1, 1)
    next_image = gather_terms(resid, full1, 1)
    fresh = squares(full1[...])
    ratio = fresh / energy
    direction = resid + ratio * direction
    image = next_image + ratio * image
    scatter_sums(split(image), merge, out2, mine2, pair2, pre2, got2, 2, image, curve2, curves2)
    step_len = fresh / curvature(curve2, curves2, 2)
    coeffs = coeffs + step_len * direction
    resid = resid - step_len * sum_up(pre2, got2, 2)

    group = NX * y + x
    at = group % (PLANE // 2) * GROUP
    square[pl.ds(pl.multiple_of(at, GROUP), GROUP), :] = coeffs
    square[pl.ds(pl.multiple_of(lax.rem(at + 64, 128), GROUP), GROUP), :] = resid
    turn[...] = square[...].T
    here = pl.ds(pl.multiple_of((x * NY + y) * 8, 8), 8)
    for a, b in far_first:
        spot = lax.rem(x + a, NX) * NY + lax.rem(y + b, NY)
        theirs = pl.ds(pl.multiple_of(spot * 8, 8), 8)
        send(turn.at[theirs], turned.at[here], TURN, at_plane(a, b))
    turned[here, :] = turn[here, :]
    drain(rows.at[pl.ds(0, (NY - 1) * ROWS)], send_sem.at[0])
    for k in range(len(BATCHES) - 1):
        some = (BATCHES[k + 1] - BATCHES[k]) * ROWS * (NX - 1)
        drain(rows.at[pl.ds(0, some)], send_sem.at[BANDS + k])
    drain(compact_in.at[pl.ds(0, (PLANE - 1) * ROWS)], send_sem.at[COMPACT])
    for k, (pair, got) in enumerate(((pair0, got0), (pair1, got1), (pair2, got2))):
        drain(pair, send_sem.at[PAIR + k])
        drain(got, send_sem.at[SUMS + k])
    for k, full in enumerate((full0, full1)):
        drain(full.at[:, pl.ds(0, (NZ - 1 + len(DIRECT)) * OWN)], send_sem.at[SLICES + k])
        drain(full.at[:, pl.ds(0, (NZ - len(DIRECT)) * OWN)], send_sem.at[HALVES + k])
    for k, (curve, curves) in enumerate(((curve1, curves1), (curve2, curves2))):
        drain(curve.at[1], send_sem.at[CURVE + k])
        drain(curves, send_sem.at[CURVES + k])
    drain(turned.at[pl.ds(0, OWN - 8)], recv_sem.at[TURN])
    lane = iota((8, 128), 1) // GROUP
    for side in range(2):
        left = jnp.zeros((8, 128), F32)
        right = left
        for a in range(NX):
            for b in range(4 * side, 4 * side + 4):
                block = turned[8 * (a * NY + b) : 8 * (a * NY + b) + 8, :]
                at = (NX * b + a) % (PLANE // 2)
                left = jnp.where(lane == at, block, left)
                right = jnp.where(lane == (at + 8) % 16, block, right)
        out_ref[0:8, 128 * side : 128 * side + 128] = left
        out_ref[8:16, 128 * side : 128 * side + 128] = pltpu.roll(right, 64, 1)

    drain(turned.at[pl.ds(0, OWN - 8)], send_sem.at[TURN])


def body(modes, targets, pairs, support):
    vmem = pl.BlockSpec(memory_space=pltpu.VMEM)
    hbm = pl.BlockSpec(memory_space=pltpu.HBM)
    both = pl.pallas_call(
        kernel,
        out_shape=jax.ShapeDtypeStruct((16, TARGETS), F32),
        in_specs=[hbm] * 4,
        out_specs=vmem,
        scratch_shapes=[
            pltpu.VMEM((ROWS, TARGETS), BF16),
            pltpu.VMEM((2, TERMS), jnp.int32),
            pltpu.VMEM((8, TARGETS), jnp.int32),
            pltpu.VMEM((LOCAL, MODES), BF16),
            pltpu.VMEM((SLAB, TARGETS + 128), BF16),
            pltpu.VMEM((PLANE * ROWS, 128), BF16),
            pltpu.VMEM((PLANE * ROWS, 128), BF16),
            pltpu.VMEM((LOCAL, LOCAL), BF16),
            pltpu.VMEM((LOCAL, OWN), BF16),
            pltpu.VMEM((MODES, TERMS), BF16),
            pltpu.VMEM((MODES, TERMS), BF16),
            pltpu.VMEM((2 * NZ, 512), jnp.int32),
            pltpu.VMEM((LOCAL, TERMS), BF16),
        ]
        + [pltpu.VMEM((GROUP, HALF), F32)] * 12
        + [pltpu.VMEM((NZ - 1 + len(DIRECT), GROUP, OWN), F32)] * 3
        + [pltpu.VMEM((GROUP, TERMS), F32)] * 2
        + [
            pltpu.VMEM((3, 1, 128), F32),
            pltpu.VMEM((3, 1, 128), F32),
            pltpu.VMEM((NZ - 1, 1, 128), F32),
            pltpu.VMEM((NZ - 1, 1, 128), F32),
            pltpu.VMEM((OWN, 128), F32),
            pltpu.VMEM((128, OWN), F32),
            pltpu.VMEM((OWN, 128), F32),
            pltpu.SemaphoreType.DMA((4,)),
            pltpu.SemaphoreType.DMA((ARRIVED,)),
            pltpu.SemaphoreType.DMA((STAGES,)),
        ],
        compiler_params=pltpu.CompilerParams(
            collective_id=0, has_side_effects=True, vmem_limit_bytes=48 * 2**20
        ),
        name="regression",
    )(*(pltpu.with_memory_space_constraint(v, pltpu.HBM) for v in (modes, targets, pairs.T, support)))
    return both[:8], both[8:]


def solution(mesh):
    rows = P(("snap", "tile"), None)
    return jax.shard_map(
        body,
        mesh=mesh,
        in_specs=(rows, rows, P(), rows),
        out_specs=(rows, rows),
        check_vma=False,
    )
```

```python
import jax
import jax.numpy as jnp
from jax import lax
from jax.experimental import pallas as pl
from jax.experimental.pallas import tpu as pltpu
from jax.sharding import PartitionSpec as P

NX, NY, NZ, NC = 4, 8, 8, 2
RING = NZ * NC
PLANE = NX * NY
MODES = 256
TARGETS = 256
TERMS = 4096
ROWS = 16
SNAPS = 8192
SLAB = NY * ROWS
LOCAL = PLANE * ROWS
OWN = TERMS // RING
HALF = TERMS // NC
GROUP = TARGETS // PLANE
CHUNK = 1024
FAR_FIRST = (4, 3, 5, 2, 6, 1, 7)
NEAR_FIRST = (1, 7, 2, 6, 3, 5, 4)
F32 = jnp.float32
BF16 = jnp.bfloat16
MESH = pl.DeviceIdType.MESH

EXTRA, SLABS, COMPACT, PAIR, SUMS, SLICES, HALVES, CURVE, CURVES, TURN = 7, 8, 11, 12, 15, 18, 20, 22, 24, 26
ARRIVED = 27
STAGES = ARRIVED + 2 * RING


def split(value):
    high = value.astype(BF16)
    low = (value - high.astype(F32)).astype(BF16)
    return jnp.concatenate([high, low], axis=0)


def merge(value):
    return value[:GROUP] + value[GROUP:]


def dot_nt(lhs, rhs):
    return lax.dot_general(lhs, rhs, (((1,), (1,)), ((), ())), preferred_element_type=F32)


def dot_nn(lhs, rhs):
    return jnp.dot(lhs, rhs, preferred_element_type=F32)


def iota(shape, dim):
    return lax.broadcasted_iota(jnp.int32, shape, dim)


def chosen(condition):
    return condition.astype(F32).astype(BF16)


def drain(ref, sem):
    pltpu.make_async_copy(ref, ref, sem).wait()


def kernel(
    modes_ref, targets_ref, pairs_ref, support_ref, out_ref,
    targets_in, pairs_in, support_in, rows, extra, compact, compact_in,
    hot_a, hot_b, terms, library,
    out0, out1, out2, mine0, mine1, mine2, pair0, pair1, pair2, pre0, pre1, pre2, got0, got1, got2,
    full0, full1, curve1, curve2, curves1, curves2, turn, square, turned, packed, unpacked, spread,
    load_sem, send_sem, recv_sem,
):
    z = lax.axis_index("snap")
    tile = lax.axis_index("tile")
    x = tile // (NY * NC)
    y = (tile // NC) % NY
    core = tile % NC

    def at_plane(step_x, step_y):
        return z, (lax.rem(x + step_x, NX) * NY + lax.rem(y + step_y, NY)) * NC + core

    def at_line(step):
        other = lax.rem(z + step, NZ)
        return other, (other, tile)

    sibling = (z, tile + 1 - 2 * core)
    opposite = lax.rem(z + NZ // 2, NZ)
    across = (opposite, tile + 1 - 2 * core)

    own_block = pl.ds(pl.multiple_of(y * ROWS, ROWS), ROWS)
    loads = [
        pltpu.make_async_copy(modes_ref, rows.at[own_block], load_sem.at[0]),
        pltpu.make_async_copy(targets_ref, targets_in, load_sem.at[1]),
        pltpu.make_async_copy(support_ref, support_in, load_sem.at[2]),
        pltpu.make_async_copy(pairs_ref, pairs_in, load_sem.at[3]),
    ]
    for load in loads:
        load.start()

    barrier = pltpu.get_barrier_semaphore()
    peers = [(a, b) for a in range(NX) for b in range(NY) if a or b]
    lines = [(a, b) for a, b in peers if not (a and b)]
    for a, b in lines:
        pl.semaphore_signal(barrier, inc=1, device_id=at_plane(a, b), device_id_type=MESH)
    for step in range(1, NZ):
        pl.semaphore_signal(barrier, inc=1, device_id=at_line(step)[1], device_id_type=MESH)
    pl.semaphore_signal(barrier, inc=1, device_id=sibling, device_id_type=MESH)
    pl.semaphore_signal(barrier, inc=1, device_id=across, device_id_type=MESH)

    def send(src, dst, stage, device, arrive=None):
        pltpu.make_async_remote_copy(
            src_ref=src, dst_ref=dst, send_sem=send_sem.at[stage],
            recv_sem=recv_sem.at[stage if arrive is None else arrive],
            device_id=device, device_id_type=MESH,
        ).start()

    for load in loads[:3]:
        load.wait()
    extra[own_block, 0:TARGETS] = targets_in[...]
    active = support_in[...].astype(F32)
    extra[own_block, TARGETS:] = jnp.concatenate(
        [active[:, :128], active[:, 128:]], axis=0
    ).astype(BF16)
    pl.semaphore_wait(barrier, len(lines) + NZ - 1 + 2)

    for step in FAR_FIRST:
        send(rows.at[own_block], rows.at[own_block], 0, at_plane(0, step), step - 1)

    def forward(block):
        source = pl.multiple_of(block * ROWS, ROWS)
        for step in (2, 1, 3):
            target = pl.multiple_of(step * SLAB + block * ROWS, ROWS)
            send(
                rows.at[pl.ds(source, ROWS)], rows.at[pl.ds(target, ROWS)], SLABS + step - 1,
                at_plane(step, 0),
            )

    forward(y)
    for step in FAR_FIRST:
        send(extra.at[own_block], extra.at[own_block], EXTRA, at_plane(0, step))

    loads[3].wait()
    pairs = pairs_in[...].astype(F32)
    stacked = jnp.concatenate(
        [pairs[side : side + 1, 512 * k : 512 * k + 512] for side in (0, 1) for k in range(NZ)],
        axis=0,
    ).astype(BF16)
    place = iota((512, 512), 1)
    origin = (place % 256) // 8 * 16 + place // 256 * 8 + place % 8
    terms[...] = dot_nn(stacked, chosen(iota((512, 512), 0) == origin)).astype(jnp.int32)
    index = iota((MODES, OWN), 0)

    def make_hot(c):
        for k in range(NZ):
            from_lane = slice(OWN * c, OWN * c + OWN)
            span = slice(HALF * c + OWN * k, HALF * c + OWN * k + OWN)
            hot_a[:, span] = chosen(index == terms[k : k + 1, from_lane])
            hot_b[:, span] = chosen(index == terms[NZ + k : NZ + k + 1, from_lane])

    make_hot(0)
    for step in NEAR_FIRST:
        drain(rows.at[pl.ds(0, ROWS)], recv_sem.at[step - 1])
        forward(lax.rem(y - step + NY, NY))

    drain(extra.at[pl.ds(0, (NY - 1) * ROWS)], recv_sem.at[EXTRA])
    line = iota((NX * ROWS, TARGETS), 0)
    wanted = (NX * y + line // ROWS) * GROUP + line % ROWS
    pick_targets = chosen((iota((NX * ROWS, TARGETS), 1) == wanted) & (line % ROWS < GROUP))
    line = iota((NX * ROWS, 128), 0)
    wanted = (NX * (y % 4) + line // ROWS) * GROUP + line % ROWS - GROUP
    pick_flags = chosen((iota((NX * ROWS, 128), 1) == wanted) & (line % ROWS >= GROUP))
    compact[...] = (
        dot_nt(pick_targets, extra[:, 0:TARGETS]) + dot_nt(pick_flags, extra[:, TARGETS:])
    ).astype(BF16)
    for step in (2, 1, 3):
        theirs = pl.ds(pl.multiple_of(lax.rem(x + step, NX) * ROWS, ROWS), ROWS)
        send(
            compact.at[theirs], compact_in.at[pl.ds(step * ROWS, ROWS)], COMPACT,
            at_plane(step, 0),
        )
    compact_in[0:ROWS, :] = compact[pl.ds(pl.multiple_of(x * ROWS, ROWS), ROWS), :]

    make_hot(1)

    def build(begin, end):
        for k in range(TERMS // CHUNK):
            span = slice(k * CHUNK, (k + 1) * CHUNK)
            c, first_z = k * CHUNK // HALF, k * CHUNK % HALF // OWN
            constant = jnp.concatenate(
                [
                    terms[NZ + j : NZ + j + 1, OWN * c : OWN * c + OWN]
                    for j in range(first_z, first_z + CHUNK // OWN)
                ],
                axis=1,
            )
            constant = (constant == MODES).astype(F32)
            first = dot_nn(rows[begin:end, :], hot_a[:, span])
            second = dot_nn(rows[begin:end, :], hot_b[:, span]) + constant
            library[begin:end, span] = (first * second).astype(BF16)

    build(0, SLAB)
    square[...] = jnp.zeros_like(square)
    quarter = iota((8, 128), 1) // PLANE
    line, lane = iota((TARGETS, TARGETS), 0), iota((TARGETS, TARGETS), 1)
    ring = line % PLANE % NY * NX + line % PLANE // NY
    spread[...] = chosen(ring * GROUP + line // PLANE == lane)
    for step in (1, 3, 2):
        drain(rows.at[pl.ds(0, SLAB)], recv_sem.at[SLABS + step - 1])
    build(SLAB, LOCAL)

    drain(compact_in.at[pl.ds(0, (NX - 1) * ROWS)], recv_sem.at[COMPACT])
    given = jnp.concatenate([compact_in[k * ROWS : (k + 1) * ROWS, :] for k in range(NX)], axis=1)
    own_half = pl.ds(pl.multiple_of(core * HALF, HALF), HALF)
    their_half = pl.ds(pl.multiple_of((1 - core) * HALF, HALF), HALF)
    own_terms = pl.ds(pl.multiple_of(core * HALF + z * OWN, OWN), OWN)
    own_slice = pl.ds(pl.multiple_of(z * OWN, OWN), OWN)

    def squares(vector):
        return jnp.sum(vector * vector, axis=1, keepdims=True)

    diagonal = iota((GROUP, 128), 0) == iota((GROUP, 128), 1)

    def to_row(column):
        return jnp.sum(jnp.where(diagonal, column, 0.0), axis=0, keepdims=True)

    def to_column(row):
        return jnp.sum(jnp.where(diagonal, row, 0.0), axis=1, keepdims=True)

    def scatter_sums(lhs, finish, out, mine, pair, pre, got, at, image=None, curve=None, curves=None):
        if image is not None:
            curve[0] = to_row(squares(image))
            send(curve.at[0], curve.at[1], CURVE + at - 1, sibling)
        out[...] = finish(dot_nn(lhs, library[:, their_half]))
        send(out, pair, PAIR + at, sibling)
        far = pl.ds(pl.multiple_of(opposite * OWN, OWN), OWN)
        send(out.at[:, far], got.at[NZ - 1], SUMS + at, across)
        mine[...] = finish(dot_nn(lhs, library[:, own_half]))
        send(mine.at[:, far], got.at[NZ // 2 - 1], SUMS + at, at_line(NZ // 2)[1])
        if image is not None:
            drain(curve.at[1], recv_sem.at[CURVE + at - 1])
            curve[2] = curve[0] + curve[1]
        drain(pair, recv_sem.at[PAIR + at])
        pre[...] = mine[...] + pair[...]
        for step in FAR_FIRST:
            other, device = at_line(step)
            theirs = pl.ds(pl.multiple_of(other * OWN, OWN), OWN)
            if step != NZ // 2:
                send(pre.at[:, theirs], got.at[step - 1], SUMS + at, device)
            if image is not None:
                send(curve.at[2], curves.at[step - 1], CURVES + at - 1, device)

    def sum_up(pre, got, at):
        drain(got, recv_sem.at[SUMS + at])
        total = pre[:, own_slice]
        for step in range(NZ):
            total = total + got[step]
        return total * mask * (1.0 / SNAPS)

    def curvature(curve, curves, at):
        drain(curves, recv_sem.at[CURVES + at - 1])
        total = curve[2]
        for step in range(1, NZ):
            total = total + curves[step - 1]
        return to_column(total) * (1.0 / SNAPS)

    def gather_terms(value, full, at):
        arrived = ARRIVED + RING * at

        def slice_of(side, step):
            begin = side * HALF + lax.rem(z - step + NZ, NZ) * OWN
            return full.at[:, pl.ds(pl.multiple_of(begin, OWN), OWN)]

        def forward(step):
            send(slice_of(core, step), slice_of(core, step), HALVES + at, sibling, arrived + NZ + step)

        def wait(side, steps):
            for step in steps:
                slot = arrived + step if side == 0 else arrived + NZ + step
                drain(full.at[:, pl.ds(0, OWN)], recv_sem.at[slot])
                if side == 0 and step != NZ // 2:
                    forward(step)

        def product(side, steps):
            total = None
            for step in steps:
                which = core if side == 0 else 1 - core
                begin = which * HALF + lax.rem(z - step + NZ, NZ) * OWN
                span = pl.ds(pl.multiple_of(begin, OWN), OWN)
                term = dot_nt(split(full[:, span]), library[:, span])
                total = term if total is None else total + term
            return total

        full[:, own_terms] = value
        for step in FAR_FIRST:
            send(
                slice_of(core, 0), slice_of(core, 0), SLICES + at, at_line(step)[1], arrived + step
            )
            if step == NZ // 2:
                send(slice_of(core, 0), slice_of(core, 0), SLICES + at, across, arrived + NZ + step)
        forward(0)
        wait(0, (1, 7))
        image = product(0, (0, 1, 7))
        wait(0, (2, 6))
        wait(1, (0,))
        image = image + product(0, (2, 6)) + product(1, (0,))
        wait(0, (3, 5))
        wait(1, (1, 7))
        image = image + product(0, (3, 5)) + product(1, (1, 7))
        wait(1, (2, 6))
        image = image + product(1, (2, 6))
        wait(0, (4,))
        wait(1, (4, 3, 5))
        return merge(image + product(0, (4,)) + product(1, (4, 3, 5)))

    scatter_sums(given, lambda value: value[:GROUP], out0, mine0, pair0, pre0, got0, 0)
    line, lane = iota((LOCAL, OWN), 0), iota((LOCAL, OWN), 1)
    from_x = lax.rem(x - line // 128 + NX, NX)
    pick = (
        (from_x * NY + line % 128 // 16 == lane // 8)
        & (line % 16 // 8 == y // 4)
        & (line % 8 == lane % 8)
    )
    mask = dot_nn(given, chosen(pick))[GROUP:]

    direction = sum_up(pre0, got0, 0)
    image = gather_terms(direction, full0, 0)
    scatter_sums(split(image), merge, out1, mine1, pair1, pre1, got1, 1, image, curve1, curves1)
    energy = squares(full0[...])
    step_len = energy / curvature(curve1, curves1, 1)
    coeffs = step_len * direction
    resid = direction - step_len * sum_up(pre1, got1, 1)
    next_image = gather_terms(resid, full1, 1)
    fresh = squares(full1[...])
    ratio = fresh / energy
    direction = resid + ratio * direction
    image = next_image + ratio * image
    scatter_sums(split(image), merge, out2, mine2, pair2, pre2, got2, 2, image, curve2, curves2)
    step_len = fresh / curvature(curve2, curves2, 2)
    coeffs = coeffs + step_len * direction
    resid = resid - step_len * sum_up(pre2, got2, 2)

    square[0:GROUP, :] = coeffs
    square[GROUP : 2 * GROUP, :] = resid
    turn[...] = square[...].T
    lane = iota((PLANE, 128), 1) // (2 * GROUP)
    total = turn[pl.ds(0, PLANE, stride=8), :]
    for k in range(1, 8):
        total = jnp.where(
            lane == k, pltpu.roll(turn[pl.ds(k, PLANE, stride=8), :], 2 * GROUP * k, 1), total
        )
    for k in range(PLANE):
        packed[k] = total[k : k + 1]
    here = x * NY + y
    far_first = sorted(peers, key=lambda peer: -min(peer[0], NX - peer[0]) - min(peer[1], NY - peer[1]))
    for a, b in far_first:
        spot = lax.rem(x + a, NX) * NY + lax.rem(y + b, NY)
        send(packed.at[spot], unpacked.at[here], TURN, at_plane(a, b))
    unpacked[here] = packed[here]
    drain(rows.at[pl.ds(0, (NY - 1) * ROWS)], send_sem.at[0])
    drain(extra.at[pl.ds(0, (NY - 1) * ROWS)], send_sem.at[EXTRA])
    for step in (1, 2, 3):
        drain(rows.at[pl.ds(0, SLAB)], send_sem.at[SLABS + step - 1])
    drain(compact_in.at[pl.ds(0, (NX - 1) * ROWS)], send_sem.at[COMPACT])
    for k, (pair, got) in enumerate(((pair0, got0), (pair1, got1), (pair2, got2))):
        drain(pair, send_sem.at[PAIR + k])
        drain(got, send_sem.at[SUMS + k])
    for k, full in enumerate((full0, full1)):
        drain(full.at[:, pl.ds(0, HALF)], send_sem.at[SLICES + k])
        drain(full.at[:, pl.ds(0, HALF - OWN)], send_sem.at[HALVES + k])
    for k, (curve, curves) in enumerate(((curve1, curves1), (curve2, curves2))):
        drain(curve.at[1], send_sem.at[CURVE + k])
        drain(curves, send_sem.at[CURVES + k])
    drain(unpacked.at[pl.ds(0, PLANE - 1)], recv_sem.at[TURN])
    received = jnp.concatenate(
        [unpacked[k] for k in range(PLANE)] + [jnp.zeros((128 - PLANE, 128), F32)], axis=0
    )
    turned[...] = received.T
    sides = []
    for out in range(2):
        for part in range(2):
            total = turned[pl.ds(out * GROUP + 4 * part, 8, stride=2 * GROUP), :]
            for k in range(1, 4):
                more = turned[pl.ds(out * GROUP + 4 * part + k, 8, stride=2 * GROUP), :]
                total = jnp.where(quarter == k, pltpu.roll(more, PLANE * k, 1), total)
            sides.append(total)
    both = jnp.concatenate(
        [jnp.concatenate(sides[0:2], axis=1), jnp.concatenate(sides[2:4], axis=1)], axis=0
    )
    high = both.astype(BF16)
    rest = both - high.astype(F32)
    middle = rest.astype(BF16)
    low = (rest - middle.astype(F32)).astype(BF16)
    moved = dot_nn(jnp.concatenate([high, middle, low], axis=0), spread[...])
    out_ref[...] = moved[0:16] + moved[16:32] + moved[32:48]

    drain(unpacked.at[pl.ds(0, PLANE - 1)], send_sem.at[TURN])


def body(modes, targets, pairs, support):
    vmem = pl.BlockSpec(memory_space=pltpu.VMEM)
    hbm = pl.BlockSpec(memory_space=pltpu.HBM)
    both = pl.pallas_call(
        kernel,
        out_shape=jax.ShapeDtypeStruct((16, TARGETS), F32),
        in_specs=[hbm] * 4,
        out_specs=vmem,
        scratch_shapes=[
            pltpu.VMEM((ROWS, TARGETS), BF16),
            pltpu.VMEM((2, TERMS), jnp.int32),
            pltpu.VMEM((8, TARGETS), jnp.int32),
            pltpu.VMEM((LOCAL, MODES), BF16),
            pltpu.VMEM((SLAB, TARGETS + 128), BF16),
            pltpu.VMEM((NX * ROWS, 128), BF16),
            pltpu.VMEM((NX * ROWS, 128), BF16),
            pltpu.VMEM((MODES, TERMS), BF16),
            pltpu.VMEM((MODES, TERMS), BF16),
            pltpu.VMEM((2 * NZ, 512), jnp.int32),
            pltpu.VMEM((LOCAL, TERMS), BF16),
        ]
        + [pltpu.VMEM((GROUP, HALF), F32)] * 12
        + [pltpu.VMEM((NZ, GROUP, OWN), F32)] * 3
        + [pltpu.VMEM((GROUP, TERMS), F32)] * 2
        + [
            pltpu.VMEM((3, 1, 128), F32),
            pltpu.VMEM((3, 1, 128), F32),
            pltpu.VMEM((NZ - 1, 1, 128), F32),
            pltpu.VMEM((NZ - 1, 1, 128), F32),
            pltpu.VMEM((OWN, 128), F32),
            pltpu.VMEM((128, OWN), F32),
            pltpu.VMEM((128, 128), F32),
            pltpu.VMEM((PLANE, 1, 128), F32),
            pltpu.VMEM((PLANE, 1, 128), F32),
            pltpu.VMEM((TARGETS, TARGETS), BF16),
            pltpu.SemaphoreType.DMA((4,)),
            pltpu.SemaphoreType.DMA((ARRIVED,)),
            pltpu.SemaphoreType.DMA((STAGES,)),
        ],
        compiler_params=pltpu.CompilerParams(
            collective_id=0, has_side_effects=True, vmem_limit_bytes=48 * 2**20
        ),
        name="regression",
    )(*(pltpu.with_memory_space_constraint(v, pltpu.HBM) for v in (modes, targets, pairs.T, support)))
    return both[:8], both[8:]


def solution(mesh):
    rows = P(("snap", "tile"), None)
    return jax.shard_map(
        body,
        mesh=mesh,
        in_specs=(rows, rows, P(), rows),
        out_specs=(rows, rows),
        check_vma=False,
    )
```

```python
import jax
import jax.numpy as jnp
from jax import lax
from jax.experimental import pallas as pl
from jax.experimental.pallas import tpu as pltpu
from jax.sharding import PartitionSpec as P

NX, NY, NZ, NC = 4, 8, 8, 2
RING = NZ * NC
PLANE = NX * NY
MODES = 256
TARGETS = 256
TERMS = 4096
ROWS = 16
SNAPS = 8192
SLAB = NY * ROWS
LOCAL = PLANE * ROWS
OWN = TERMS // RING
HALF = TERMS // NC
GROUP = TARGETS // PLANE
CHUNK = 2048
FAR_FIRST = (4, 3, 5, 2, 6, 1, 7)
NEAR_FIRST = (1, 7, 2, 6, 3, 5, 4)
F32 = jnp.float32
BF16 = jnp.bfloat16
MESH = pl.DeviceIdType.MESH

EXTRA, SLABS, COMPACT, PAIR, SUMS, SLICES, HALVES, CURVE, CURVES, TURN = 7, 8, 11, 12, 15, 18, 20, 22, 24, 26
ARRIVED = 27
STAGES = ARRIVED + 2 * RING


def split(value):
    high = value.astype(BF16)
    low = (value - high.astype(F32)).astype(BF16)
    return jnp.concatenate([high, low], axis=0)


def merge(value):
    return value[:GROUP] + value[GROUP:]


def dot_nt(lhs, rhs):
    return lax.dot_general(lhs, rhs, (((1,), (1,)), ((), ())), preferred_element_type=F32)


def dot_nn(lhs, rhs):
    return jnp.dot(lhs, rhs, preferred_element_type=F32)


def iota(shape, dim):
    return lax.broadcasted_iota(jnp.int32, shape, dim)


def chosen(condition):
    return condition.astype(F32).astype(BF16)


def drain(ref, sem):
    pltpu.make_async_copy(ref, ref, sem).wait()


def kernel(
    modes_ref, targets_ref, pairs_ref, support_ref, out_ref,
    targets_in, pairs_in, support_in, rows, leaving, extra, compact, compact_in,
    hot_a, hot_b, terms, library,
    out0, out1, out2, mine0, mine1, mine2, pair0, pair1, pair2, pre0, pre1, pre2, got0, got1, got2,
    full0, full1, curve1, curve2, curves1, curves2, turn, square, turned, packed, unpacked, spread,
    load_sem, send_sem, recv_sem,
):
    z = lax.axis_index("snap")
    tile = lax.axis_index("tile")
    x = tile // (NY * NC)
    y = (tile // NC) % NY
    core = tile % NC

    def at_plane(step_x, step_y):
        return z, (lax.rem(x + step_x, NX) * NY + lax.rem(y + step_y, NY)) * NC + core

    def at_line(step):
        other = lax.rem(z + step, NZ)
        return other, (other, tile)

    sibling = (z, tile + 1 - 2 * core)
    opposite = lax.rem(z + NZ // 2, NZ)
    across = (opposite, tile + 1 - 2 * core)

    own_block = pl.ds(pl.multiple_of(y * ROWS, ROWS), ROWS)
    loads = [
        pltpu.make_async_copy(modes_ref, rows.at[own_block], load_sem.at[0]),
        pltpu.make_async_copy(targets_ref, targets_in, load_sem.at[1]),
        pltpu.make_async_copy(support_ref, support_in, load_sem.at[2]),
        pltpu.make_async_copy(pairs_ref, pairs_in, load_sem.at[3]),
    ]
    for load in loads:
        load.start()

    barrier = pltpu.get_barrier_semaphore()
    peers = [(a, b) for a in range(NX) for b in range(NY) if a or b]
    lines = [(a, b) for a, b in peers if not (a and b)]
    for a, b in lines:
        pl.semaphore_signal(barrier, inc=1, device_id=at_plane(a, b), device_id_type=MESH)
    for step in range(1, NZ):
        pl.semaphore_signal(barrier, inc=1, device_id=at_line(step)[1], device_id_type=MESH)
    pl.semaphore_signal(barrier, inc=1, device_id=sibling, device_id_type=MESH)
    pl.semaphore_signal(barrier, inc=1, device_id=across, device_id_type=MESH)

    def send(src, dst, stage, device, arrive=None):
        pltpu.make_async_remote_copy(
            src_ref=src, dst_ref=dst, send_sem=send_sem.at[stage],
            recv_sem=recv_sem.at[stage if arrive is None else arrive],
            device_id=device, device_id_type=MESH,
        ).start()

    for load in loads[:3]:
        load.wait()
    given = targets_in[...].astype(F32)
    active = support_in[...].astype(F32)
    active = jnp.concatenate([active[:, :128], active[:, 128:]], axis=0)
    lane = iota((ROWS, 128), 1)
    for k in range(NY):
        left = given[:, k // 4 * 128 : k // 4 * 128 + 128]
        shift = 32 * (k % 4)
        left = pltpu.roll(left, 128 - shift, 1) if shift else left
        right = pltpu.roll(active, (160 - shift) % 128, 1) if shift != 32 else active
        both = jnp.where(lane < 32, left, jnp.where(lane < 64, right, 0.0))
        leaving[k * ROWS : (k + 1) * ROWS, :] = both.astype(BF16)
    extra[own_block, :] = leaving[own_block, :]
    pl.semaphore_wait(barrier, len(lines) + NZ - 1 + 2)

    for step in FAR_FIRST:
        send(rows.at[own_block], rows.at[own_block], 0, at_plane(0, step), step - 1)

    def forward(block):
        source = pl.multiple_of(block * ROWS, ROWS)
        for step in (2, 1, 3):
            target = pl.multiple_of(step * SLAB + block * ROWS, ROWS)
            send(
                rows.at[pl.ds(source, ROWS)], rows.at[pl.ds(target, ROWS)], SLABS + step - 1,
                at_plane(step, 0),
            )

    forward(y)
    for step in FAR_FIRST:
        theirs = pl.ds(pl.multiple_of(lax.rem(y + step, NY) * ROWS, ROWS), ROWS)
        send(leaving.at[theirs], extra.at[own_block], EXTRA, at_plane(0, step))

    loads[3].wait()
    pairs = pairs_in[...].astype(F32)
    stacked = jnp.concatenate(
        [pairs[side : side + 1, 512 * k : 512 * k + 512] for side in (0, 1) for k in range(NZ)],
        axis=0,
    ).astype(BF16)
    place = iota((512, 512), 1)
    origin = (place % 256) // 8 * 16 + place // 256 * 8 + place % 8
    terms[...] = dot_nn(stacked, chosen(iota((512, 512), 0) == origin)).astype(jnp.int32)
    index = iota((MODES, OWN), 0)

    def make_hot(c):
        for k in range(NZ):
            from_lane = slice(OWN * c, OWN * c + OWN)
            span = slice(HALF * c + OWN * k, HALF * c + OWN * k + OWN)
            hot_a[:, span] = chosen(index == terms[k : k + 1, from_lane])
            hot_b[:, span] = chosen(index == terms[NZ + k : NZ + k + 1, from_lane])

    make_hot(0)
    for step in NEAR_FIRST:
        drain(rows.at[pl.ds(0, ROWS)], recv_sem.at[step - 1])
        forward(lax.rem(y - step + NY, NY))

    drain(extra.at[pl.ds(0, (NY - 1) * ROWS)], recv_sem.at[EXTRA])
    line = iota((NX * ROWS, 128), 0)
    column = line // ROWS * GROUP + line % GROUP + jnp.where(line % ROWS < GROUP, 0, 32)
    compact[...] = dot_nt(chosen(iota((NX * ROWS, 128), 1) == column), extra[...]).astype(BF16)
    for step in (2, 1, 3):
        theirs = pl.ds(pl.multiple_of(lax.rem(x + step, NX) * ROWS, ROWS), ROWS)
        send(
            compact.at[theirs], compact_in.at[pl.ds(step * ROWS, ROWS)], COMPACT,
            at_plane(step, 0),
        )
    compact_in[0:ROWS, :] = compact[pl.ds(pl.multiple_of(x * ROWS, ROWS), ROWS), :]

    make_hot(1)

    def build(begin, end):
        for k in range(TERMS // CHUNK):
            span = slice(k * CHUNK, (k + 1) * CHUNK)
            c, first_z = k * CHUNK // HALF, k * CHUNK % HALF // OWN
            constant = jnp.concatenate(
                [
                    terms[NZ + j : NZ + j + 1, OWN * c : OWN * c + OWN]
                    for j in range(first_z, first_z + CHUNK // OWN)
                ],
                axis=1,
            )
            constant = (constant == MODES).astype(F32)
            first = dot_nn(rows[begin:end, :], hot_a[:, span])
            second = dot_nn(rows[begin:end, :], hot_b[:, span]) + constant
            library[begin:end, span] = (first * second).astype(BF16)

    build(0, SLAB)
    square[...] = jnp.zeros_like(square)
    quarter = iota((8, 128), 1) // PLANE
    line, lane = iota((TARGETS, TARGETS), 0), iota((TARGETS, TARGETS), 1)
    ring = line % PLANE % NY * NX + line % PLANE // NY
    spread[...] = chosen(ring * GROUP + line // PLANE == lane)
    for step in (1, 3, 2):
        drain(rows.at[pl.ds(0, SLAB)], recv_sem.at[SLABS + step - 1])
    build(SLAB, LOCAL)

    drain(compact_in.at[pl.ds(0, (NX - 1) * ROWS)], recv_sem.at[COMPACT])
    given = jnp.concatenate([compact_in[k * ROWS : (k + 1) * ROWS, :] for k in range(NX)], axis=1)
    own_half = pl.ds(pl.multiple_of(core * HALF, HALF), HALF)
    their_half = pl.ds(pl.multiple_of((1 - core) * HALF, HALF), HALF)
    own_terms = pl.ds(pl.multiple_of(core * HALF + z * OWN, OWN), OWN)
    own_slice = pl.ds(pl.multiple_of(z * OWN, OWN), OWN)

    def squares(vector):
        return jnp.sum(vector * vector, axis=1, keepdims=True)

    diagonal = iota((GROUP, 128), 0) == iota((GROUP, 128), 1)

    def to_row(column):
        return jnp.sum(jnp.where(diagonal, column, 0.0), axis=0, keepdims=True)

    def to_column(row):
        return jnp.sum(jnp.where(diagonal, row, 0.0), axis=1, keepdims=True)

    def scatter_sums(lhs, finish, out, mine, pair, pre, got, at, image=None, curve=None, curves=None):
        if image is not None:
            curve[0] = to_row(squares(image))
            send(curve.at[0], curve.at[1], CURVE + at - 1, sibling)
            send(curve.at[0], curves.at[NZ // 2 - 1], CURVES + at - 1, at_line(NZ // 2)[1])
            send(curve.at[0], curves.at[NZ - 1], CURVES + at - 1, across)
        out[...] = finish(dot_nn(lhs, library[:, their_half]))
        send(out, pair, PAIR + at, sibling)
        far = pl.ds(pl.multiple_of(opposite * OWN, OWN), OWN)
        send(out.at[:, far], got.at[NZ - 1], SUMS + at, across)
        mine[...] = finish(dot_nn(lhs, library[:, own_half]))
        send(mine.at[:, far], got.at[NZ // 2 - 1], SUMS + at, at_line(NZ // 2)[1])
        if image is not None:
            drain(curve.at[1], recv_sem.at[CURVE + at - 1])
            curve[2] = curve[0] + curve[1]
        drain(pair, recv_sem.at[PAIR + at])
        pre[...] = mine[...] + pair[...]
        for step in FAR_FIRST:
            other, device = at_line(step)
            theirs = pl.ds(pl.multiple_of(other * OWN, OWN), OWN)
            if step == NZ // 2:
                continue
            send(pre.at[:, theirs], got.at[step - 1], SUMS + at, device)
            if image is not None:
                send(curve.at[2], curves.at[step - 1], CURVES + at - 1, device)

    def sum_up(pre, got, at):
        drain(got, recv_sem.at[SUMS + at])
        total = pre[:, own_slice]
        for step in range(NZ):
            total = total + got[step]
        return total * mask * (1.0 / SNAPS)

    def curvature(curve, curves, at):
        drain(curves, recv_sem.at[CURVES + at - 1])
        total = curve[2]
        for step in range(NZ):
            total = total + curves[step]
        return to_column(total) * (1.0 / SNAPS)

    def gather_terms(value, full, at):
        arrived = ARRIVED + RING * at

        def slice_of(side, step):
            begin = side * HALF + lax.rem(z - step + NZ, NZ) * OWN
            return full.at[:, pl.ds(pl.multiple_of(begin, OWN), OWN)]

        def forward(step):
            send(slice_of(core, step), slice_of(core, step), HALVES + at, sibling, arrived + NZ + step)

        def wait(side, steps):
            for step in steps:
                slot = arrived + step if side == 0 else arrived + NZ + step
                drain(full.at[:, pl.ds(0, OWN)], recv_sem.at[slot])
                if side == 0 and step != NZ // 2:
                    forward(step)

        def product(side, steps):
            total = None
            for step in steps:
                which = core if side == 0 else 1 - core
                begin = which * HALF + lax.rem(z - step + NZ, NZ) * OWN
                span = pl.ds(pl.multiple_of(begin, OWN), OWN)
                term = dot_nt(split(full[:, span]), library[:, span])
                total = term if total is None else total + term
            return total

        full[:, own_terms] = value
        for step in FAR_FIRST:
            send(
                slice_of(core, 0), slice_of(core, 0), SLICES + at, at_line(step)[1], arrived + step
            )
            if step == NZ // 2:
                send(slice_of(core, 0), slice_of(core, 0), SLICES + at, across, arrived + NZ + step)
        forward(0)
        image = product(0, (0,))
        wait(1, (0,))
        image = image + product(1, (0,))
        wait(0, (1, 7))
        image = image + product(0, (1, 7))
        wait(0, (2, 6))
        wait(0, (3, 5))
        image = image + product(0, (2, 6, 3, 5))
        wait(1, (1, 7))
        image = image + product(1, (1, 7))
        wait(0, (4,))
        wait(1, (4,))
        image = image + product(0, (4,)) + product(1, (4,))
        wait(1, (2, 6))
        image = image + product(1, (2, 6))
        wait(1, (3, 5))
        return merge(image + product(1, (3, 5)))

    scatter_sums(given, lambda value: value[:GROUP], out0, mine0, pair0, pre0, got0, 0)
    line, lane = iota((LOCAL, OWN), 0), iota((LOCAL, OWN), 1)
    from_x = lax.rem(x - line // 128 + NX, NX)
    pick = (
        (from_x * NY + line % 128 // 16 == lane // 8)
        & (line % 16 // 8 == y // 4)
        & (line % 8 == lane % 8)
    )
    mask = dot_nn(given, chosen(pick))[GROUP:]

    direction = sum_up(pre0, got0, 0)
    image = gather_terms(direction, full0, 0)
    scatter_sums(split(image), merge, out1, mine1, pair1, pre1, got1, 1, image, curve1, curves1)
    energy = squares(full0[...])
    step_len = energy / curvature(curve1, curves1, 1)
    coeffs = step_len * direction
    resid = direction - step_len * sum_up(pre1, got1, 1)
    next_image = gather_terms(resid, full1, 1)
    fresh = squares(full1[...])
    ratio = fresh / energy
    direction = resid + ratio * direction
    image = next_image + ratio * image
    scatter_sums(split(image), merge, out2, mine2, pair2, pre2, got2, 2, image, curve2, curves2)
    step_len = fresh / curvature(curve2, curves2, 2)
    coeffs = coeffs + step_len * direction
    resid = resid - step_len * sum_up(pre2, got2, 2)

    square[0:GROUP, :] = coeffs
    square[GROUP : 2 * GROUP, :] = resid
    turn[...] = square[...].T
    lane = iota((PLANE, 128), 1) // (2 * GROUP)
    total = turn[pl.ds(0, PLANE, stride=8), :]
    for k in range(1, 8):
        total = jnp.where(
            lane == k, pltpu.roll(turn[pl.ds(k, PLANE, stride=8), :], 2 * GROUP * k, 1), total
        )
    for k in range(PLANE):
        packed[k] = total[k : k + 1]
    here = x * NY + y
    far_first = sorted(peers, key=lambda peer: -min(peer[0], NX - peer[0]) - min(peer[1], NY - peer[1]))
    for a, b in far_first:
        spot = lax.rem(x + a, NX) * NY + lax.rem(y + b, NY)
        send(packed.at[spot], unpacked.at[here], TURN, at_plane(a, b))
    unpacked[here] = packed[here]
    drain(rows.at[pl.ds(0, (NY - 1) * ROWS)], send_sem.at[0])
    drain(extra.at[pl.ds(0, (NY - 1) * ROWS)], send_sem.at[EXTRA])
    for step in (1, 2, 3):
        drain(rows.at[pl.ds(0, SLAB)], send_sem.at[SLABS + step - 1])
    drain(compact_in.at[pl.ds(0, (NX - 1) * ROWS)], send_sem.at[COMPACT])
    for k, (pair, got) in enumerate(((pair0, got0), (pair1, got1), (pair2, got2))):
        drain(pair, send_sem.at[PAIR + k])
        drain(got, send_sem.at[SUMS + k])
    for k, full in enumerate((full0, full1)):
        drain(full.at[:, pl.ds(0, HALF)], send_sem.at[SLICES + k])
        drain(full.at[:, pl.ds(0, HALF - OWN)], send_sem.at[HALVES + k])
    for k, (curve, curves) in enumerate(((curve1, curves1), (curve2, curves2))):
        drain(curve.at[1], send_sem.at[CURVE + k])
        drain(curves, send_sem.at[CURVES + k])
    drain(unpacked.at[pl.ds(0, PLANE - 1)], recv_sem.at[TURN])
    received = jnp.concatenate(
        [unpacked[k] for k in range(PLANE)] + [jnp.zeros((128 - PLANE, 128), F32)], axis=0
    )
    turned[...] = received.T
    sides = []
    for out in range(2):
        for part in range(2):
            total = turned[pl.ds(out * GROUP + 4 * part, 8, stride=2 * GROUP), :]
            for k in range(1, 4):
                more = turned[pl.ds(out * GROUP + 4 * part + k, 8, stride=2 * GROUP), :]
                total = jnp.where(quarter == k, pltpu.roll(more, PLANE * k, 1), total)
            sides.append(total)
    both = jnp.concatenate(
        [jnp.concatenate(sides[0:2], axis=1), jnp.concatenate(sides[2:4], axis=1)], axis=0
    )
    high = both.astype(BF16)
    rest = both - high.astype(F32)
    middle = rest.astype(BF16)
    low = (rest - middle.astype(F32)).astype(BF16)
    moved = dot_nn(jnp.concatenate([high, middle, low], axis=0), spread[...])
    out_ref[...] = moved[0:16] + moved[16:32] + moved[32:48]

    drain(unpacked.at[pl.ds(0, PLANE - 1)], send_sem.at[TURN])


def body(modes, targets, pairs, support):
    vmem = pl.BlockSpec(memory_space=pltpu.VMEM)
    hbm = pl.BlockSpec(memory_space=pltpu.HBM)
    both = pl.pallas_call(
        kernel,
        out_shape=jax.ShapeDtypeStruct((16, TARGETS), F32),
        in_specs=[hbm] * 4,
        out_specs=vmem,
        scratch_shapes=[
            pltpu.VMEM((ROWS, TARGETS), BF16),
            pltpu.VMEM((2, TERMS), jnp.int32),
            pltpu.VMEM((8, TARGETS), jnp.int32),
            pltpu.VMEM((LOCAL, MODES), BF16),
            pltpu.VMEM((SLAB, 128), BF16),
            pltpu.VMEM((SLAB, 128), BF16),
            pltpu.VMEM((NX * ROWS, 128), BF16),
            pltpu.VMEM((NX * ROWS, 128), BF16),
            pltpu.VMEM((MODES, TERMS), BF16),
            pltpu.VMEM((MODES, TERMS), BF16),
            pltpu.VMEM((2 * NZ, 512), jnp.int32),
            pltpu.VMEM((LOCAL, TERMS), BF16),
        ]
        + [pltpu.VMEM((GROUP, HALF), F32)] * 12
        + [pltpu.VMEM((NZ, GROUP, OWN), F32)] * 3
        + [pltpu.VMEM((GROUP, TERMS), F32)] * 2
        + [
            pltpu.VMEM((3, 1, 128), F32),
            pltpu.VMEM((3, 1, 128), F32),
            pltpu.VMEM((NZ, 1, 128), F32),
            pltpu.VMEM((NZ, 1, 128), F32),
            pltpu.VMEM((OWN, 128), F32),
            pltpu.VMEM((128, OWN), F32),
            pltpu.VMEM((128, 128), F32),
            pltpu.VMEM((PLANE, 1, 128), F32),
            pltpu.VMEM((PLANE, 1, 128), F32),
            pltpu.VMEM((TARGETS, TARGETS), BF16),
            pltpu.SemaphoreType.DMA((4,)),
            pltpu.SemaphoreType.DMA((ARRIVED,)),
            pltpu.SemaphoreType.DMA((STAGES,)),
        ],
        compiler_params=pltpu.CompilerParams(
            collective_id=0, has_side_effects=True, vmem_limit_bytes=48 * 2**20
        ),
        name="regression",
    )(*(pltpu.with_memory_space_constraint(v, pltpu.HBM) for v in (modes, targets, pairs.T, support)))
    return both[:8], both[8:]


def solution(mesh):
    rows = P(("snap", "tile"), None)
    return jax.shard_map(
        body,
        mesh=mesh,
        in_specs=(rows, rows, P(), rows),
        out_specs=(rows, rows),
        check_vma=False,
    )
```

```python
import jax
import jax.numpy as jnp
from jax import lax
from jax.experimental import pallas as pl
from jax.experimental.pallas import tpu as pltpu
from jax.sharding import PartitionSpec as P

NX, NY, NZ, NC = 4, 8, 8, 2
RING = NZ * NC
PLANE = NX * NY
MODES = 256
TARGETS = 256
TERMS = 4096
ROWS = 16
SNAPS = 8192
SLAB = NY * ROWS
LOCAL = PLANE * ROWS
OWN = TERMS // RING
HALF = TERMS // NC
GROUP = TARGETS // PLANE
CHUNK = 2048
FAR_FIRST = (4, 3, 5, 2, 6, 1, 7)
NEAR_FIRST = (1, 7, 2, 6, 3, 5, 4)
F32 = jnp.float32
BF16 = jnp.bfloat16
MESH = pl.DeviceIdType.MESH

EXTRA, SLABS, COMPACT, PAIR, SUMS, SLICES, HALVES, CURVE, CURVES, TURN = 7, 8, 11, 12, 15, 18, 20, 22, 24, 26
ARRIVED = 27
MIDDLE = ARRIVED + 2 * RING
STAGES = MIDDLE + 3


def split(value):
    high = value.astype(BF16)
    low = (value - high.astype(F32)).astype(BF16)
    return jnp.concatenate([high, low], axis=0)


def merge(value):
    return value[:GROUP] + value[GROUP:]


def dot_nt(lhs, rhs):
    return lax.dot_general(lhs, rhs, (((1,), (1,)), ((), ())), preferred_element_type=F32)


def dot_nn(lhs, rhs):
    return jnp.dot(lhs, rhs, preferred_element_type=F32)


def iota(shape, dim):
    return lax.broadcasted_iota(jnp.int32, shape, dim)


def chosen(condition):
    return condition.astype(F32).astype(BF16)


def drain(ref, sem):
    pltpu.make_async_copy(ref, ref, sem).wait()


def kernel(
    modes_ref, targets_ref, pairs_ref, support_ref, out_ref,
    targets_in, pairs_in, support_in, rows, leaving, extra, compact, compact_in,
    hot_a, hot_b, constant, terms, library,
    out0, out1, out2, mine0, mine1, mine2, pair0, pair1, pair2, pre0, pre1, pre2, got0, got1, got2,
    full0, full1, curve1, curve2, curves1, curves2, turn, square, turned, packed, unpacked, spread,
    load_sem, send_sem, recv_sem,
):
    z = lax.axis_index("snap")
    tile = lax.axis_index("tile")
    x = tile // (NY * NC)
    y = (tile // NC) % NY
    core = tile % NC

    def at_plane(step_x, step_y):
        return z, (lax.rem(x + step_x, NX) * NY + lax.rem(y + step_y, NY)) * NC + core

    def at_line(step):
        other = lax.rem(z + step, NZ)
        return other, (other, tile)

    sibling = (z, tile + 1 - 2 * core)
    opposite = lax.rem(z + NZ // 2, NZ)
    across = (opposite, tile + 1 - 2 * core)

    own_block = pl.ds(pl.multiple_of(y * ROWS, ROWS), ROWS)
    loads = [
        pltpu.make_async_copy(modes_ref, rows.at[own_block], load_sem.at[0]),
        pltpu.make_async_copy(targets_ref, targets_in, load_sem.at[1]),
        pltpu.make_async_copy(support_ref, support_in, load_sem.at[2]),
        pltpu.make_async_copy(pairs_ref, pairs_in, load_sem.at[3]),
    ]
    for load in loads:
        load.start()

    barrier = pltpu.get_barrier_semaphore()
    peers = [(a, b) for a in range(NX) for b in range(NY) if a or b]
    lines = [(a, b) for a, b in peers if not (a and b)]
    for a, b in lines:
        pl.semaphore_signal(barrier, inc=1, device_id=at_plane(a, b), device_id_type=MESH)
    for step in range(1, NZ):
        pl.semaphore_signal(barrier, inc=1, device_id=at_line(step)[1], device_id_type=MESH)
    pl.semaphore_signal(barrier, inc=1, device_id=sibling, device_id_type=MESH)
    pl.semaphore_signal(barrier, inc=1, device_id=across, device_id_type=MESH)

    def send(src, dst, stage, device, arrive=None):
        pltpu.make_async_remote_copy(
            src_ref=src, dst_ref=dst, send_sem=send_sem.at[stage],
            recv_sem=recv_sem.at[stage if arrive is None else arrive],
            device_id=device, device_id_type=MESH,
        ).start()

    for load in loads[:3]:
        load.wait()
    given = targets_in[...].astype(F32)
    active = support_in[...].astype(F32)
    active = jnp.concatenate([active[:, :128], active[:, 128:]], axis=0)
    lane = iota((ROWS, 128), 1)
    for k in range(NY):
        left = given[:, k // 4 * 128 : k // 4 * 128 + 128]
        shift = 32 * (k % 4)
        left = pltpu.roll(left, 128 - shift, 1) if shift else left
        right = pltpu.roll(active, (160 - shift) % 128, 1) if shift != 32 else active
        both = jnp.where(lane < 32, left, jnp.where(lane < 64, right, 0.0))
        leaving[k * ROWS : (k + 1) * ROWS, :] = both.astype(BF16)
    extra[own_block, :] = leaving[own_block, :]
    pl.semaphore_wait(barrier, len(lines) + NZ - 1 + 2)

    for step in FAR_FIRST:
        send(rows.at[own_block], rows.at[own_block], 0, at_plane(0, step), step - 1)

    def forward(block):
        source = pl.multiple_of(block * ROWS, ROWS)
        for step in (2, 1, 3):
            target = pl.multiple_of(step * SLAB + block * ROWS, ROWS)
            send(
                rows.at[pl.ds(source, ROWS)], rows.at[pl.ds(target, ROWS)], SLABS + step - 1,
                at_plane(step, 0),
            )

    forward(y)
    for step in FAR_FIRST:
        theirs = pl.ds(pl.multiple_of(lax.rem(y + step, NY) * ROWS, ROWS), ROWS)
        send(leaving.at[theirs], extra.at[own_block], EXTRA, at_plane(0, step))

    loads[3].wait()
    pairs = pairs_in[...].astype(F32)
    stacked = jnp.concatenate(
        [pairs[side : side + 1, 512 * k : 512 * k + 512] for side in (0, 1) for k in range(NZ)],
        axis=0,
    ).astype(BF16)
    place = iota((512, 512), 1)
    origin = (place % 256) // 8 * 16 + place // 256 * 8 + place % 8
    terms[...] = dot_nn(stacked, chosen(iota((512, 512), 0) == origin)).astype(jnp.int32)
    index = iota((MODES, OWN), 0)

    def make_hot(c):
        side = jnp.where(core == c, 0, HALF)
        for k in range(NZ):
            from_lane = slice(OWN * c, OWN * c + OWN)
            begin = side + OWN * lax.rem(k - z + NZ, NZ)
            span = pl.ds(pl.multiple_of(begin, OWN), OWN)
            second = terms[NZ + k : NZ + k + 1, from_lane]
            hot_a[:, span] = chosen(index == terms[k : k + 1, from_lane])
            hot_b[:, span] = chosen(index == second)
            constant[:, span] = (second == MODES).astype(F32)

    make_hot(0)
    for step in NEAR_FIRST:
        drain(rows.at[pl.ds(0, ROWS)], recv_sem.at[step - 1])
        forward(lax.rem(y - step + NY, NY))

    drain(extra.at[pl.ds(0, (NY - 1) * ROWS)], recv_sem.at[EXTRA])
    line = iota((NX * ROWS, 128), 0)
    column = line // ROWS * GROUP + line % GROUP + jnp.where(line % ROWS < GROUP, 0, 32)
    compact[...] = dot_nt(chosen(iota((NX * ROWS, 128), 1) == column), extra[...]).astype(BF16)
    for step in (2, 1, 3):
        theirs = pl.ds(pl.multiple_of(lax.rem(x + step, NX) * ROWS, ROWS), ROWS)
        send(
            compact.at[theirs], compact_in.at[pl.ds(step * ROWS, ROWS)], COMPACT,
            at_plane(step, 0),
        )
    compact_in[0:ROWS, :] = compact[pl.ds(pl.multiple_of(x * ROWS, ROWS), ROWS), :]

    make_hot(1)

    def build(begin, end):
        for k in range(TERMS // CHUNK):
            span = slice(k * CHUNK, (k + 1) * CHUNK)
            first = dot_nn(rows[begin:end, :], hot_a[:, span])
            second = dot_nn(rows[begin:end, :], hot_b[:, span]) + constant[:, span]
            library[begin:end, span] = (first * second).astype(BF16)

    build(0, SLAB)
    square[...] = jnp.zeros_like(square)
    quarter = iota((8, 128), 1) // PLANE
    line, lane = iota((TARGETS, TARGETS), 0), iota((TARGETS, TARGETS), 1)
    ring = line % PLANE % NY * NX + line % PLANE // NY
    spread[...] = chosen(ring * GROUP + line // PLANE == lane)
    for step in (1, 3, 2):
        drain(rows.at[pl.ds(0, SLAB)], recv_sem.at[SLABS + step - 1])
    build(SLAB, LOCAL)

    drain(compact_in.at[pl.ds(0, (NX - 1) * ROWS)], recv_sem.at[COMPACT])
    given = jnp.concatenate([compact_in[k * ROWS : (k + 1) * ROWS, :] for k in range(NX)], axis=1)
    def squares(vector):
        return jnp.sum(vector * vector, axis=1, keepdims=True)

    diagonal = iota((GROUP, 128), 0) == iota((GROUP, 128), 1)

    def to_row(column):
        return jnp.sum(jnp.where(diagonal, column, 0.0), axis=0, keepdims=True)

    def to_column(row):
        return jnp.sum(jnp.where(diagonal, row, 0.0), axis=1, keepdims=True)

    def scatter_sums(lhs, finish, out, mine, pair, pre, got, at, image=None, curve=None, curves=None):
        if image is not None:
            curve[0] = to_row(squares(image))
            send(curve.at[0], curve.at[1], CURVE + at - 1, sibling)
            send(curve.at[0], curves.at[NZ // 2 - 1], CURVES + at - 1, at_line(NZ // 2)[1])
            send(curve.at[0], curves.at[NZ - 1], CURVES + at - 1, across)
        far = pl.ds(NZ // 2 * OWN, OWN)
        middle, start, end = (slice(a * OWN, b * OWN) for a, b in ((3, 6), (0, 3), (6, 8)))

        def partial(side, where):
            columns = slice(side * HALF + where.start, side * HALF + where.stop)
            return finish(dot_nn(lhs, library[:, columns]))

        out[:, middle] = partial(1, middle)
        send(out.at[:, middle], pair.at[:, middle], PAIR + at, sibling, MIDDLE + at)
        send(out.at[:, far], got.at[NZ - 1], SUMS + at, across)
        mine[:, middle] = partial(0, middle)
        send(mine.at[:, far], got.at[NZ // 2 - 1], SUMS + at, at_line(NZ // 2)[1])
        for where in (start, end):
            out[:, where] = partial(1, where)
            send(out.at[:, where], pair.at[:, where], PAIR + at, sibling)
        for where in (start, end):
            mine[:, where] = partial(0, where)

        def share(step):
            device = at_line(step)[1]
            send(pre.at[:, pl.ds(step * OWN, OWN)], got.at[step - 1], SUMS + at, device)
            if image is not None:
                send(curve.at[2], curves.at[step - 1], CURVES + at - 1, device)

        if image is not None:
            drain(curve.at[1], recv_sem.at[CURVE + at - 1])
            curve[2] = curve[0] + curve[1]
        drain(pair.at[:, middle], recv_sem.at[MIDDLE + at])
        pre[:, middle] = mine[:, middle] + pair[:, middle]
        share(3)
        share(5)
        drain(pair.at[:, pl.ds(0, 5 * OWN)], recv_sem.at[PAIR + at])
        for where in (start, end):
            pre[:, where] = mine[:, where] + pair[:, where]
        for step in (2, 6, 1, 7):
            share(step)

    def sum_up(pre, got, at):
        drain(got, recv_sem.at[SUMS + at])
        total = pre[:, :OWN]
        for step in range(NZ):
            total = total + got[step]
        return total * mask * (1.0 / SNAPS)

    def curvature(curve, curves, at):
        drain(curves, recv_sem.at[CURVES + at - 1])
        total = curve[2]
        for step in range(NZ):
            total = total + curves[step]
        return to_column(total) * (1.0 / SNAPS)

    def gather_terms(value, full, at):
        arrived = ARRIVED + RING * at

        def span(side, step):
            return pl.ds(side * HALF + (NZ - step) % NZ * OWN, OWN)

        def forward(step):
            send(
                full.at[:, span(0, step)], full.at[:, span(1, step)], HALVES + at, sibling,
                arrived + NZ + step,
            )

        def wait(side, steps):
            for step in steps:
                slot = arrived + step if side == 0 else arrived + NZ + step
                drain(full.at[:, pl.ds(0, OWN)], recv_sem.at[slot])
                if side == 0 and step != NZ // 2:
                    forward(step)

        def product(side, steps):
            total = None
            for step in steps:
                term = dot_nt(split(full[:, span(side, step)]), library[:, span(side, step)])
                total = term if total is None else total + term
            return total

        full[:, :OWN] = value
        mine = full.at[:, pl.ds(0, OWN)]
        for step in FAR_FIRST:
            send(mine, full.at[:, span(0, step)], SLICES + at, at_line(step)[1], arrived + step)
            if step == NZ // 2:
                send(mine, full.at[:, span(1, step)], SLICES + at, across, arrived + NZ + step)
        forward(0)
        image = product(0, (0,))
        wait(1, (0,))
        image = image + product(1, (0,))
        wait(0, (1, 7))
        image = image + product(0, (1, 7))
        wait(0, (2, 6))
        wait(0, (3, 5))
        image = image + product(0, (2, 6, 3, 5))
        wait(1, (1, 7))
        image = image + product(1, (1, 7))
        wait(0, (4,))
        wait(1, (4,))
        image = image + product(0, (4,)) + product(1, (4,))
        wait(1, (2, 6))
        image = image + product(1, (2, 6))
        wait(1, (3, 5))
        return merge(image + product(1, (3, 5)))

    scatter_sums(given, lambda value: value[:GROUP], out0, mine0, pair0, pre0, got0, 0)
    line, lane = iota((LOCAL, OWN), 0), iota((LOCAL, OWN), 1)
    from_x = lax.rem(x - line // 128 + NX, NX)
    pick = (
        (from_x * NY + line % 128 // 16 == lane // 8)
        & (line % 16 // 8 == y // 4)
        & (line % 8 == lane % 8)
    )
    mask = dot_nn(given, chosen(pick))[GROUP:]

    direction = sum_up(pre0, got0, 0)
    image = gather_terms(direction, full0, 0)
    scatter_sums(split(image), merge, out1, mine1, pair1, pre1, got1, 1, image, curve1, curves1)
    energy = squares(full0[...])
    step_len = energy / curvature(curve1, curves1, 1)
    coeffs = step_len * direction
    resid = direction - step_len * sum_up(pre1, got1, 1)
    next_image = gather_terms(resid, full1, 1)
    fresh = squares(full1[...])
    ratio = fresh / energy
    direction = resid + ratio * direction
    image = next_image + ratio * image
    scatter_sums(split(image), merge, out2, mine2, pair2, pre2, got2, 2, image, curve2, curves2)
    step_len = fresh / curvature(curve2, curves2, 2)
    coeffs = coeffs + step_len * direction
    resid = resid - step_len * sum_up(pre2, got2, 2)

    square[0:GROUP, :] = coeffs
    square[GROUP : 2 * GROUP, :] = resid
    turn[...] = square[...].T
    lane = iota((PLANE, 128), 1) // (2 * GROUP)
    total = turn[pl.ds(0, PLANE, stride=8), :]
    for k in range(1, 8):
        total = jnp.where(
            lane == k, pltpu.roll(turn[pl.ds(k, PLANE, stride=8), :], 2 * GROUP * k, 1), total
        )
    for k in range(PLANE):
        packed[k] = total[k : k + 1]
    here = x * NY + y
    far_first = sorted(peers, key=lambda peer: -min(peer[0], NX - peer[0]) - min(peer[1], NY - peer[1]))
    for a, b in far_first:
        spot = lax.rem(x + a, NX) * NY + lax.rem(y + b, NY)
        send(packed.at[spot], unpacked.at[here], TURN, at_plane(a, b))
    unpacked[here] = packed[here]
    drain(rows.at[pl.ds(0, (NY - 1) * ROWS)], send_sem.at[0])
    drain(extra.at[pl.ds(0, (NY - 1) * ROWS)], send_sem.at[EXTRA])
    for step in (1, 2, 3):
        drain(rows.at[pl.ds(0, SLAB)], send_sem.at[SLABS + step - 1])
    drain(compact_in.at[pl.ds(0, (NX - 1) * ROWS)], send_sem.at[COMPACT])
    for k, (pair, got) in enumerate(((pair0, got0), (pair1, got1), (pair2, got2))):
        drain(pair, send_sem.at[PAIR + k])
        drain(got, send_sem.at[SUMS + k])
    for k, full in enumerate((full0, full1)):
        drain(full.at[:, pl.ds(0, HALF)], send_sem.at[SLICES + k])
        drain(full.at[:, pl.ds(0, HALF - OWN)], send_sem.at[HALVES + k])
    for k, (curve, curves) in enumerate(((curve1, curves1), (curve2, curves2))):
        drain(curve.at[1], send_sem.at[CURVE + k])
        drain(curves, send_sem.at[CURVES + k])
    drain(unpacked.at[pl.ds(0, PLANE - 1)], recv_sem.at[TURN])
    received = jnp.concatenate(
        [unpacked[k] for k in range(PLANE)] + [jnp.zeros((128 - PLANE, 128), F32)], axis=0
    )
    turned[...] = received.T
    sides = []
    for out in range(2):
        for part in range(2):
            total = turned[pl.ds(out * GROUP + 4 * part, 8, stride=2 * GROUP), :]
            for k in range(1, 4):
                more = turned[pl.ds(out * GROUP + 4 * part + k, 8, stride=2 * GROUP), :]
                total = jnp.where(quarter == k, pltpu.roll(more, PLANE * k, 1), total)
            sides.append(total)
    both = jnp.concatenate(
        [jnp.concatenate(sides[0:2], axis=1), jnp.concatenate(sides[2:4], axis=1)], axis=0
    )
    high = both.astype(BF16)
    rest = both - high.astype(F32)
    middle = rest.astype(BF16)
    low = (rest - middle.astype(F32)).astype(BF16)
    moved = dot_nn(jnp.concatenate([high, middle, low], axis=0), spread[...])
    out_ref[...] = moved[0:16] + moved[16:32] + moved[32:48]

    drain(unpacked.at[pl.ds(0, PLANE - 1)], send_sem.at[TURN])


def body(modes, targets, pairs, support):
    vmem = pl.BlockSpec(memory_space=pltpu.VMEM)
    hbm = pl.BlockSpec(memory_space=pltpu.HBM)
    both = pl.pallas_call(
        kernel,
        out_shape=jax.ShapeDtypeStruct((16, TARGETS), F32),
        in_specs=[hbm] * 4,
        out_specs=vmem,
        scratch_shapes=[
            pltpu.VMEM((ROWS, TARGETS), BF16),
            pltpu.VMEM((2, TERMS), jnp.int32),
            pltpu.VMEM((8, TARGETS), jnp.int32),
            pltpu.VMEM((LOCAL, MODES), BF16),
            pltpu.VMEM((SLAB, 128), BF16),
            pltpu.VMEM((SLAB, 128), BF16),
            pltpu.VMEM((NX * ROWS, 128), BF16),
            pltpu.VMEM((NX * ROWS, 128), BF16),
            pltpu.VMEM((MODES, TERMS), BF16),
            pltpu.VMEM((MODES, TERMS), BF16),
            pltpu.VMEM((1, TERMS), F32),
            pltpu.VMEM((2 * NZ, 512), jnp.int32),
            pltpu.VMEM((LOCAL, TERMS), BF16),
        ]
        + [pltpu.VMEM((GROUP, HALF), F32)] * 12
        + [pltpu.VMEM((NZ, GROUP, OWN), F32)] * 3
        + [pltpu.VMEM((GROUP, TERMS), F32)] * 2
        + [
            pltpu.VMEM((3, 1, 128), F32),
            pltpu.VMEM((3, 1, 128), F32),
            pltpu.VMEM((NZ, 1, 128), F32),
            pltpu.VMEM((NZ, 1, 128), F32),
            pltpu.VMEM((OWN, 128), F32),
            pltpu.VMEM((128, OWN), F32),
            pltpu.VMEM((128, 128), F32),
            pltpu.VMEM((PLANE, 1, 128), F32),
            pltpu.VMEM((PLANE, 1, 128), F32),
            pltpu.VMEM((TARGETS, TARGETS), BF16),
            pltpu.SemaphoreType.DMA((4,)),
            pltpu.SemaphoreType.DMA((ARRIVED,)),
            pltpu.SemaphoreType.DMA((STAGES,)),
        ],
        compiler_params=pltpu.CompilerParams(
            collective_id=0, has_side_effects=True, vmem_limit_bytes=48 * 2**20
        ),
        name="regression",
    )(*(pltpu.with_memory_space_constraint(v, pltpu.HBM) for v in (modes, targets, pairs.T, support)))
    return both[:8], both[8:]


def solution(mesh):
    rows = P(("snap", "tile"), None)
    return jax.shard_map(
        body,
        mesh=mesh,
        in_specs=(rows, rows, P(), rows),
        out_specs=(rows, rows),
        check_vma=False,
    )
```

```python
import jax
import jax.numpy as jnp
from jax import lax
from jax.experimental import pallas as pl
from jax.experimental.pallas import tpu as pltpu
from jax.sharding import PartitionSpec as P

NX, NY, NZ, NC = 4, 8, 8, 2
RING = NZ * NC
PLANE = NX * NY
MODES = 256
TARGETS = 256
TERMS = 4096
ROWS = 16
SNAPS = 8192
SLAB = NY * ROWS
LOCAL = PLANE * ROWS
OWN = TERMS // RING
HALF = TERMS // NC
GROUP = TARGETS // PLANE
CHUNK = 2048
FAR_FIRST = (4, 3, 5, 2, 6, 1, 7)
NEAR_FIRST = (1, 7, 2, 6, 3, 5, 4)
F32 = jnp.float32
BF16 = jnp.bfloat16
MESH = pl.DeviceIdType.MESH

EXTRA, SLABS, COMPACT, PAIR, SUMS, SLICES, HALVES, CURVE, CURVES, TURN = 7, 8, 11, 12, 15, 18, 20, 22, 24, 26
ARRIVED = 27
MIDDLE = ARRIVED + 2 * RING
STAGES = MIDDLE + 3


def split(value):
    high = value.astype(BF16)
    low = (value - high.astype(F32)).astype(BF16)
    return jnp.concatenate([high, low], axis=0)


def merge(value):
    return value[:GROUP] + value[GROUP:]


def dot_nt(lhs, rhs):
    return lax.dot_general(lhs, rhs, (((1,), (1,)), ((), ())), preferred_element_type=F32)


def dot_nn(lhs, rhs):
    return jnp.dot(lhs, rhs, preferred_element_type=F32)


def iota(shape, dim):
    return lax.broadcasted_iota(jnp.int32, shape, dim)


def chosen(condition):
    return condition.astype(F32).astype(BF16)


def drain(ref, sem):
    pltpu.make_async_copy(ref, ref, sem).wait()


def kernel(
    modes_ref, targets_ref, pairs_ref, support_ref, out_ref,
    targets_in, pairs_in, support_in, rows, leaving, extra, compact, compact_in,
    hot_a, hot_b, constant, terms, library,
    out0, out1, out2, mine0, mine1, mine2, pair0, pair1, pair2, pre0, pre1, pre2, got0, got1, got2,
    full0, full1, curve1, curve2, curves1, curves2, turn, square, turned, packed, unpacked, spread,
    load_sem, send_sem, recv_sem,
):
    z = lax.axis_index("snap")
    tile = lax.axis_index("tile")
    x = tile // (NY * NC)
    y = (tile // NC) % NY
    core = tile % NC

    def at_plane(step_x, step_y):
        return z, (lax.rem(x + step_x, NX) * NY + lax.rem(y + step_y, NY)) * NC + core

    def at_line(step):
        other = lax.rem(z + step, NZ)
        return other, (other, tile)

    sibling = (z, tile + 1 - 2 * core)
    opposite = lax.rem(z + NZ // 2, NZ)
    across = (opposite, tile + 1 - 2 * core)

    own_block = pl.ds(pl.multiple_of(y * ROWS, ROWS), ROWS)
    loads = [
        pltpu.make_async_copy(modes_ref, rows.at[own_block], load_sem.at[0]),
        pltpu.make_async_copy(targets_ref, targets_in, load_sem.at[1]),
        pltpu.make_async_copy(support_ref, support_in, load_sem.at[2]),
        pltpu.make_async_copy(pairs_ref, pairs_in, load_sem.at[3]),
    ]
    for load in loads:
        load.start()

    barrier = pltpu.get_barrier_semaphore()
    peers = [(a, b) for a in range(NX) for b in range(NY) if a or b]
    lines = [(a, b) for a, b in peers if not (a and b)]
    for a, b in lines:
        pl.semaphore_signal(barrier, inc=1, device_id=at_plane(a, b), device_id_type=MESH)
    for step in range(1, NZ):
        pl.semaphore_signal(barrier, inc=1, device_id=at_line(step)[1], device_id_type=MESH)
    pl.semaphore_signal(barrier, inc=1, device_id=sibling, device_id_type=MESH)
    pl.semaphore_signal(barrier, inc=1, device_id=across, device_id_type=MESH)

    def send(src, dst, stage, device, arrive=None):
        pltpu.make_async_remote_copy(
            src_ref=src, dst_ref=dst, send_sem=send_sem.at[stage],
            recv_sem=recv_sem.at[stage if arrive is None else arrive],
            device_id=device, device_id_type=MESH,
        ).start()

    for load in loads[:3]:
        load.wait()
    given = targets_in[...].astype(F32)
    active = support_in[...].astype(F32)
    active = jnp.concatenate([active[:, :128], active[:, 128:]], axis=0)
    lane = iota((ROWS, 128), 1)
    for k in range(NY):
        left = given[:, k // 4 * 128 : k // 4 * 128 + 128]
        shift = 32 * (k % 4)
        left = pltpu.roll(left, 128 - shift, 1) if shift else left
        right = pltpu.roll(active, (160 - shift) % 128, 1) if shift != 32 else active
        both = jnp.where(lane < 32, left, jnp.where(lane < 64, right, 0.0))
        leaving[k * ROWS : (k + 1) * ROWS, :] = both.astype(BF16)
    extra[own_block, :] = leaving[own_block, :]
    pl.semaphore_wait(barrier, len(lines) + NZ - 1 + 2)

    for step in FAR_FIRST:
        send(rows.at[own_block], rows.at[own_block], 0, at_plane(0, step), step - 1)

    def forward(block):
        source = pl.multiple_of(block * ROWS, ROWS)
        for step in (2, 1, 3):
            target = pl.multiple_of(step * SLAB + block * ROWS, ROWS)
            send(
                rows.at[pl.ds(source, ROWS)], rows.at[pl.ds(target, ROWS)], SLABS + step - 1,
                at_plane(step, 0),
            )

    forward(y)
    for step in FAR_FIRST:
        theirs = pl.ds(pl.multiple_of(lax.rem(y + step, NY) * ROWS, ROWS), ROWS)
        send(leaving.at[theirs], extra.at[own_block], EXTRA, at_plane(0, step))

    loads[3].wait()
    pairs = pairs_in[...].astype(F32)
    stacked = jnp.concatenate(
        [pairs[side : side + 1, 512 * k : 512 * k + 512] for side in (0, 1) for k in range(NZ)],
        axis=0,
    ).astype(BF16)
    place = iota((512, 512), 1)
    origin = (place % 256) // 8 * 16 + place // 256 * 8 + place % 8
    terms[...] = dot_nn(stacked, chosen(iota((512, 512), 0) == origin)).astype(jnp.int32)
    index = iota((MODES, OWN), 0)

    def make_hot(c):
        side = jnp.where(core == c, 0, HALF)
        for k in range(NZ):
            from_lane = slice(OWN * c, OWN * c + OWN)
            begin = side + OWN * lax.rem(k - z + NZ, NZ)
            span = pl.ds(pl.multiple_of(begin, OWN), OWN)
            second = terms[NZ + k : NZ + k + 1, from_lane]
            hot_a[:, span] = chosen(index == terms[k : k + 1, from_lane])
            hot_b[:, span] = chosen(index == second)
            constant[:, span] = (second == MODES).astype(F32)

    make_hot(0)
    for step in NEAR_FIRST:
        drain(rows.at[pl.ds(0, ROWS)], recv_sem.at[step - 1])
        forward(lax.rem(y - step + NY, NY))

    drain(extra.at[pl.ds(0, (NY - 1) * ROWS)], recv_sem.at[EXTRA])
    line = iota((NX * ROWS, 128), 0)
    column = line // ROWS * GROUP + line % GROUP + jnp.where(line % ROWS < GROUP, 0, 32)
    compact[...] = dot_nt(chosen(iota((NX * ROWS, 128), 1) == column), extra[...]).astype(BF16)
    for step in (2, 1, 3):
        theirs = pl.ds(pl.multiple_of(lax.rem(x + step, NX) * ROWS, ROWS), ROWS)
        send(
            compact.at[theirs], compact_in.at[pl.ds(step * ROWS, ROWS)], COMPACT,
            at_plane(step, 0),
        )
    compact_in[0:ROWS, :] = compact[pl.ds(pl.multiple_of(x * ROWS, ROWS), ROWS), :]

    make_hot(1)

    def build(begin, end):
        for k in range(TERMS // CHUNK):
            span = slice(k * CHUNK, (k + 1) * CHUNK)
            first = dot_nn(rows[begin:end, :], hot_a[:, span])
            second = dot_nn(rows[begin:end, :], hot_b[:, span]) + constant[:, span]
            library[begin:end, span] = (first * second).astype(BF16)

    build(0, SLAB)
    square[...] = jnp.zeros_like(square)
    quarter = iota((8, 128), 1) // PLANE
    line, lane = iota((TARGETS, TARGETS), 0), iota((TARGETS, TARGETS), 1)
    ring = line % PLANE % NY * NX + line % PLANE // NY
    spread[...] = chosen(ring * GROUP + line // PLANE == lane)
    drain(rows.at[pl.ds(0, SLAB)], recv_sem.at[SLABS])
    build(SLAB, 2 * SLAB)
    for step in (3, 2):
        drain(rows.at[pl.ds(0, SLAB)], recv_sem.at[SLABS + step - 1])
    build(2 * SLAB, LOCAL)

    drain(compact_in.at[pl.ds(0, (NX - 1) * ROWS)], recv_sem.at[COMPACT])
    given = jnp.concatenate([compact_in[k * ROWS : (k + 1) * ROWS, :] for k in range(NX)], axis=1)
    def squares(vector):
        return jnp.sum(vector * vector, axis=1, keepdims=True)

    diagonal = iota((GROUP, 128), 0) == iota((GROUP, 128), 1)

    def to_row(column):
        return jnp.sum(jnp.where(diagonal, column, 0.0), axis=0, keepdims=True)

    def to_column(row):
        return jnp.sum(jnp.where(diagonal, row, 0.0), axis=1, keepdims=True)

    def scatter_sums(lhs, finish, out, mine, pair, pre, got, at, image=None, curve=None, curves=None):
        if image is not None:
            curve[0] = to_row(squares(image))
            send(curve.at[0], curve.at[1], CURVE + at - 1, sibling)
            send(curve.at[0], curves.at[NZ // 2 - 1], CURVES + at - 1, at_line(NZ // 2)[1])
            send(curve.at[0], curves.at[NZ - 1], CURVES + at - 1, across)
        far = pl.ds(NZ // 2 * OWN, OWN)
        middle, start, end = (slice(a * OWN, b * OWN) for a, b in ((3, 6), (0, 3), (6, 8)))

        def partial(side, where):
            columns = slice(side * HALF + where.start, side * HALF + where.stop)
            return finish(dot_nn(lhs, library[:, columns]))

        out[:, middle] = partial(1, middle)
        send(out.at[:, middle], pair.at[:, middle], PAIR + at, sibling, MIDDLE + at)
        send(out.at[:, far], got.at[NZ - 1], SUMS + at, across)
        mine[:, middle] = partial(0, middle)
        send(mine.at[:, far], got.at[NZ // 2 - 1], SUMS + at, at_line(NZ // 2)[1])
        for where in (start, end):
            out[:, where] = partial(1, where)
            send(out.at[:, where], pair.at[:, where], PAIR + at, sibling)
        for where in (start, end):
            mine[:, where] = partial(0, where)

        def share(step):
            device = at_line(step)[1]
            send(pre.at[:, pl.ds(step * OWN, OWN)], got.at[step - 1], SUMS + at, device)
            if image is not None:
                send(curve.at[2], curves.at[step - 1], CURVES + at - 1, device)

        if image is not None:
            drain(curve.at[1], recv_sem.at[CURVE + at - 1])
            curve[2] = curve[0] + curve[1]
        drain(pair.at[:, middle], recv_sem.at[MIDDLE + at])
        pre[:, middle] = mine[:, middle] + pair[:, middle]
        share(3)
        share(5)
        drain(pair.at[:, pl.ds(0, 5 * OWN)], recv_sem.at[PAIR + at])
        for where in (start, end):
            pre[:, where] = mine[:, where] + pair[:, where]
        for step in (2, 6, 1, 7):
            share(step)

    def sum_up(pre, got, at):
        drain(got, recv_sem.at[SUMS + at])
        total = pre[:, :OWN]
        for step in range(NZ):
            total = total + got[step]
        return total * mask * (1.0 / SNAPS)

    def curvature(curve, curves, at):
        drain(curves, recv_sem.at[CURVES + at - 1])
        total = curve[2]
        for step in range(NZ):
            total = total + curves[step]
        return to_column(total) * (1.0 / SNAPS)

    def gather_terms(value, full, at):
        arrived = ARRIVED + RING * at

        def span(side, step):
            return pl.ds(side * HALF + (NZ - step) % NZ * OWN, OWN)

        def forward(step):
            send(
                full.at[:, span(0, step)], full.at[:, span(1, step)], HALVES + at, sibling,
                arrived + NZ + step,
            )

        def wait(side, steps):
            for step in steps:
                slot = arrived + step if side == 0 else arrived + NZ + step
                drain(full.at[:, pl.ds(0, OWN)], recv_sem.at[slot])
                if side == 0 and step != NZ // 2:
                    forward(step)

        def product(side, steps):
            total = None
            for step in steps:
                term = dot_nt(split(full[:, span(side, step)]), library[:, span(side, step)])
                total = term if total is None else total + term
            return total

        full[:, :OWN] = value
        mine = full.at[:, pl.ds(0, OWN)]
        for step in FAR_FIRST:
            send(mine, full.at[:, span(0, step)], SLICES + at, at_line(step)[1], arrived + step)
            if step == NZ // 2:
                send(mine, full.at[:, span(1, step)], SLICES + at, across, arrived + NZ + step)
        forward(0)
        image = product(0, (0,))
        wait(1, (0,))
        image = image + product(1, (0,))
        wait(0, (1, 7))
        image = image + product(0, (1, 7))
        wait(0, (2, 6))
        wait(0, (3, 5))
        image = image + product(0, (2, 6, 3, 5))
        wait(1, (1, 7))
        image = image + product(1, (1, 7))
        wait(0, (4,))
        wait(1, (4,))
        image = image + product(0, (4,)) + product(1, (4,))
        wait(1, (2, 6))
        image = image + product(1, (2, 6))
        wait(1, (3, 5))
        return merge(image + product(1, (3, 5)))

    scatter_sums(given, lambda value: value[:GROUP], out0, mine0, pair0, pre0, got0, 0)
    line, lane = iota((LOCAL, OWN), 0), iota((LOCAL, OWN), 1)
    from_x = lax.rem(x - line // 128 + NX, NX)
    pick = (
        (from_x * NY + line % 128 // 16 == lane // 8)
        & (line % 16 // 8 == y // 4)
        & (line % 8 == lane % 8)
    )
    mask = dot_nn(given, chosen(pick))[GROUP:]

    direction = sum_up(pre0, got0, 0)
    image = gather_terms(direction, full0, 0)
    scatter_sums(split(image), merge, out1, mine1, pair1, pre1, got1, 1, image, curve1, curves1)
    energy = squares(full0[...])
    step_len = energy / curvature(curve1, curves1, 1)
    coeffs = step_len * direction
    resid = direction - step_len * sum_up(pre1, got1, 1)
    next_image = gather_terms(resid, full1, 1)
    fresh = squares(full1[...])
    ratio = fresh / energy
    direction = resid + ratio * direction
    image = next_image + ratio * image
    scatter_sums(split(image), merge, out2, mine2, pair2, pre2, got2, 2, image, curve2, curves2)
    step_len = fresh / curvature(curve2, curves2, 2)
    coeffs = coeffs + step_len * direction
    resid = resid - step_len * sum_up(pre2, got2, 2)

    square[0:GROUP, :] = coeffs
    square[GROUP : 2 * GROUP, :] = resid
    turn[...] = square[...].T
    lane = iota((PLANE, 128), 1) // (2 * GROUP)
    total = turn[pl.ds(0, PLANE, stride=8), :]
    for k in range(1, 8):
        total = jnp.where(
            lane == k, pltpu.roll(turn[pl.ds(k, PLANE, stride=8), :], 2 * GROUP * k, 1), total
        )
    for k in range(PLANE):
        packed[k] = total[k : k + 1]
    here = x * NY + y
    far_first = sorted(peers, key=lambda peer: -min(peer[0], NX - peer[0]) - min(peer[1], NY - peer[1]))
    for a, b in far_first:
        spot = lax.rem(x + a, NX) * NY + lax.rem(y + b, NY)
        send(packed.at[spot], unpacked.at[here], TURN, at_plane(a, b))
    unpacked[here] = packed[here]
    drain(rows.at[pl.ds(0, (NY - 1) * ROWS)], send_sem.at[0])
    drain(extra.at[pl.ds(0, (NY - 1) * ROWS)], send_sem.at[EXTRA])
    for step in (1, 2, 3):
        drain(rows.at[pl.ds(0, SLAB)], send_sem.at[SLABS + step - 1])
    drain(compact_in.at[pl.ds(0, (NX - 1) * ROWS)], send_sem.at[COMPACT])
    for k, (pair, got) in enumerate(((pair0, got0), (pair1, got1), (pair2, got2))):
        drain(pair, send_sem.at[PAIR + k])
        drain(got, send_sem.at[SUMS + k])
    for k, full in enumerate((full0, full1)):
        drain(full.at[:, pl.ds(0, HALF)], send_sem.at[SLICES + k])
        drain(full.at[:, pl.ds(0, HALF - OWN)], send_sem.at[HALVES + k])
    for k, (curve, curves) in enumerate(((curve1, curves1), (curve2, curves2))):
        drain(curve.at[1], send_sem.at[CURVE + k])
        drain(curves, send_sem.at[CURVES + k])
    drain(unpacked.at[pl.ds(0, PLANE - 1)], recv_sem.at[TURN])
    received = jnp.concatenate(
        [unpacked[k] for k in range(PLANE)] + [jnp.zeros((128 - PLANE, 128), F32)], axis=0
    )
    turned[...] = received.T
    sides = []
    for out in range(2):
        for part in range(2):
            total = turned[pl.ds(out * GROUP + 4 * part, 8, stride=2 * GROUP), :]
            for k in range(1, 4):
                more = turned[pl.ds(out * GROUP + 4 * part + k, 8, stride=2 * GROUP), :]
                total = jnp.where(quarter == k, pltpu.roll(more, PLANE * k, 1), total)
            sides.append(total)
    both = jnp.concatenate(
        [jnp.concatenate(sides[0:2], axis=1), jnp.concatenate(sides[2:4], axis=1)], axis=0
    )
    high = both.astype(BF16)
    rest = both - high.astype(F32)
    middle = rest.astype(BF16)
    low = (rest - middle.astype(F32)).astype(BF16)
    moved = dot_nn(jnp.concatenate([high, middle, low], axis=0), spread[...])
    out_ref[...] = moved[0:16] + moved[16:32] + moved[32:48]

    drain(unpacked.at[pl.ds(0, PLANE - 1)], send_sem.at[TURN])


def body(modes, targets, pairs, support):
    vmem = pl.BlockSpec(memory_space=pltpu.VMEM)
    hbm = pl.BlockSpec(memory_space=pltpu.HBM)
    both = pl.pallas_call(
        kernel,
        out_shape=jax.ShapeDtypeStruct((16, TARGETS), F32),
        in_specs=[hbm] * 4,
        out_specs=vmem,
        scratch_shapes=[
            pltpu.VMEM((ROWS, TARGETS), BF16),
            pltpu.VMEM((2, TERMS), jnp.int32),
            pltpu.VMEM((8, TARGETS), jnp.int32),
            pltpu.VMEM((LOCAL, MODES), BF16),
            pltpu.VMEM((SLAB, 128), BF16),
            pltpu.VMEM((SLAB, 128), BF16),
            pltpu.VMEM((NX * ROWS, 128), BF16),
            pltpu.VMEM((NX * ROWS, 128), BF16),
            pltpu.VMEM((MODES, TERMS), BF16),
            pltpu.VMEM((MODES, TERMS), BF16),
            pltpu.VMEM((1, TERMS), F32),
            pltpu.VMEM((2 * NZ, 512), jnp.int32),
            pltpu.VMEM((LOCAL, TERMS), BF16),
        ]
        + [pltpu.VMEM((GROUP, HALF), F32)] * 12
        + [pltpu.VMEM((NZ, GROUP, OWN), F32)] * 3
        + [pltpu.VMEM((GROUP, TERMS), F32)] * 2
        + [
            pltpu.VMEM((3, 1, 128), F32),
            pltpu.VMEM((3, 1, 128), F32),
            pltpu.VMEM((NZ, 1, 128), F32),
            pltpu.VMEM((NZ, 1, 128), F32),
            pltpu.VMEM((OWN, 128), F32),
            pltpu.VMEM((128, OWN), F32),
            pltpu.VMEM((128, 128), F32),
            pltpu.VMEM((PLANE, 1, 128), F32),
            pltpu.VMEM((PLANE, 1, 128), F32),
            pltpu.VMEM((TARGETS, TARGETS), BF16),
            pltpu.SemaphoreType.DMA((4,)),
            pltpu.SemaphoreType.DMA((ARRIVED,)),
            pltpu.SemaphoreType.DMA((STAGES,)),
        ],
        compiler_params=pltpu.CompilerParams(
            collective_id=0, has_side_effects=True, vmem_limit_bytes=48 * 2**20
        ),
        name="regression",
    )(*(pltpu.with_memory_space_constraint(v, pltpu.HBM) for v in (modes, targets, pairs.T, support)))
    return both[:8], both[8:]


def solution(mesh):
    rows = P(("snap", "tile"), None)
    return jax.shard_map(
        body,
        mesh=mesh,
        in_specs=(rows, rows, P(), rows),
        out_specs=(rows, rows),
        check_vma=False,
    )
```

```python
import jax
import jax.numpy as jnp
from jax import lax
from jax.experimental import pallas as pl
from jax.experimental.pallas import tpu as pltpu
from jax.sharding import PartitionSpec as P

NX, NY, NZ, NC = 4, 8, 8, 2
RING = NZ * NC
PLANE = NX * NY
MODES = 256
TARGETS = 256
TERMS = 4096
ROWS = 16
SNAPS = 8192
SLAB = NY * ROWS
LOCAL = PLANE * ROWS
OWN = TERMS // RING
HALF = TERMS // NC
GROUP = TARGETS // PLANE
CHUNK = 2048
FAR_FIRST = (4, 3, 5, 2, 6, 1, 7)
NEAR_FIRST = (1, 7, 2, 6, 3, 5, 4)
F32 = jnp.float32
BF16 = jnp.bfloat16
MESH = pl.DeviceIdType.MESH

EXTRA, SLABS, COMPACT, PAIR, SUMS, SLICES, HALVES, CURVE, CURVES, TURN = 7, 8, 11, 12, 15, 18, 20, 22, 24, 26
ARRIVED = 27
MIDDLE = ARRIVED + 2 * RING
STAGES = MIDDLE + 3


def split(value):
    high = value.astype(BF16)
    low = (value - high.astype(F32)).astype(BF16)
    return jnp.concatenate([high, low], axis=0)


def merge(value):
    return value[:GROUP] + value[GROUP:]


def dot_nt(lhs, rhs):
    return lax.dot_general(lhs, rhs, (((1,), (1,)), ((), ())), preferred_element_type=F32)


def dot_nn(lhs, rhs):
    return jnp.dot(lhs, rhs, preferred_element_type=F32)


def iota(shape, dim):
    return lax.broadcasted_iota(jnp.int32, shape, dim)


def chosen(condition):
    return condition.astype(F32).astype(BF16)


def drain(ref, sem):
    pltpu.make_async_copy(ref, ref, sem).wait()


def kernel(
    modes_ref, targets_ref, pairs_ref, support_ref, out_ref,
    targets_in, pairs_in, support_in, rows, leaving, extra, compact, compact_in,
    hot_a, hot_b, constant, terms, library,
    out0, out1, out2, mine0, mine1, mine2, pair0, pair1, pair2, pre0, pre1, pre2, got0, got1, got2,
    full0, full1, curve1, curve2, curves1, curves2, turn, square, turned, packed, unpacked, spread,
    load_sem, send_sem, recv_sem,
):
    z = lax.axis_index("snap")
    tile = lax.axis_index("tile")
    x = tile // (NY * NC)
    y = (tile // NC) % NY
    core = tile % NC

    def at_plane(step_x, step_y):
        return z, (lax.rem(x + step_x, NX) * NY + lax.rem(y + step_y, NY)) * NC + core

    def at_line(step):
        other = lax.rem(z + step, NZ)
        return other, (other, tile)

    sibling = (z, tile + 1 - 2 * core)
    opposite = lax.rem(z + NZ // 2, NZ)
    across = (opposite, tile + 1 - 2 * core)

    own_block = pl.ds(pl.multiple_of(y * ROWS, ROWS), ROWS)
    loads = [
        pltpu.make_async_copy(modes_ref, rows.at[own_block], load_sem.at[0]),
        pltpu.make_async_copy(targets_ref, targets_in, load_sem.at[1]),
        pltpu.make_async_copy(support_ref, support_in, load_sem.at[2]),
        pltpu.make_async_copy(pairs_ref, pairs_in, load_sem.at[3]),
    ]
    for load in loads:
        load.start()

    barrier = pltpu.get_barrier_semaphore()
    peers = [(a, b) for a in range(NX) for b in range(NY) if a or b]
    lines = [(a, b) for a, b in peers if not (a and b)]
    for a, b in lines:
        pl.semaphore_signal(barrier, inc=1, device_id=at_plane(a, b), device_id_type=MESH)
    for step in range(1, NZ):
        pl.semaphore_signal(barrier, inc=1, device_id=at_line(step)[1], device_id_type=MESH)
    pl.semaphore_signal(barrier, inc=1, device_id=sibling, device_id_type=MESH)
    pl.semaphore_signal(barrier, inc=1, device_id=across, device_id_type=MESH)

    def send(src, dst, stage, device, arrive=None):
        pltpu.make_async_remote_copy(
            src_ref=src, dst_ref=dst, send_sem=send_sem.at[stage],
            recv_sem=recv_sem.at[stage if arrive is None else arrive],
            device_id=device, device_id_type=MESH,
        ).start()

    for load in loads[:3]:
        load.wait()
    given = targets_in[...].astype(F32)
    active = support_in[...].astype(F32)
    active = jnp.concatenate([active[:, :128], active[:, 128:]], axis=0)
    lane = iota((ROWS, 128), 1)
    for k in range(NY):
        left = given[:, k // 4 * 128 : k // 4 * 128 + 128]
        shift = 32 * (k % 4)
        left = pltpu.roll(left, 128 - shift, 1) if shift else left
        right = pltpu.roll(active, (160 - shift) % 128, 1) if shift != 32 else active
        both = jnp.where(lane < 32, left, jnp.where(lane < 64, right, 0.0))
        leaving[k * ROWS : (k + 1) * ROWS, :] = both.astype(BF16)
    extra[own_block, :] = leaving[own_block, :]
    pl.semaphore_wait(barrier, len(lines) + NZ - 1 + 2)

    for step in FAR_FIRST:
        send(rows.at[own_block], rows.at[own_block], 0, at_plane(0, step), step - 1)

    def forward(block):
        source = pl.multiple_of(block * ROWS, ROWS)
        for step in (2, 1, 3):
            target = pl.multiple_of(step * SLAB + block * ROWS, ROWS)
            send(
                rows.at[pl.ds(source, ROWS)], rows.at[pl.ds(target, ROWS)], SLABS + step - 1,
                at_plane(step, 0),
            )

    forward(y)
    for step in FAR_FIRST:
        theirs = pl.ds(pl.multiple_of(lax.rem(y + step, NY) * ROWS, ROWS), ROWS)
        send(leaving.at[theirs], extra.at[own_block], EXTRA, at_plane(0, step))

    loads[3].wait()
    pairs = pairs_in[...].astype(F32)
    stacked = jnp.concatenate(
        [pairs[side : side + 1, 512 * k : 512 * k + 512] for side in (0, 1) for k in range(NZ)],
        axis=0,
    ).astype(BF16)
    place = iota((512, 512), 1)
    origin = (place % 256) // 8 * 16 + place // 256 * 8 + place % 8
    terms[...] = dot_nn(stacked, chosen(iota((512, 512), 0) == origin)).astype(jnp.int32)
    index = iota((MODES, OWN), 0)

    def make_hot(c):
        side = jnp.where(core == c, 0, HALF)
        for k in range(NZ):
            from_lane = slice(OWN * c, OWN * c + OWN)
            begin = side + OWN * lax.rem(k - z + NZ, NZ)
            span = pl.ds(pl.multiple_of(begin, OWN), OWN)
            second = terms[NZ + k : NZ + k + 1, from_lane]
            hot_a[:, span] = chosen(index == terms[k : k + 1, from_lane])
            hot_b[:, span] = chosen(index == second)
            constant[:, span] = (second == MODES).astype(F32)

    make_hot(0)
    for step in NEAR_FIRST:
        drain(rows.at[pl.ds(0, ROWS)], recv_sem.at[step - 1])
        forward(lax.rem(y - step + NY, NY))

    drain(extra.at[pl.ds(0, (NY - 1) * ROWS)], recv_sem.at[EXTRA])
    line = iota((NX * ROWS, 128), 0)
    column = line // ROWS * GROUP + line % GROUP + jnp.where(line % ROWS < GROUP, 0, 32)
    compact[...] = dot_nt(chosen(iota((NX * ROWS, 128), 1) == column), extra[...]).astype(BF16)
    for step in (2, 1, 3):
        theirs = pl.ds(pl.multiple_of(lax.rem(x + step, NX) * ROWS, ROWS), ROWS)
        send(
            compact.at[theirs], compact_in.at[pl.ds(step * ROWS, ROWS)], COMPACT,
            at_plane(step, 0),
        )
    compact_in[0:ROWS, :] = compact[pl.ds(pl.multiple_of(x * ROWS, ROWS), ROWS), :]

    make_hot(1)

    def build(begin, end):
        for k in range(TERMS // CHUNK):
            span = slice(k * CHUNK, (k + 1) * CHUNK)
            first = dot_nn(rows[begin:end, :], hot_a[:, span])
            second = dot_nn(rows[begin:end, :], hot_b[:, span]) + constant[:, span]
            library[begin:end, span] = (first * second).astype(BF16)

    build(0, SLAB)
    square[...] = jnp.zeros_like(square)
    quarter = iota((8, 128), 1) // PLANE
    line, lane = iota((TARGETS, TARGETS), 0), iota((TARGETS, TARGETS), 1)
    ring = line % PLANE % NY * NX + line % PLANE // NY
    spread[...] = chosen(ring * GROUP + line // PLANE == lane)
    drain(rows.at[pl.ds(0, SLAB)], recv_sem.at[SLABS])
    build(SLAB, 2 * SLAB)
    for step in (3, 2):
        drain(rows.at[pl.ds(0, SLAB)], recv_sem.at[SLABS + step - 1])
        build(step * SLAB, (step + 1) * SLAB)

    drain(compact_in.at[pl.ds(0, (NX - 1) * ROWS)], recv_sem.at[COMPACT])
    given = jnp.concatenate([compact_in[k * ROWS : (k + 1) * ROWS, :] for k in range(NX)], axis=1)
    def squares(vector):
        return jnp.sum(vector * vector, axis=1, keepdims=True)

    diagonal = iota((GROUP, 128), 0) == iota((GROUP, 128), 1)

    def to_row(column):
        return jnp.sum(jnp.where(diagonal, column, 0.0), axis=0, keepdims=True)

    def to_column(row):
        return jnp.sum(jnp.where(diagonal, row, 0.0), axis=1, keepdims=True)

    def scatter_sums(lhs, finish, out, mine, pair, pre, got, at, image=None, curve=None, curves=None):
        if image is not None:
            curve[0] = to_row(squares(image))
            send(curve.at[0], curve.at[1], CURVE + at - 1, sibling)
            send(curve.at[0], curves.at[NZ // 2 - 1], CURVES + at - 1, at_line(NZ // 2)[1])
            send(curve.at[0], curves.at[NZ - 1], CURVES + at - 1, across)
        far = pl.ds(NZ // 2 * OWN, OWN)
        middle, start, end = (slice(a * OWN, b * OWN) for a, b in ((3, 6), (0, 3), (6, 8)))

        def partial(side, where):
            columns = slice(side * HALF + where.start, side * HALF + where.stop)
            return finish(dot_nn(lhs, library[:, columns]))

        out[:, middle] = partial(1, middle)
        send(out.at[:, middle], pair.at[:, middle], PAIR + at, sibling, MIDDLE + at)
        send(out.at[:, far], got.at[NZ - 1], SUMS + at, across)
        mine[:, middle] = partial(0, middle)
        send(mine.at[:, far], got.at[NZ // 2 - 1], SUMS + at, at_line(NZ // 2)[1])
        for where in (start, end):
            out[:, where] = partial(1, where)
            send(out.at[:, where], pair.at[:, where], PAIR + at, sibling)
        for where in (start, end):
            mine[:, where] = partial(0, where)

        def share(step):
            device = at_line(step)[1]
            send(pre.at[:, pl.ds(step * OWN, OWN)], got.at[step - 1], SUMS + at, device)
            if image is not None:
                send(curve.at[2], curves.at[step - 1], CURVES + at - 1, device)

        if image is not None:
            drain(curve.at[1], recv_sem.at[CURVE + at - 1])
            curve[2] = curve[0] + curve[1]
        drain(pair.at[:, middle], recv_sem.at[MIDDLE + at])
        pre[:, middle] = mine[:, middle] + pair[:, middle]
        share(3)
        share(5)
        drain(pair.at[:, pl.ds(0, 5 * OWN)], recv_sem.at[PAIR + at])
        for where in (start, end):
            pre[:, where] = mine[:, where] + pair[:, where]
        for step in (2, 6, 1, 7):
            share(step)

    def sum_up(pre, got, at):
        drain(got, recv_sem.at[SUMS + at])
        total = pre[:, :OWN]
        for step in range(NZ):
            total = total + got[step]
        return total * mask * (1.0 / SNAPS)

    def curvature(curve, curves, at):
        drain(curves, recv_sem.at[CURVES + at - 1])
        total = curve[2]
        for step in range(NZ):
            total = total + curves[step]
        return to_column(total) * (1.0 / SNAPS)

    def gather_terms(value, full, at):
        arrived = ARRIVED + RING * at

        def span(side, step):
            return pl.ds(side * HALF + (NZ - step) % NZ * OWN, OWN)

        def forward(step):
            send(
                full.at[:, span(0, step)], full.at[:, span(1, step)], HALVES + at, sibling,
                arrived + NZ + step,
            )

        def wait(side, steps):
            for step in steps:
                slot = arrived + step if side == 0 else arrived + NZ + step
                drain(full.at[:, pl.ds(0, OWN)], recv_sem.at[slot])
                if side == 0 and step != NZ // 2:
                    forward(step)

        def product(side, steps):
            total = None
            for step in steps:
                term = dot_nt(split(full[:, span(side, step)]), library[:, span(side, step)])
                total = term if total is None else total + term
            return total

        full[:, :OWN] = value
        mine = full.at[:, pl.ds(0, OWN)]
        for step in FAR_FIRST:
            send(mine, full.at[:, span(0, step)], SLICES + at, at_line(step)[1], arrived + step)
            if step == NZ // 2:
                send(mine, full.at[:, span(1, step)], SLICES + at, across, arrived + NZ + step)
        forward(0)
        image = product(0, (0,))
        wait(1, (0,))
        image = image + product(1, (0,))
        wait(0, (1, 7))
        image = image + product(0, (1, 7))
        wait(0, (2, 6))
        wait(0, (3, 5))
        image = image + product(0, (2, 6, 3, 5))
        wait(1, (1, 7))
        image = image + product(1, (1, 7))
        wait(0, (4,))
        wait(1, (4,))
        image = image + product(0, (4,)) + product(1, (4,))
        wait(1, (2, 6))
        image = image + product(1, (2, 6))
        wait(1, (3, 5))
        return merge(image + product(1, (3, 5)))

    scatter_sums(given, lambda value: value[:GROUP], out0, mine0, pair0, pre0, got0, 0)
    line, lane = iota((LOCAL, OWN), 0), iota((LOCAL, OWN), 1)
    from_x = lax.rem(x - line // 128 + NX, NX)
    pick = (
        (from_x * NY + line % 128 // 16 == lane // 8)
        & (line % 16 // 8 == y // 4)
        & (line % 8 == lane % 8)
    )
    mask = dot_nn(given, chosen(pick))[GROUP:]

    direction = sum_up(pre0, got0, 0)
    image = gather_terms(direction, full0, 0)
    scatter_sums(split(image), merge, out1, mine1, pair1, pre1, got1, 1, image, curve1, curves1)
    energy = squares(full0[...])
    step_len = energy / curvature(curve1, curves1, 1)
    coeffs = step_len * direction
    resid = direction - step_len * sum_up(pre1, got1, 1)
    next_image = gather_terms(resid, full1, 1)
    fresh = squares(full1[...])
    ratio = fresh / energy
    direction = resid + ratio * direction
    image = next_image + ratio * image
    scatter_sums(split(image), merge, out2, mine2, pair2, pre2, got2, 2, image, curve2, curves2)
    step_len = fresh / curvature(curve2, curves2, 2)
    coeffs = coeffs + step_len * direction
    resid = resid - step_len * sum_up(pre2, got2, 2)

    square[0:GROUP, :] = coeffs
    square[GROUP : 2 * GROUP, :] = resid
    turn[...] = square[...].T
    lane = iota((PLANE, 128), 1) // (2 * GROUP)
    total = turn[pl.ds(0, PLANE, stride=8), :]
    for k in range(1, 8):
        total = jnp.where(
            lane == k, pltpu.roll(turn[pl.ds(k, PLANE, stride=8), :], 2 * GROUP * k, 1), total
        )
    for k in range(PLANE):
        packed[k] = total[k : k + 1]
    here = x * NY + y
    far_first = sorted(peers, key=lambda peer: -min(peer[0], NX - peer[0]) - min(peer[1], NY - peer[1]))
    for a, b in far_first:
        spot = lax.rem(x + a, NX) * NY + lax.rem(y + b, NY)
        send(packed.at[spot], unpacked.at[here], TURN, at_plane(a, b))
    unpacked[here] = packed[here]
    drain(rows.at[pl.ds(0, (NY - 1) * ROWS)], send_sem.at[0])
    drain(extra.at[pl.ds(0, (NY - 1) * ROWS)], send_sem.at[EXTRA])
    for step in (1, 2, 3):
        drain(rows.at[pl.ds(0, SLAB)], send_sem.at[SLABS + step - 1])
    drain(compact_in.at[pl.ds(0, (NX - 1) * ROWS)], send_sem.at[COMPACT])
    for k, (pair, got) in enumerate(((pair0, got0), (pair1, got1), (pair2, got2))):
        drain(pair, send_sem.at[PAIR + k])
        drain(got, send_sem.at[SUMS + k])
    for k, full in enumerate((full0, full1)):
        drain(full.at[:, pl.ds(0, HALF)], send_sem.at[SLICES + k])
        drain(full.at[:, pl.ds(0, HALF - OWN)], send_sem.at[HALVES + k])
    for k, (curve, curves) in enumerate(((curve1, curves1), (curve2, curves2))):
        drain(curve.at[1], send_sem.at[CURVE + k])
        drain(curves, send_sem.at[CURVES + k])
    drain(unpacked.at[pl.ds(0, PLANE - 1)], recv_sem.at[TURN])
    received = jnp.concatenate(
        [unpacked[k] for k in range(PLANE)] + [jnp.zeros((128 - PLANE, 128), F32)], axis=0
    )
    turned[...] = received.T
    sides = []
    for out in range(2):
        for part in range(2):
            total = turned[pl.ds(out * GROUP + 4 * part, 8, stride=2 * GROUP), :]
            for k in range(1, 4):
                more = turned[pl.ds(out * GROUP + 4 * part + k, 8, stride=2 * GROUP), :]
                total = jnp.where(quarter == k, pltpu.roll(more, PLANE * k, 1), total)
            sides.append(total)
    both = jnp.concatenate(
        [jnp.concatenate(sides[0:2], axis=1), jnp.concatenate(sides[2:4], axis=1)], axis=0
    )
    high = both.astype(BF16)
    rest = both - high.astype(F32)
    middle = rest.astype(BF16)
    low = (rest - middle.astype(F32)).astype(BF16)
    moved = dot_nn(jnp.concatenate([high, middle, low], axis=0), spread[...])
    out_ref[...] = moved[0:16] + moved[16:32] + moved[32:48]

    drain(unpacked.at[pl.ds(0, PLANE - 1)], send_sem.at[TURN])


def body(modes, targets, pairs, support):
    vmem = pl.BlockSpec(memory_space=pltpu.VMEM)
    hbm = pl.BlockSpec(memory_space=pltpu.HBM)
    both = pl.pallas_call(
        kernel,
        out_shape=jax.ShapeDtypeStruct((16, TARGETS), F32),
        in_specs=[hbm] * 4,
        out_specs=vmem,
        scratch_shapes=[
            pltpu.VMEM((ROWS, TARGETS), BF16),
            pltpu.VMEM((2, TERMS), jnp.int32),
            pltpu.VMEM((8, TARGETS), jnp.int32),
            pltpu.VMEM((LOCAL, MODES), BF16),
            pltpu.VMEM((SLAB, 128), BF16),
            pltpu.VMEM((SLAB, 128), BF16),
            pltpu.VMEM((NX * ROWS, 128), BF16),
            pltpu.VMEM((NX * ROWS, 128), BF16),
            pltpu.VMEM((MODES, TERMS), BF16),
            pltpu.VMEM((MODES, TERMS), BF16),
            pltpu.VMEM((1, TERMS), F32),
            pltpu.VMEM((2 * NZ, 512), jnp.int32),
            pltpu.VMEM((LOCAL, TERMS), BF16),
        ]
        + [pltpu.VMEM((GROUP, HALF), F32)] * 12
        + [pltpu.VMEM((NZ, GROUP, OWN), F32)] * 3
        + [pltpu.VMEM((GROUP, TERMS), F32)] * 2
        + [
            pltpu.VMEM((3, 1, 128), F32),
            pltpu.VMEM((3, 1, 128), F32),
            pltpu.VMEM((NZ, 1, 128), F32),
            pltpu.VMEM((NZ, 1, 128), F32),
            pltpu.VMEM((OWN, 128), F32),
            pltpu.VMEM((128, OWN), F32),
            pltpu.VMEM((128, 128), F32),
            pltpu.VMEM((PLANE, 1, 128), F32),
            pltpu.VMEM((PLANE, 1, 128), F32),
            pltpu.VMEM((TARGETS, TARGETS), BF16),
            pltpu.SemaphoreType.DMA((4,)),
            pltpu.SemaphoreType.DMA((ARRIVED,)),
            pltpu.SemaphoreType.DMA((STAGES,)),
        ],
        compiler_params=pltpu.CompilerParams(
            collective_id=0, has_side_effects=True, vmem_limit_bytes=48 * 2**20
        ),
        name="regression",
    )(*(pltpu.with_memory_space_constraint(v, pltpu.HBM) for v in (modes, targets, pairs.T, support)))
    return both[:8], both[8:]


def solution(mesh):
    rows = P(("snap", "tile"), None)
    return jax.shard_map(
        body,
        mesh=mesh,
        in_specs=(rows, rows, P(), rows),
        out_specs=(rows, rows),
        check_vma=False,
    )
```
